32 devices in a mesh: pix: 8 (over y, x, core), ion: 4 (over z).
Axes of the slice: x: 2, y: 2, z: 4, core: 2. Of those that a mesh axis runs over, the one named last changes fastest.
Arguments:
- images: bfloat16 [20480, 16384], P('ion', 'pix')
- stencil: float32 [5, 16384], P(None, 'pix'), may hold values from 0.05 to 0.4
- pairs: int32 [192, 2], P('ion'), may hold values from 0 to 159, as said below
- live: int32 [4], P('ion'), may hold values from 16 to 48, as said below
- rule_of_block: int32 [160], replicated, may hold values from 0 to 63
- adduct: bfloat16 [64, 128, 128], P('ion'), may hold values from -6 to 6
Outputs:
- smoothed: bfloat16 [20480, 16384], P('ion', 'pix')
- scores: bfloat16 [192, 128, 128], P('ion', 'pix')
The draws below stay inside these ranges and needn't reach their ends.
Inputs may be any that keep to these rules, and one draw needn't show every extreme that they name: Slot s belongs to ion block range of index s // 48 of ion: a lies in that index's own 20480 // (128 * 4) blocks, and |a - b| <= 3. Entries of unused slots are valid pairs too. `live`: some index of ion uses all its slots.
All inputs are finite; a program needn't handle non-finite values.
Results may differ from the reference program's by a relative error of at most 0.0053.
Values may be sent and summed in bfloat16 or wider, within the bound.
No kernel may reach another device: no remote copies, remote signals or barrier semaphores. Data moves between devices by JAX's collectives and lax.ppermute only.
A program may use at most 192 MiB of HBM per device.

```python
import math
import jax
import jax.numpy as jnp
from jax import lax

IONS = 20480
BLOCK = 128
RULES = 64
REACH = 3
PAIRS_DEV = 48
PIXELS = 16384
NBLK = 160
PAIR_SLOTS = 192
N_ION = 4


def draw_images(key, part):
    key_row_block, key_cols, key_base = jax.random.split(key, 3)
    row_scale = jnp.exp(jax.random.uniform(key_row_block, (IONS, 1), jnp.float32, math.log(0.3), math.log(3.0)))
    position = jnp.arange(PIXELS, dtype=jnp.float32) / max(PIXELS - 1, 1)
    col_scale = jnp.exp(jax.random.uniform(key_cols, (1, PIXELS), jnp.float32, math.log(0.3), math.log(3.0)))
    col_scale = col_scale * (0.5 + position)[None, :]
    base = jax.random.normal(key_base, (IONS, PIXELS), jnp.float32)
    return (base * row_scale * col_scale).astype(jnp.bfloat16)


def pair_tables(key):
    base = jax.random.fold_in(key, 7717)
    key_live, key_top, key_block, key_offset = jax.random.split(base, 4)
    local_blocks = IONS // (BLOCK * N_ION)
    live_counts = jax.random.randint(key_live, (N_ION,), PAIRS_DEV // 3, PAIRS_DEV + 1)
    top_index = jax.random.randint(key_top, (), 0, N_ION)
    live_counts = live_counts.at[top_index].set(PAIRS_DEV)
    block_local = jax.random.randint(key_block, (N_ION, PAIRS_DEV), 0, local_blocks)
    offsets = jax.random.randint(key_offset, (N_ION, PAIRS_DEV), -REACH, REACH + 1)
    block_local = block_local.at[:, 0].set(0).at[:, 1].set(local_blocks - 1)
    offsets = offsets.at[:, 0].set(-REACH).at[:, 1].set(REACH)
    device_ids = jnp.arange(N_ION, dtype=jnp.int32)[:, None]
    first_block = device_ids * local_blocks + block_local
    partner_block = jnp.clip(first_block + offsets, 0, NBLK - 1)
    table = jnp.stack([first_block, partner_block], axis=-1).reshape(PAIR_SLOTS, 2)
    return (table.astype(jnp.int32), live_counts.astype(jnp.int32))


def draw_pairs(key, part):
    return pair_tables(key)[0]


def draw_live(key, part):
    return pair_tables(key)[1]


def plant(values, own_key, low, high):
    dims = values.shape
    spot = [jax.random.randint(jax.random.fold_in(own_key, axis), (), 0, dims[axis]) for axis in range(len(dims))]
    values = values.at[tuple(spot)].set(low)
    longest = dims.index(max(dims))
    spot[longest] = (spot[longest] + 1) % dims[longest]
    return values.at[tuple(spot)].set(high)


def steps_of(key, shape, cuts, smallest, top_value):
    level = 1.0
    for axis_at, shards_of in cuts:
        heights = jax.random.uniform(jax.random.fold_in(jax.random.fold_in(key, 6), axis_at), (shards_of,), jnp.float32, smallest / len(cuts), top_value / len(cuts))
        level = level * jnp.repeat(jnp.exp(heights), shape[axis_at] // shards_of).reshape((-1,) + (1,) * (len(shape) - 1 - axis_at))
    return level


def noise(rng, dims, width, bound, cuts=(), held_as=jnp.bfloat16):
    entries = jax.random.normal(rng, dims, jnp.float32) * width
    if len(cuts) > 0:
        entries = steps_of(rng, dims, cuts, -0.22, 0.18) * entries
    return jnp.clip(entries, min=-bound, max=bound).astype(held_as)


def setup_inputs(seed: int = 0) -> dict:
    arg_keys = jax.random.split(jax.random.key(seed), 7)
    images = draw_images(jax.random.fold_in(arg_keys[6], 71), 0)
    stencil = jnp.clip(0.05 + 0.35 * jax.random.uniform(arg_keys[1], (5, PIXELS), jnp.float32) ** steps_of(arg_keys[1], (5, PIXELS), ((1, 8),), -0.2, 0.2), 0.05, 0.4)
    pairs = draw_pairs(jax.random.fold_in(arg_keys[6], 71), 0)
    live = draw_live(jax.random.fold_in(arg_keys[6], 71), 0)
    rule_of_block = plant(jax.random.randint(arg_keys[4], (NBLK,), 0, RULES), jax.random.fold_in(arg_keys[4], 1), 0, RULES - 1).astype(jnp.int32)
    adduct = noise(arg_keys[5], (RULES, BLOCK, BLOCK), 1.0, 6.0, ((0, 4),))
    return dict(images=images, stencil=stencil, pairs=pairs, live=live, rule_of_block=rule_of_block, adduct=adduct)


def smooth_block(pieces):
    rows, weights = pieces
    padded = jnp.pad(rows.astype(jnp.float32), ((0, 0), (2, 2)))
    total = jnp.zeros(rows.shape, jnp.float32)
    for tap in range(5):
        total = total + weights[tap][None, :] * padded[:, tap:tap + PIXELS]
    return total.astype(jnp.bfloat16)

def reference(images, stencil, pairs, live, rule_of_block, adduct):
    blocks = images.reshape(NBLK, BLOCK, PIXELS)

    def one_block(rows):
        return smooth_block((rows, stencil))
    smoothed = lax.map(one_block, blocks).reshape(IONS, PIXELS)

    def block_energy(rows):
        values = rows.astype(jnp.float32)
        return lax.optimization_barrier(jnp.mean(values * values, axis=1))
    energy = lax.map(block_energy, smoothed.reshape(NBLK, BLOCK, PIXELS)).reshape(IONS)
    inverse = 1.0 / jnp.sqrt(energy + 1e-06)

    def one_pair(pair):
        first = (pair[0] * BLOCK).astype(jnp.int32)
        second = (pair[1] * BLOCK).astype(jnp.int32)
        left_operand = lax.dynamic_slice_in_dim(smoothed, first, BLOCK, 0)
        right_operand = lax.dynamic_slice_in_dim(smoothed, second, BLOCK, 0)
        gram = jnp.dot(left_operand, right_operand.T, preferred_element_type=jnp.float32)
        inv_left = lax.dynamic_slice_in_dim(inverse, first, BLOCK, 0)
        inv_right = lax.dynamic_slice_in_dim(inverse, second, BLOCK, 0)
        coloc = (gram * inv_left[:, None] * inv_right[None, :] / PIXELS).astype(jnp.bfloat16)
        table = adduct[rule_of_block[pair[1]]]
        return jnp.dot(coloc, table, preferred_element_type=jnp.float32)
    scores = lax.map(one_pair, pairs)
    slot_numbers = jnp.arange(PAIR_SLOTS, dtype=jnp.int32)
    used = slot_numbers % PAIRS_DEV < live[slot_numbers // PAIRS_DEV]
    scores = jnp.where(used[:, None, None], scores, 0.0).astype(jnp.bfloat16)
    return (smoothed, scores)
```

```python
import functools

import jax
import jax.numpy as jnp
from jax import lax
from jax.experimental import pallas as pl
from jax.experimental.pallas import tpu as pltpu
from jax.sharding import PartitionSpec as P

REACH = 3
TAPS = 5
LANES = 128
HALF = LANES // 2
VMEM_BYTES = 58 * 1024 * 1024


def params():
    return pltpu.CompilerParams(vmem_limit_bytes=VMEM_BYTES)


def cost(flops, moved):
    return pl.CostEstimate(flops=flops, bytes_accessed=moved, transcendentals=0)


def whole(shape):
    return pl.BlockSpec(shape, lambda *_: (0,) * len(shape))


def weights_kernel(stencil_ref, out_ref):
    tiles = stencil_ref.shape[1] // LANES
    k = lax.broadcasted_iota(jnp.int32, (2 * LANES, LANES), 0)
    lane = lax.broadcasted_iota(jnp.int32, (2 * LANES, LANES), 1)
    first = lane < HALF
    tap = k - lane + jnp.where(first, 2 - LANES, 2)
    low_half = lax.broadcasted_iota(jnp.int32, (TAPS, LANES), 1) < HALF
    zeros = jnp.zeros((TAPS, LANES), jnp.float32)
    for j in range(-1, tiles):
        here = stencil_ref[:, j * LANES : (j + 1) * LANES] if j >= 0 else zeros
        after = stencil_ref[:, (j + 1) * LANES : (j + 2) * LANES] if j + 1 < tiles else zeros
        mixed = jnp.where(low_half, after, here)
        w = jnp.zeros((2 * LANES, LANES), jnp.float32)
        for t in range(TAPS):
            w = jnp.where(tap == t, mixed[t : t + 1, :], w)
        high = w.astype(jnp.bfloat16)
        low = (w - high.astype(jnp.float32)).astype(jnp.bfloat16)
        out_ref[j + 1, :, :LANES] = high
        out_ref[j + 1, :, LANES:] = low


def smooth_rows(x_ref, halo_ref, w_ref, store):
    tiles = x_ref.shape[1] // LANES
    rows = x_ref.shape[0]
    first = lax.broadcasted_iota(jnp.int32, (rows, LANES), 1) < HALF
    before = None
    for j in range(-1, tiles):
        if j < 0:
            window = jnp.concatenate([halo_ref[...], x_ref[:, :LANES]], axis=1)
        elif j == tiles - 1:
            window = jnp.concatenate([x_ref[:, j * LANES :], halo_ref[...]], axis=1)
        else:
            window = x_ref[:, j * LANES : (j + 2) * LANES]
        both = jnp.dot(window, w_ref[j + 1], preferred_element_type=jnp.float32)
        now = both[:, :LANES] + both[:, LANES:]
        if j >= 0:
            store(j, jnp.where(first, before, now).astype(jnp.bfloat16))
        before = now


def edges_kernel(x_ref, halo_ref, w_ref, top_ref, bottom_ref):
    step = pl.program_id(0)

    def run(out_ref):
        def store(j, values):
            out_ref[:, j * LANES : (j + 1) * LANES] = values

        smooth_rows(x_ref, halo_ref, w_ref, store)

    pl.when(step < REACH)(lambda: run(top_ref))
    pl.when(step >= REACH)(lambda: run(bottom_ref))


def gram_of(left, right):
    return lax.dot_general(
        left, right, (((1,), (1,)), ((), ())), preferred_element_type=jnp.float32
    )


def main_kernel(steps, group, block, rel_ref, x_ref, halo_ref, w_ref, out_ref, energy_ref, gram_ref, held):
    step = pl.program_id(0)
    blocks = steps * group
    rows, width = x_ref.shape

    @pl.when(step < steps)
    def smooth():
        total = [jnp.zeros((rows, LANES), jnp.float32)]

        def store(j, values):
            columns = slice(j * LANES, (j + 1) * LANES)
            out_ref[:, columns] = values
            held[pl.ds(step * group, group), :, columns] = values.reshape(group, block, LANES)
            wide = values.astype(jnp.float32)
            total[0] = total[0] + wide * wide

        smooth_rows(x_ref, halo_ref, w_ref, store)
        for g in range(group):
            part = total[0][g * block : (g + 1) * block, :]
            energy_ref[pl.ds(step * group + g, 1), :] = jnp.sum(part.T, axis=0, keepdims=True)

    @pl.when(step == steps)
    def grams():
        slots = gram_ref.shape[0]

        def one(s, carry):
            a = rel_ref[2 * s]
            b = jnp.clip(rel_ref[2 * s + 1], 0, blocks - 1)
            gram_ref[s] = gram_of(held[a], held[b])
            return carry

        lax.fori_loop(0, slots, one, 0, unroll=4)


def cross_kernel(blocks, block, chips, share, info_ref, rel_ref, gram_ref, energy_ref, top_ref, bottom_ref,
                 down_ref, up_ref, keep_ref, give_ref, spare, wide, table):
    core = info_ref[0]
    slots = gram_ref.shape[0]
    e_rows = table.shape[0]
    e_at = chips * slots * share

    table[...] = jnp.zeros_like(table)
    table[REACH : REACH + blocks, :] = energy_ref[...]
    for k in range(REACH):
        for ref, row in ((down_ref, k), (up_ref, REACH + blocks + k)):
            acc = jnp.zeros((block, LANES), jnp.float32)
            for j in range(ref.shape[1] // LANES):
                v = ref[k * block : (k + 1) * block, j * LANES : (j + 1) * LANES].astype(jnp.float32)
                acc = acc + v * v
            table[row : row + 1, :] = jnp.sum(acc.T, axis=0, keepdims=True)

    def emit(s, rows_of):
        for chip in range(chips):
            at = pl.multiple_of((chip * slots + s) * share, share)
            keep_ref[pl.ds(at, share), :] = rows_of(pl.multiple_of((2 * chip + core) * share, share))
            wide[pl.ds(at, share), :] = rows_of(pl.multiple_of((2 * chip + 1 - core) * share, share))

    def one(s, carry):
        a, b = rel_ref[2 * s], rel_ref[2 * s + 1]
        emit(s, lambda at: gram_ref[s, pl.ds(at, share), :])

        def crossing(own_ref, own, other_ref, other):
            own = pl.multiple_of(own * block, block)
            other = pl.multiple_of(other * block, block)
            spare[...] = gram_of(own_ref[pl.ds(own, block), :], other_ref[pl.ds(other, block), :])
            emit(s, lambda at: spare[pl.ds(at, share), :])

        @pl.when(b < 0)
        def below():
            crossing(top_ref, a, down_ref, b + REACH)

        @pl.when(b >= blocks)
        def above():
            crossing(bottom_ref, a - (blocks - REACH), up_ref, b - blocks)

        return carry

    lax.fori_loop(0, slots, one, 0)
    give_ref[:e_at, :] = wide[...].astype(jnp.bfloat16)
    energies = table[...]
    high = energies.astype(jnp.bfloat16)
    give_ref[e_at : e_at + e_rows, :] = high
    give_ref[e_at + e_rows :, :] = (energies - high.astype(jnp.float32)).astype(jnp.bfloat16)
    keep_ref[e_at : e_at + e_rows, :] = energies


def chip_kernel(chips, rows, e_rows, info_ref, keep_ref, got_ref, own_ref, *out_refs):
    chip = info_ref[1]
    e_at = chips * rows
    energies = keep_ref[e_at:, :] + (
        got_ref[e_at : e_at + e_rows, :].astype(jnp.float32) + got_ref[e_at + e_rows :, :].astype(jnp.float32)
    )
    high = energies.astype(jnp.bfloat16)
    low = (energies - high.astype(jnp.float32)).astype(jnp.bfloat16)
    for d in range(chips):
        at = pl.multiple_of((chip ^ d) * rows, rows)
        total = keep_ref[pl.ds(at, rows), :] + got_ref[pl.ds(at, rows), :].astype(jnp.float32)
        if d == 0:
            own_ref[:rows, :] = total
            own_ref[rows:, :] = energies
        else:
            out = out_refs[d - 1]
            out[:rows, :] = total.astype(jnp.bfloat16)
            out[rows : rows + e_rows, :] = high
            out[rows + e_rows :, :] = low


def score_kernel(share, e_rows, pixel_count, info_ref, rel_ref, rule_ref, own_ref, *refs):
    got_refs, (table_ref, out_ref, gram, inverse) = refs[:-4], refs[-4:]
    rows = gram.shape[0]
    slots = rows // share
    live, offset = info_ref[2], info_ref[3]
    total = own_ref[:rows, :]
    energies = own_ref[rows:, :]
    for got in got_refs:
        total = total + got[:rows, :].astype(jnp.float32)
        energies = energies + (
            got[rows : rows + e_rows, :].astype(jnp.float32) + got[rows + e_rows :, :].astype(jnp.float32)
        )
    gram[...] = total
    inverse[...] = 1.0 / jnp.sqrt(energies / pixel_count + 1e-06)
    lane = lax.broadcasted_iota(jnp.int32, (share, LANES), 1)
    mine = lane == lax.broadcasted_iota(jnp.int32, (share, LANES), 0) + offset

    def one(s, carry):
        inv_a = inverse[pl.ds(rel_ref[2 * s] + REACH, 1), :]
        inv_b = inverse[pl.ds(rel_ref[2 * s + 1] + REACH, 1), :]
        inv_a = jnp.sum(jnp.where(mine, inv_a, 0.0), axis=1, keepdims=True)
        g = gram[pl.ds(pl.multiple_of(s * share, share), share), :]
        coloc = (g * inv_a * inv_b / pixel_count).astype(jnp.bfloat16)
        scores = jnp.dot(coloc, table_ref[rule_ref[s]], preferred_element_type=jnp.float32)
        out_ref[s] = jnp.where(s < live, scores, 0.0).astype(jnp.bfloat16)
        return carry

    lax.fori_loop(0, slots, one, 0, unroll=4)


def on_device(images, stencil, pairs, live, rule_of_block, adduct):
    rows, width = images.shape
    rules_here, block, _ = adduct.shape
    blocks = rows // block
    slots = pairs.shape[0]
    tiles = width // LANES
    n_pix, n_ion = lax.axis_size("pix"), lax.axis_size("ion")
    pix, ion = lax.axis_index("pix"), lax.axis_index("ion")
    pixel_count = width * n_pix
    chips, share = n_pix // 2, block // n_pix
    core, chip = pix % 2, pix // 2

    def shifted(axis, size, up, value):
        steps = [(i, i + 1) if up else (i + 1, i) for i in range(size - 1)]
        return lax.ppermute(value, axis, steps)

    before = shifted("pix", n_pix, True, images[:, width - 2 :])
    after = shifted("pix", n_pix, False, images[:, :2])

    flat = adduct.reshape(rules_here * block, block)
    part = rules_here * block // n_pix
    flat = lax.dynamic_slice_in_dim(flat, pix * part, part, 0)
    table = lax.all_gather(flat, ("ion", "pix"), axis=0, tiled=True)
    table = table.reshape(n_ion * rules_here, block, block)

    weights = pl.pallas_call(
        weights_kernel,
        out_shape=jax.ShapeDtypeStruct((tiles + 1, 2 * LANES, 2 * LANES), jnp.bfloat16),
        compiler_params=params(),
        cost_estimate=cost(0, tiles * 2**17),
        name="band_weights",
    )(stencil)

    halo = jnp.concatenate([after, jnp.zeros((rows, LANES - 4), images.dtype), before], axis=1)

    edge = REACH * block

    def edge_block(i):
        return jnp.where(i < REACH, i, blocks - 2 * REACH + i)

    top, bottom = pl.pallas_call(
        edges_kernel,
        grid=(2 * REACH,),
        in_specs=[
            pl.BlockSpec((block, width), lambda i: (edge_block(i), 0)),
            pl.BlockSpec((block, LANES), lambda i: (edge_block(i), 0)),
            whole(weights.shape),
        ],
        out_specs=[
            pl.BlockSpec((block, width), lambda i: (jnp.minimum(i, REACH - 1), 0)),
            pl.BlockSpec((block, width), lambda i: (jnp.maximum(i - REACH, 0), 0)),
        ],
        out_shape=[jax.ShapeDtypeStruct((edge, width), jnp.bfloat16)] * 2,
        compiler_params=params(),
        cost_estimate=cost(2 * edge * width * 1024, 8 * edge * width),
        name="smooth_edges",
    )(images, halo, weights)

    down = shifted("ion", n_ion, True, bottom)
    up = shifted("ion", n_ion, False, top)

    relative = (pairs - ion * blocks).reshape(-1)
    group = next(g for g in (4, 2, 1) if blocks % g == 0)
    steps = blocks // group
    smoothed, energy, grams = pl.pallas_call(
        functools.partial(main_kernel, steps, group, block),
        grid_spec=pltpu.PrefetchScalarGridSpec(
            num_scalar_prefetch=1,
            grid=(steps + 1,),
            in_specs=[
                pl.BlockSpec((group * block, width), lambda i, _: (jnp.minimum(i, steps - 1), 0)),
                pl.BlockSpec((group * block, LANES), lambda i, _: (jnp.minimum(i, steps - 1), 0)),
                whole(weights.shape),
            ],
            out_specs=[
                pl.BlockSpec((group * block, width), lambda i, _: (jnp.minimum(i, steps - 1), 0)),
                whole((blocks, LANES)),
                whole((slots, block, block)),
            ],
            scratch_shapes=[pltpu.VMEM((blocks, block, width), jnp.bfloat16)],
        ),
        out_shape=[
            jax.ShapeDtypeStruct((rows, width), jnp.bfloat16),
            jax.ShapeDtypeStruct((blocks, LANES), jnp.float32),
            jax.ShapeDtypeStruct((slots, block, block), jnp.float32),
        ],
        compiler_params=params(),
        cost_estimate=cost(rows * width * 1024 + 2 * slots * block * block * width, 4 * rows * width),
        name="smooth_and_gram",
    )(relative, images, halo, weights)

    info = jnp.stack([core, chip, live[0], pix * share]).astype(jnp.int32)
    smem = pl.BlockSpec(memory_space=pltpu.SMEM)
    vmem = pl.BlockSpec(memory_space=pltpu.VMEM)
    e_rows = -(-(blocks + 2 * REACH) // 16) * 16
    g_rows = slots * share
    keep, give = pl.pallas_call(
        functools.partial(cross_kernel, blocks, block, chips, share),
        in_specs=[smem, smem] + [vmem] * 6,
        out_specs=[vmem, vmem],
        out_shape=[
            jax.ShapeDtypeStruct((chips * g_rows + e_rows, LANES), jnp.float32),
            jax.ShapeDtypeStruct((chips * g_rows + 2 * e_rows, LANES), jnp.bfloat16),
        ],
        scratch_shapes=[
            pltpu.VMEM((block, block), jnp.float32),
            pltpu.VMEM((chips * g_rows, LANES), jnp.float32),
            pltpu.VMEM((e_rows, LANES), jnp.float32),
        ],
        compiler_params=params(),
        cost_estimate=cost(0, 8 * edge * width),
        name="cross_grams",
    )(info, relative, grams, energy, top, bottom, down, up)

    got = lax.ppermute(give, "pix", [(i, i ^ 1) for i in range(n_pix)])
    message = jax.ShapeDtypeStruct((g_rows + 2 * e_rows, LANES), jnp.bfloat16)
    own, *messages = pl.pallas_call(
        functools.partial(chip_kernel, chips, g_rows, e_rows),
        in_specs=[smem, vmem, vmem],
        out_specs=[vmem] * chips,
        out_shape=[jax.ShapeDtypeStruct((g_rows + e_rows, LANES), jnp.float32)] + [message] * (chips - 1),
        compiler_params=params(),
        name="chip_sums",
    )(info, keep, got)
    received = [
        lax.ppermute(m, "pix", [(i, i ^ (2 * (d + 1))) for i in range(n_pix)]) for d, m in enumerate(messages)
    ]

    rules = jnp.take(rule_of_block, pairs[:, 1], axis=0)
    scores = pl.pallas_call(
        functools.partial(score_kernel, share, e_rows, pixel_count),
        in_specs=[smem, smem, smem] + [vmem] * (chips + 1),
        out_specs=vmem,
        out_shape=jax.ShapeDtypeStruct((slots, share, block), jnp.bfloat16),
        scratch_shapes=[pltpu.VMEM((g_rows, LANES), jnp.float32), pltpu.VMEM((e_rows, LANES), jnp.float32)],
        compiler_params=params(),
        name="scores",
    )(info, relative, rules, own, *received, table)
    return (smoothed, scores)


def solution(mesh):
    return jax.shard_map(
        on_device,
        mesh=mesh,
        in_specs=(
            P("ion", "pix"),
            P(None, "pix"),
            P("ion", None),
            P("ion"),
            P(),
            P("ion", None, None),
        ),
        out_specs=(P("ion", "pix"), P("ion", "pix", None)),
        check_vma=False,
    )
```

```python
import functools

import jax
import jax.numpy as jnp
from jax import lax
from jax.experimental import pallas as pl
from jax.experimental.pallas import tpu as pltpu
from jax.sharding import PartitionSpec as P

REACH = 3
TAPS = 5
LANES = 128
HALF = LANES // 2
TILE = 2 * LANES
DEPTH = 6 * LANES
VMEM_BYTES = 58 * 1024 * 1024


def params():
    return pltpu.CompilerParams(vmem_limit_bytes=VMEM_BYTES)


def cost(flops, moved):
    return pl.CostEstimate(flops=flops, bytes_accessed=moved, transcendentals=0)


def whole(shape):
    return pl.BlockSpec(shape, lambda *_: (0,) * len(shape))


def split(values):
    high = values.astype(jnp.bfloat16)
    return high, (values - high.astype(jnp.float32)).astype(jnp.bfloat16)


def weights_kernel(stencil_ref, out_ref):
    k = lax.broadcasted_iota(jnp.int32, (TILE, TILE), 0)
    n = lax.broadcasted_iota(jnp.int32, (TILE, TILE), 1)
    inner = k - n + 2
    k, n = k[:LANES], n[:LANES]
    outer = k - n + jnp.where(k < HALF, TILE + 2, 2 - LANES)
    for j in range(out_ref.shape[0]):
        taps = stencil_ref[:, j * TILE : (j + 1) * TILE]
        main = jnp.zeros((TILE, TILE), jnp.float32)
        edge = jnp.zeros((LANES, TILE), jnp.float32)
        for t in range(TAPS):
            main = jnp.where(inner == t, taps[t : t + 1, :], main)
            edge = jnp.where(outer == t, taps[t : t + 1, :], edge)
        out_ref[j, :TILE], out_ref[j, TILE : 2 * TILE] = split(main)
        out_ref[j, 2 * TILE : 2 * TILE + LANES], out_ref[j, 2 * TILE + LANES :] = split(edge)


def smooth_rows(x_ref, halo_ref, w_ref, store):
    rows, width = x_ref.shape
    tiles = width // TILE
    first = lax.broadcasted_iota(jnp.int32, (rows, LANES), 1) < HALF
    for j in range(tiles):
        own = x_ref[:, j * TILE : (j + 1) * TILE]
        before = halo_ref[...] if j == 0 else x_ref[:, j * TILE - LANES : j * TILE]
        after = halo_ref[...] if j == tiles - 1 else x_ref[:, (j + 1) * TILE : (j + 1) * TILE + LANES]
        edge = jnp.where(first, after, before)
        window = jnp.concatenate([own, own, edge, edge], axis=1)
        store(j, jnp.dot(window, w_ref[j], preferred_element_type=jnp.float32))


def lane_pairs(values):
    squares = values * values
    return squares[:, :LANES] + squares[:, LANES:]


def row_sums(part):
    return jnp.sum(part.T, axis=0, keepdims=True)


def gram_of(left, right):
    return lax.dot_general(
        left, right, (((1,), (1,)), ((), ())), preferred_element_type=jnp.float32
    )


def by_core(gram, chips, core):
    parts = gram.reshape(chips, 2, gram.shape[0] // (2 * chips), gram.shape[1])
    return jnp.where(core == 0, parts[:, 0], parts[:, 1]), jnp.where(core == 0, parts[:, 1], parts[:, 0])


def main_kernel(steps, group, block, info_ref, rel_ref, x_ref, halo_ref, w_ref,
                out_ref, energy_ref, keep_ref, give_ref, held, wide):
    step = pl.program_id(0)
    blocks = steps * group
    slots, chips = wide.shape[:2]

    @pl.when(step < steps)
    def smooth():
        total = [None]

        def store(j, values):
            columns = slice(j * TILE, (j + 1) * TILE)
            rounded = values.astype(jnp.bfloat16)
            out_ref[:, columns] = rounded
            held[pl.ds(step * group, group), :, columns] = rounded.reshape(group, block, TILE)
            squares = lane_pairs(values)
            total[0] = squares if j == 0 else total[0] + squares

        smooth_rows(x_ref, halo_ref, w_ref, store)
        for g in range(group):
            energy_ref[pl.ds(step * group + g, 1), :] = row_sums(total[0][g * block : (g + 1) * block, :])

    @pl.when(step == steps)
    def grams():
        core = info_ref[0]

        def one(s, carry):
            a = rel_ref[2 * s]
            b = jnp.clip(rel_ref[2 * s + 1], 0, blocks - 1)
            keep_ref[s], wide[s] = by_core(gram_of(held[a], held[b]), chips, core)
            return carry

        lax.fori_loop(0, slots, one, 0, unroll=4)
        give_ref[:slots] = wide[...].astype(jnp.bfloat16)


def cross_kernel(blocks, block, info_ref, rel_ref, slots, down_ref, up_ref, down_halo_ref, up_halo_ref, w_ref, energy_ref,
                 smoothed_ref, keep_in, give_in, keep_ref, give_ref, near, own, table, keep_part, give_part, sems):
    del keep_in, give_in
    core = info_ref[0]
    chips, share = keep_part.shape[1:3]
    units = 2 * table.shape[0] // block
    edge = REACH * block
    rows = blocks * block
    copies = [
        pltpu.make_async_copy(smoothed_ref.at[pl.ds(0, edge)], own.at[0], sems.at[0]),
        pltpu.make_async_copy(smoothed_ref.at[pl.ds(rows - edge, edge)], own.at[1], sems.at[1]),
    ]
    for copy in copies:
        copy.start()

    table[...] = jnp.zeros_like(table)
    table[REACH : REACH + blocks, :] = energy_ref[...]
    for side, (x_ref, halo_ref) in enumerate(((down_ref, down_halo_ref), (up_ref, up_halo_ref))):
        total = [None]

        def store(j, values):
            near[side, :, j * TILE : (j + 1) * TILE] = values.astype(jnp.bfloat16)
            squares = lane_pairs(values)
            total[0] = squares if j == 0 else total[0] + squares

        smooth_rows(x_ref, halo_ref, w_ref, store)
        for k in range(REACH):
            row = side * (REACH + blocks) + k
            table[row : row + 1, :] = row_sums(total[0][k * block : (k + 1) * block, :])
    for copy in copies:
        copy.wait()

    high, low = split(table[...])
    shape = (units, chips, share, LANES)
    keep_part[:units] = table[...].reshape(shape)
    give_part[:units] = high.reshape(shape)
    give_part[units:] = low.reshape(shape)
    copies = [
        pltpu.make_async_copy(keep_part.at[pl.ds(0, units)], keep_ref.at[pl.ds(slots, units)], sems.at[0]),
        pltpu.make_async_copy(give_part, give_ref.at[pl.ds(slots, 2 * units)], sems.at[1]),
    ]
    for copy in copies:
        copy.start()
    for copy in copies:
        copy.wait()

    def one(s, carry):
        a, b = rel_ref[2 * s], rel_ref[2 * s + 1]

        @pl.when((b < 0) | (b >= blocks))
        def crossing():
            side = (b >= 0).astype(jnp.int32)
            a_row = pl.multiple_of((a - side * (blocks - REACH)) * block, block)
            b_row = pl.multiple_of((b + REACH - side * (blocks + REACH)) * block, block)
            gram = gram_of(own[side, pl.ds(a_row, block), :], near[side, pl.ds(b_row, block), :])
            mine, other = by_core(gram, chips, core)
            keep_part[0] = mine
            give_part[0] = other.astype(jnp.bfloat16)
            first = pltpu.make_async_copy(keep_part.at[0], keep_ref.at[s], sems.at[0])
            second = pltpu.make_async_copy(give_part.at[0], give_ref.at[s], sems.at[1])
            first.start()
            second.start()
            first.wait()
            second.wait()

        return carry

    lax.fori_loop(0, slots, one, 0)


def chip_kernel(slots, units, info_ref, keep_ref, got_ref, own_ref, *out_refs):
    chip = info_ref[1]
    chips, share = keep_ref.shape[1:3]
    shape = (units * chips, share, LANES)
    energies = keep_ref[slots:] + (
        got_ref[slots : slots + units].astype(jnp.float32) + got_ref[slots + units :].astype(jnp.float32)
    )
    high, low = split(energies)
    for d in range(chips):
        total = keep_ref[:slots, chip ^ d] + got_ref[:slots, chip ^ d].astype(jnp.float32)
        if d == 0:
            own_ref[:slots] = total
            own_ref[slots:] = energies.reshape(shape)
        else:
            out = out_refs[d - 1]
            out[:slots] = total.astype(jnp.bfloat16)
            out[slots : slots + units * chips] = high.reshape(shape)
            out[slots + units * chips :] = low.reshape(shape)


def score_kernel(slots, pixel_count, info_ref, rel_ref, place_ref, own_ref, *refs):
    got_refs, (table_ref, out_ref, gram, inverse) = refs[:-4], refs[-4:]
    share = gram.shape[1]
    block = table_ref.shape[1]
    e_units = inverse.shape[0] // share
    live, offset = info_ref[2], info_ref[3]
    total = own_ref[:slots]
    energies = own_ref[slots:]
    for got in got_refs:
        total = total + got[:slots].astype(jnp.float32)
        energies = energies + (
            got[slots : slots + e_units].astype(jnp.float32) + got[slots + e_units :].astype(jnp.float32)
        )
    gram[...] = total
    inverse[...] = (1.0 / jnp.sqrt(energies / pixel_count + 1e-06)).reshape(inverse.shape)
    lane = lax.broadcasted_iota(jnp.int32, (share, LANES), 1)
    mine = lane == lax.broadcasted_iota(jnp.int32, (share, LANES), 0) + offset

    def one(s, carry):
        inv_a = inverse[pl.ds(rel_ref[2 * s] + REACH, 1), :]
        inv_b = inverse[pl.ds(rel_ref[2 * s + 1] + REACH, 1), :]
        inv_a = jnp.sum(jnp.where(mine, inv_a, 0.0), axis=1, keepdims=True)
        coloc = (gram[s] * inv_a * inv_b / pixel_count).astype(jnp.bfloat16)
        matrix = table_ref[pl.ds(pl.multiple_of(place_ref[s], block), block), :]
        scores = jnp.dot(coloc, matrix, preferred_element_type=jnp.float32)
        out_ref[s] = jnp.where(s < live, scores, 0.0).astype(jnp.bfloat16)
        return carry

    lax.fori_loop(0, slots, one, 0, unroll=4)


def on_device(images, stencil, pairs, live, rule_of_block, adduct):
    rows, width = images.shape
    rules_here, block, _ = adduct.shape
    blocks = rows // block
    slots = pairs.shape[0]
    n_pix, n_ion = lax.axis_size("pix"), lax.axis_size("ion")
    pix, ion = lax.axis_index("pix"), lax.axis_index("ion")
    pixel_count = width * n_pix
    chips, share = n_pix // 2, block // n_pix
    core, chip = pix % 2, pix // 2
    edge = REACH * block

    def shifted(axis, size, up, value):
        steps = [(i, i + 1) if up else (i + 1, i) for i in range(size - 1)]
        return lax.ppermute(value, axis, steps)

    def to_neighbours(value):
        return (
            shifted("ion", n_ion, True, value[rows - edge :]),
            shifted("ion", n_ion, False, value[:edge]),
        )

    before = shifted("pix", n_pix, True, images[:, width - 2 :])
    after = shifted("pix", n_pix, False, images[:, :2])
    down, up = to_neighbours(images)
    halo = jnp.concatenate([after, jnp.zeros((rows, LANES - 4), images.dtype), before], axis=1)
    down_halo, up_halo = to_neighbours(halo)

    flat = adduct.reshape(rules_here * block, block)
    part = rules_here * block // n_pix
    flat = lax.dynamic_slice_in_dim(flat, pix * part, part, 0)
    table = lax.all_gather(flat, "ion", axis=0, tiled=True)
    table = lax.all_gather(table, "pix", axis=0, tiled=True)
    rules = jnp.take(rule_of_block, pairs[:, 1], axis=0)
    if part % block == 0:
        row = rules % rules_here * block
        place = (row // part * n_ion + rules // rules_here) * part + row % part
    else:
        table = table.reshape(n_pix, n_ion, part, block).swapaxes(0, 1).reshape(-1, block)
        place = rules * block

    weights = pl.pallas_call(
        weights_kernel,
        out_shape=jax.ShapeDtypeStruct((width // TILE, DEPTH, TILE), jnp.bfloat16),
        compiler_params=params(),
        cost_estimate=cost(0, width * DEPTH * 2),
        name="band_weights",
    )(stencil)

    info = jnp.stack([core, chip, live[0], pix * share]).astype(jnp.int32)
    relative = (pairs - ion * blocks).reshape(-1)
    group = next(g for g in (4, 2, 1) if blocks % g == 0)
    steps = blocks // group
    units = -(-2 * (blocks + 2 * REACH) // block)
    half = (chips, share, LANES)
    keep_shape = (slots + units, *half)
    give_shape = (slots + 2 * units, *half)

    def rows_at(columns):
        return pl.BlockSpec((group * block, columns), lambda i, *_: (jnp.minimum(i, steps - 1), 0))

    smoothed, energy, keep, give = pl.pallas_call(
        functools.partial(main_kernel, steps, group, block),
        grid_spec=pltpu.PrefetchScalarGridSpec(
            num_scalar_prefetch=2,
            grid=(steps + 1,),
            in_specs=[rows_at(width), rows_at(LANES), whole(weights.shape)],
            out_specs=[rows_at(width), whole((blocks, LANES)), whole(keep_shape), whole(give_shape)],
            scratch_shapes=[
                pltpu.VMEM((blocks, block, width), jnp.bfloat16),
                pltpu.VMEM((slots, *half), jnp.float32),
            ],
        ),
        out_shape=[
            jax.ShapeDtypeStruct((rows, width), jnp.bfloat16),
            jax.ShapeDtypeStruct((blocks, LANES), jnp.float32),
            jax.ShapeDtypeStruct(keep_shape, jnp.float32),
            jax.ShapeDtypeStruct(give_shape, jnp.bfloat16),
        ],
        compiler_params=params(),
        cost_estimate=cost(2 * rows * width * DEPTH + 2 * slots * block * block * width, 4 * rows * width),
        name="smooth_and_gram",
    )(info, relative, images, halo, weights)

    smem = pl.BlockSpec(memory_space=pltpu.SMEM)
    vmem = pl.BlockSpec(memory_space=pltpu.VMEM)
    hbm = pl.BlockSpec(memory_space=pl.ANY)

    def cross(info_ref, rel_ref, *refs):
        cross_kernel(blocks, block, info_ref, rel_ref, slots, *refs)

    keep, give = pl.pallas_call(
        cross,
        in_specs=[smem, smem] + [vmem] * 6 + [hbm] * 3,
        out_specs=[hbm, hbm],
        out_shape=[jax.ShapeDtypeStruct(keep_shape, jnp.float32), jax.ShapeDtypeStruct(give_shape, jnp.bfloat16)],
        input_output_aliases={9: 0, 10: 1},
        scratch_shapes=[
            pltpu.VMEM((2, edge, width), jnp.bfloat16),
            pltpu.VMEM((2, edge, width), jnp.bfloat16),
            pltpu.VMEM((units * block // 2, LANES), jnp.float32),
            pltpu.VMEM((units, *half), jnp.float32),
            pltpu.VMEM((2 * units, *half), jnp.bfloat16),
            pltpu.SemaphoreType.DMA((2,)),
        ],
        compiler_params=params(),
        cost_estimate=cost(4 * edge * width * DEPTH, 8 * edge * width),
        name="cross_grams",
    )(info, relative, down, up, down_halo, up_halo, weights, energy, smoothed, keep, give)

    got = lax.ppermute(give, "pix", [(i, i ^ 1) for i in range(n_pix)])
    message = jax.ShapeDtypeStruct((slots + 2 * units * chips, share, LANES), jnp.bfloat16)
    own, *messages = pl.pallas_call(
        functools.partial(chip_kernel, slots, units),
        in_specs=[smem, vmem, vmem],
        out_specs=[vmem] * chips,
        out_shape=[jax.ShapeDtypeStruct((slots + units * chips, share, LANES), jnp.float32)]
        + [message] * (chips - 1),
        compiler_params=params(),
        name="chip_sums",
    )(info, keep, got)
    received = [
        lax.ppermute(m, "pix", [(i, i ^ (2 * (d + 1))) for i in range(n_pix)]) for d, m in enumerate(messages)
    ]

    scores = pl.pallas_call(
        functools.partial(score_kernel, slots, pixel_count),
        in_specs=[smem, smem, smem] + [vmem] * (chips + 1),
        out_specs=vmem,
        out_shape=jax.ShapeDtypeStruct((slots, share, block), jnp.bfloat16),
        scratch_shapes=[
            pltpu.VMEM((slots, share, LANES), jnp.float32),
            pltpu.VMEM((units * block // 2, LANES), jnp.float32),
        ],
        compiler_params=params(),
        name="scores",
    )(info, relative, place, own, *received, table)
    return (smoothed, scores)


def solution(mesh):
    return jax.shard_map(
        on_device,
        mesh=mesh,
        in_specs=(
            P("ion", "pix"),
            P(None, "pix"),
            P("ion", None),
            P("ion"),
            P(),
            P("ion", None, None),
        ),
        out_specs=(P("ion", "pix"), P("ion", "pix", None)),
        check_vma=False,
    )
```

```python
import functools

import jax
import jax.numpy as jnp
from jax import lax
from jax.experimental import pallas as pl
from jax.experimental.pallas import tpu as pltpu
from jax.sharding import PartitionSpec as P

REACH = 3
TAPS = 5
LANES = 128
HALF = LANES // 2
TILE = 2 * LANES
DEPTH = 6 * LANES
VMEM_BYTES = 58 * 1024 * 1024


def params():
    return pltpu.CompilerParams(vmem_limit_bytes=VMEM_BYTES)


def cost(flops, moved):
    return pl.CostEstimate(flops=flops, bytes_accessed=moved, transcendentals=0)


def whole(shape):
    return pl.BlockSpec(shape, lambda *_: (0,) * len(shape))


def split(values):
    high = values.astype(jnp.bfloat16)
    return high, (values - high.astype(jnp.float32)).astype(jnp.bfloat16)


def weights_kernel(stencil_ref, out_ref):
    k = lax.broadcasted_iota(jnp.int32, (TILE, TILE), 0)
    n = lax.broadcasted_iota(jnp.int32, (TILE, TILE), 1)
    inner = k - n + 2
    k, n = k[:LANES], n[:LANES]
    outer = k - n + jnp.where(k < HALF, TILE + 2, 2 - LANES)
    for j in range(out_ref.shape[0]):
        taps = stencil_ref[:, j * TILE : (j + 1) * TILE]
        main = jnp.zeros((TILE, TILE), jnp.float32)
        edge = jnp.zeros((LANES, TILE), jnp.float32)
        for t in range(TAPS):
            main = jnp.where(inner == t, taps[t : t + 1, :], main)
            edge = jnp.where(outer == t, taps[t : t + 1, :], edge)
        out_ref[j, :TILE], out_ref[j, TILE : 2 * TILE] = split(main)
        out_ref[j, 2 * TILE : 2 * TILE + LANES], out_ref[j, 2 * TILE + LANES :] = split(edge)


def smooth_rows(x_ref, halo, w_ref, store):
    rows, width = x_ref.shape
    tiles = width // TILE
    first = lax.broadcasted_iota(jnp.int32, (rows, LANES), 1) < HALF
    for j in range(tiles):
        own = x_ref[:, j * TILE : (j + 1) * TILE]
        before = halo if j == 0 else x_ref[:, j * TILE - LANES : j * TILE]
        after = halo if j == tiles - 1 else x_ref[:, (j + 1) * TILE : (j + 1) * TILE + LANES]
        edge = jnp.where(first, after, before)
        window = jnp.concatenate([own, own, edge, edge], axis=1)
        store(j, jnp.dot(window, w_ref[j], preferred_element_type=jnp.float32))


def lane_pairs(values):
    squares = values * values
    return squares[:, :LANES] + squares[:, LANES:]


def row_sums(part):
    return jnp.sum(part.T, axis=0, keepdims=True)


def gram_of(left, right):
    return lax.dot_general(
        left, right, (((1,), (1,)), ((), ())), preferred_element_type=jnp.float32
    )


def by_core(gram, chips, core):
    parts = gram.reshape(chips, 2, gram.shape[0] // (2 * chips), gram.shape[1])
    return jnp.where(core == 0, parts[:, 0], parts[:, 1]), jnp.where(core == 0, parts[:, 1], parts[:, 0])


def cut_kernel(edge, images_ref, first_ref, last_ref, top_ref, bottom_ref, head_ref, tail_ref, sems):
    rows = images_ref.shape[0]
    copies = [
        pltpu.make_async_copy(images_ref.at[pl.ds(0, edge)], top_ref, sems.at[0]),
        pltpu.make_async_copy(images_ref.at[pl.ds(rows - edge, edge)], bottom_ref, sems.at[1]),
    ]
    for copy in copies:
        copy.start()
    row = lax.broadcasted_iota(jnp.int32, (8, LANES), 0)
    lane = lax.broadcasted_iota(jnp.int32, (8, LANES), 1)
    for source, out, shift in ((first_ref, head_ref, 0), (last_ref, tail_ref, LANES - 8)):
        pick = (lane == row + shift).astype(jnp.bfloat16)
        out[...] = gram_of(pick, source[...]).astype(jnp.bfloat16)
    for copy in copies:
        copy.wait()


def halo_tile(columns_ref):
    columns = columns_ref[...].astype(jnp.float32).T.astype(jnp.bfloat16)
    row = lax.broadcasted_iota(jnp.int32, (8, LANES), 0)
    lane = lax.broadcasted_iota(jnp.int32, (8, LANES), 1)
    place = (lane == row + jnp.where(row < 4, 0, LANES - 8)).astype(jnp.bfloat16)
    return jnp.dot(columns, place, preferred_element_type=jnp.float32).astype(jnp.bfloat16)


def smooth_kernel(group, block, x_ref, columns_ref, w_ref, out_ref, energy_ref):
    step = pl.program_id(0)
    total = [None]

    def store(j, values):
        out_ref[:, j * TILE : (j + 1) * TILE] = values.astype(jnp.bfloat16)
        squares = lane_pairs(values)
        total[0] = squares if j == 0 else total[0] + squares

    smooth_rows(x_ref, halo_tile(columns_ref), w_ref, store)
    for g in range(group):
        energy_ref[pl.ds(step * group + g, 1), :] = row_sums(total[0][g * block : (g + 1) * block, :])


def gram_kernel(blocks, block, info_ref, rel_ref, down_ref, up_ref, down_columns_ref, up_columns_ref, w_ref, energy_ref,
                smoothed_ref, keep_ref, give_ref, held, wide, table, sems):
    core = info_ref[0]
    slots, chips, share = wide.shape[:3]
    units = keep_ref.shape[0] - slots
    parts = sems.shape[0]
    count = blocks // parts
    copies = [
        pltpu.make_async_copy(
            smoothed_ref.at[pl.ds(p * count, count)], held.at[pl.ds(REACH + p * count, count)], sems.at[p]
        )
        for p in range(parts)
    ]
    for copy in copies:
        copy.start()

    table[...] = jnp.zeros_like(table)
    table[REACH : REACH + blocks, :] = energy_ref[...]
    for first, x_ref, columns_ref in ((0, down_ref, down_columns_ref), (REACH + blocks, up_ref, up_columns_ref)):
        total = [None]

        def store(j, values):
            rounded = values.astype(jnp.bfloat16).reshape(REACH, block, TILE)
            held[first : first + REACH, :, j * TILE : (j + 1) * TILE] = rounded
            squares = lane_pairs(values)
            total[0] = squares if j == 0 else total[0] + squares

        smooth_rows(x_ref, halo_tile(columns_ref), w_ref, store)
        for k in range(REACH):
            table[first + k : first + k + 1, :] = row_sums(total[0][k * block : (k + 1) * block, :])

    high, low = split(table[...])
    shape = (units, chips, share, LANES)
    keep_ref[slots:] = table[...].reshape(shape)
    give_ref[slots : slots + units] = high.reshape(shape)
    give_ref[slots + units :] = low.reshape(shape)
    for copy in copies:
        copy.wait()

    def one(s, carry):
        gram = gram_of(held[rel_ref[2 * s] + REACH], held[rel_ref[2 * s + 1] + REACH])
        keep_ref[s], wide[s] = by_core(gram, chips, core)
        return carry

    lax.fori_loop(0, slots, one, 0, unroll=4)
    give_ref[:slots] = wide[...].astype(jnp.bfloat16)


def chip_kernel(slots, units, info_ref, keep_ref, got_ref, own_ref, *out_refs):
    chip = info_ref[1]
    chips, share = keep_ref.shape[1:3]
    shape = (units * chips, share, LANES)
    energies = keep_ref[slots:] + (
        got_ref[slots : slots + units].astype(jnp.float32) + got_ref[slots + units :].astype(jnp.float32)
    )
    high, low = split(energies)
    for d in range(chips):
        total = keep_ref[:slots, chip ^ d] + got_ref[:slots, chip ^ d].astype(jnp.float32)
        if d == 0:
            own_ref[:slots] = total
            own_ref[slots:] = energies.reshape(shape)
        else:
            out = out_refs[d - 1]
            out[:slots] = total.astype(jnp.bfloat16)
            out[slots : slots + units * chips] = high.reshape(shape)
            out[slots + units * chips :] = low.reshape(shape)


def score_kernel(slots, pixel_count, info_ref, rel_ref, place_ref, own_ref, *refs):
    got_refs, (table_ref, out_ref, gram, inverse) = refs[:-4], refs[-4:]
    share = gram.shape[1]
    block = table_ref.shape[1]
    e_units = inverse.shape[0] // share
    live, offset = info_ref[2], info_ref[3]
    total = own_ref[:slots]
    energies = own_ref[slots:]
    for got in got_refs:
        total = total + got[:slots].astype(jnp.float32)
        energies = energies + (
            got[slots : slots + e_units].astype(jnp.float32) + got[slots + e_units :].astype(jnp.float32)
        )
    gram[...] = total
    inverse[...] = (1.0 / jnp.sqrt(energies / pixel_count + 1e-06)).reshape(inverse.shape)
    lane = lax.broadcasted_iota(jnp.int32, (share, LANES), 1)
    mine = lane == lax.broadcasted_iota(jnp.int32, (share, LANES), 0) + offset

    def one(s, carry):
        inv_a = inverse[pl.ds(rel_ref[2 * s] + REACH, 1), :]
        inv_b = inverse[pl.ds(rel_ref[2 * s + 1] + REACH, 1), :]
        inv_a = jnp.sum(jnp.where(mine, inv_a, 0.0), axis=1, keepdims=True)
        coloc = (gram[s] * inv_a * inv_b / pixel_count).astype(jnp.bfloat16)
        matrix = table_ref[pl.ds(pl.multiple_of(place_ref[s], block), block), :]
        scores = jnp.dot(coloc, matrix, preferred_element_type=jnp.float32)
        out_ref[s] = jnp.where(s < live, scores, 0.0).astype(jnp.bfloat16)
        return carry

    lax.fori_loop(0, slots, one, 0, unroll=4)


def on_device(images, stencil, pairs, live, rule_of_block, adduct):
    rows, width = images.shape
    rules_here, block, _ = adduct.shape
    blocks = rows // block
    slots = pairs.shape[0]
    n_pix, n_ion = lax.axis_size("pix"), lax.axis_size("ion")
    pix, ion = lax.axis_index("pix"), lax.axis_index("ion")
    pixel_count = width * n_pix
    chips, share = n_pix // 2, block // n_pix
    core, chip = pix % 2, pix // 2
    edge = REACH * block

    def shifted(axis, size, up, value):
        steps = [(i, i + 1) if up else (i + 1, i) for i in range(size - 1)]
        return lax.ppermute(value, axis, steps)

    vmem = pl.BlockSpec(memory_space=pltpu.VMEM)
    smem = pl.BlockSpec(memory_space=pltpu.SMEM)
    hbm = pl.BlockSpec(memory_space=pl.ANY)
    edge_rows = jax.ShapeDtypeStruct((edge, width), images.dtype)
    edge_columns = jax.ShapeDtypeStruct((8, rows), images.dtype)
    top, bottom, head, tail = pl.pallas_call(
        functools.partial(cut_kernel, edge),
        grid=(1,),
        in_specs=[
            hbm,
            pl.BlockSpec((rows, LANES), lambda i: (0, 0)),
            pl.BlockSpec((rows, LANES), lambda i: (0, width // LANES - 1)),
        ],
        out_specs=[hbm, hbm, whole((8, rows)), whole((8, rows))],
        out_shape=[edge_rows, edge_rows, edge_columns, edge_columns],
        scratch_shapes=[pltpu.SemaphoreType.DMA((2,))],
        compiler_params=params(),
        name="cut_edges",
    )(images, images, images)

    before = shifted("pix", n_pix, True, tail[6:])
    after = shifted("pix", n_pix, False, head[:2])
    down = shifted("ion", n_ion, True, bottom)
    up = shifted("ion", n_ion, False, top)
    columns = jnp.concatenate([after, jnp.zeros((4, rows), images.dtype), before], axis=0)
    down_columns = shifted("ion", n_ion, True, columns[:, rows - edge :])
    up_columns = shifted("ion", n_ion, False, columns[:, :edge])

    flat = adduct.reshape(rules_here * block, block)
    part = rules_here * block // n_pix
    flat = lax.dynamic_slice_in_dim(flat, pix * part, part, 0)
    table, distance = flat, 1
    while distance < n_ion:
        other = lax.ppermute(table, "ion", [(i, i ^ distance) for i in range(n_ion)])
        table, distance = jnp.concatenate([table, other], axis=0), 2 * distance
    table = lax.all_gather(table, "pix", axis=0, tiled=True)
    rules = jnp.take(rule_of_block, pairs[:, 1], axis=0)
    if part % block == 0:
        row = rules % rules_here * block
        place = (row // part * n_ion + ((rules // rules_here) ^ ion)) * part + row % part
    else:
        table = table.reshape(n_pix, n_ion, part, block).swapaxes(0, 1).reshape(-1, block)
        place = (((rules // rules_here) ^ ion) * rules_here + rules % rules_here) * block

    weights = pl.pallas_call(
        weights_kernel,
        out_shape=jax.ShapeDtypeStruct((width // TILE, DEPTH, TILE), jnp.bfloat16),
        compiler_params=params(),
        cost_estimate=cost(0, width * DEPTH * 2),
        name="band_weights",
    )(stencil)

    info = jnp.stack([core, chip, live[0], pix * share]).astype(jnp.int32)
    relative = (pairs - ion * blocks).reshape(-1)
    group = next(g for g in (4, 2, 1) if blocks % g == 0)
    steps = blocks // group
    units = -(-2 * (blocks + 2 * REACH) // block)
    half = (chips, share, LANES)
    keep_shape = (slots + units, *half)
    give_shape = (slots + 2 * units, *half)

    def rows_at(columns):
        return pl.BlockSpec((group * block, columns), lambda i: (i, 0))

    smoothed, energy = pl.pallas_call(
        functools.partial(smooth_kernel, group, block),
        grid=(steps,),
        in_specs=[rows_at(width), pl.BlockSpec((8, group * block), lambda i: (0, i)), whole(weights.shape)],
        out_specs=[rows_at(width), whole((blocks, LANES))],
        out_shape=[
            jax.ShapeDtypeStruct((rows, width), jnp.bfloat16),
            jax.ShapeDtypeStruct((blocks, LANES), jnp.float32),
        ],
        compiler_params=params(),
        cost_estimate=cost(2 * rows * width * DEPTH, 4 * rows * width),
        name="smooth",
    )(images, columns, weights)

    keep, give = pl.pallas_call(
        functools.partial(gram_kernel, blocks, block),
        in_specs=[smem, smem] + [vmem] * 6 + [hbm],
        out_specs=[vmem, vmem],
        out_shape=[jax.ShapeDtypeStruct(keep_shape, jnp.float32), jax.ShapeDtypeStruct(give_shape, jnp.bfloat16)],
        scratch_shapes=[
            pltpu.VMEM((blocks + 2 * REACH, block, width), jnp.bfloat16),
            pltpu.VMEM((slots, *half), jnp.float32),
            pltpu.VMEM((units * block // 2, LANES), jnp.float32),
            pltpu.SemaphoreType.DMA((2,)),
        ],
        compiler_params=params(),
        cost_estimate=cost(4 * edge * width * DEPTH + 2 * slots * block * block * width, 2 * rows * width),
        name="grams",
    )(info, relative, down, up, down_columns, up_columns, weights, energy, smoothed.reshape(blocks, block, width))

    got = lax.ppermute(give, "pix", [(i, i ^ 1) for i in range(n_pix)])
    message = jax.ShapeDtypeStruct((slots + 2 * units * chips, share, LANES), jnp.bfloat16)
    own, *messages = pl.pallas_call(
        functools.partial(chip_kernel, slots, units),
        in_specs=[smem, vmem, vmem],
        out_specs=[vmem] * chips,
        out_shape=[jax.ShapeDtypeStruct((slots + units * chips, share, LANES), jnp.float32)]
        + [message] * (chips - 1),
        compiler_params=params(),
        name="chip_sums",
    )(info, keep, got)
    received = [
        lax.ppermute(m, "pix", [(i, i ^ (2 * (d + 1))) for i in range(n_pix)]) for d, m in enumerate(messages)
    ]

    scores = pl.pallas_call(
        functools.partial(score_kernel, slots, pixel_count),
        in_specs=[smem, smem, smem] + [vmem] * (chips + 1),
        out_specs=vmem,
        out_shape=jax.ShapeDtypeStruct((slots, share, block), jnp.bfloat16),
        scratch_shapes=[
            pltpu.VMEM((slots, share, LANES), jnp.float32),
            pltpu.VMEM((units * block // 2, LANES), jnp.float32),
        ],
        compiler_params=params(),
        name="scores",
    )(info, relative, place, own, *received, table)
    return (smoothed, scores)


def solution(mesh):
    return jax.shard_map(
        on_device,
        mesh=mesh,
        in_specs=(
            P("ion", "pix"),
            P(None, "pix"),
            P("ion", None),
            P("ion"),
            P(),
            P("ion", None, None),
        ),
        out_specs=(P("ion", "pix"), P("ion", "pix", None)),
        check_vma=False,
    )
```

```python
import functools

import jax
import jax.numpy as jnp
from jax import lax
from jax.experimental import pallas as pl
from jax.experimental.pallas import tpu as pltpu
from jax.sharding import PartitionSpec as P

REACH = 3
TAPS = 5
LANES = 128
HALF = LANES // 2
TILE = 2 * LANES
DEPTH = 6 * LANES
VMEM_BYTES = 58 * 1024 * 1024


def params():
    return pltpu.CompilerParams(vmem_limit_bytes=VMEM_BYTES)


def cost(flops, moved):
    return pl.CostEstimate(flops=flops, bytes_accessed=moved, transcendentals=0)


def whole(shape):
    return pl.BlockSpec(shape, lambda *_: (0,) * len(shape))


def split(values):
    high = values.astype(jnp.bfloat16)
    return high, (values - high.astype(jnp.float32)).astype(jnp.bfloat16)


def weights_kernel(stencil_ref, out_ref):
    k = lax.broadcasted_iota(jnp.int32, (TILE, TILE), 0)
    n = lax.broadcasted_iota(jnp.int32, (TILE, TILE), 1)
    inner = k - n + 2
    k, n = k[:LANES], n[:LANES]
    outer = k - n + jnp.where(k < HALF, TILE + 2, 2 - LANES)
    for j in range(out_ref.shape[0]):
        taps = stencil_ref[:, j * TILE : (j + 1) * TILE]
        main = jnp.zeros((TILE, TILE), jnp.float32)
        edge = jnp.zeros((LANES, TILE), jnp.float32)
        for t in range(TAPS):
            main = jnp.where(inner == t, taps[t : t + 1, :], main)
            edge = jnp.where(outer == t, taps[t : t + 1, :], edge)
        out_ref[j, :TILE], out_ref[j, TILE : 2 * TILE] = split(main)
        out_ref[j, 2 * TILE : 2 * TILE + LANES], out_ref[j, 2 * TILE + LANES :] = split(edge)


def smooth_rows(x_ref, halo, w_ref, store):
    rows, width = x_ref.shape
    tiles = width // TILE
    first = lax.broadcasted_iota(jnp.int32, (rows, LANES), 1) < HALF
    for j in range(tiles):
        own = x_ref[:, j * TILE : (j + 1) * TILE]
        before = halo if j == 0 else x_ref[:, j * TILE - LANES : j * TILE]
        after = halo if j == tiles - 1 else x_ref[:, (j + 1) * TILE : (j + 1) * TILE + LANES]
        edge = jnp.where(first, after, before)
        window = jnp.concatenate([own, own, edge, edge], axis=1)
        store(j, jnp.dot(window, w_ref[j], preferred_element_type=jnp.float32))


def lane_pairs(values):
    squares = values * values
    return squares[:, :LANES] + squares[:, LANES:]


def row_sums(part):
    return jnp.sum(part.T, axis=0, keepdims=True)


def gram_of(left, right):
    return lax.dot_general(
        left, right, (((1,), (1,)), ((), ())), preferred_element_type=jnp.float32
    )


def by_core(gram, chips, core):
    parts = gram.reshape(chips, 2, gram.shape[0] // (2 * chips), gram.shape[1])
    return jnp.where(core == 0, parts[:, 0], parts[:, 1]), jnp.where(core == 0, parts[:, 1], parts[:, 0])


def cut_kernel(images_ref, top_ref, bottom_ref, head_ref, tail_ref, strips, bands, sems):
    rows, width = images_ref.shape
    edge = top_ref.shape[0]
    reads = [
        pltpu.make_async_copy(images_ref.at[:, pl.ds(0, LANES)], strips.at[0], sems.at[0]),
        pltpu.make_async_copy(images_ref.at[:, pl.ds(width - LANES, LANES)], strips.at[1], sems.at[1]),
        pltpu.make_async_copy(images_ref.at[pl.ds(0, edge)], bands.at[0], sems.at[2]),
        pltpu.make_async_copy(images_ref.at[pl.ds(rows - edge, edge)], bands.at[1], sems.at[3]),
    ]
    writes = [
        pltpu.make_async_copy(bands.at[0], top_ref, sems.at[4]),
        pltpu.make_async_copy(bands.at[1], bottom_ref, sems.at[5]),
    ]
    for copy in reads:
        copy.start()
    row = lax.broadcasted_iota(jnp.int32, (8, LANES), 0)
    lane = lax.broadcasted_iota(jnp.int32, (8, LANES), 1)
    for k, (out, shift) in enumerate(((head_ref, 0), (tail_ref, LANES - 8))):
        reads[k].wait()
        pick = (lane == row + shift).astype(jnp.bfloat16)
        out[...] = gram_of(pick, strips[k]).astype(jnp.bfloat16)
    for k in range(2):
        reads[2 + k].wait()
        writes[k].start()
    for copy in writes:
        copy.wait()


def halo_tile(columns_ref):
    columns = columns_ref[...].astype(jnp.float32).T.astype(jnp.bfloat16)
    row = lax.broadcasted_iota(jnp.int32, (8, LANES), 0)
    lane = lax.broadcasted_iota(jnp.int32, (8, LANES), 1)
    place = (lane == row + jnp.where(row < 4, 0, LANES - 8)).astype(jnp.bfloat16)
    return jnp.dot(columns, place, preferred_element_type=jnp.float32).astype(jnp.bfloat16)


def main_kernel(steps, group, block, pairs_ref, x_ref, columns_ref, w_ref,
                out_ref, energy_ref, keep_ref, give_ref, held, wide):
    step = pl.program_id(0)
    blocks = steps * group
    slots, chips = wide.shape[:2]

    @pl.when(step < steps)
    def smooth():
        total = [None]

        def store(j, values):
            columns = slice(j * TILE, (j + 1) * TILE)
            rounded = values.astype(jnp.bfloat16)
            out_ref[:, columns] = rounded
            held[pl.ds(step * group, group), :, columns] = rounded.reshape(group, block, TILE)
            squares = lane_pairs(values)
            total[0] = squares if j == 0 else total[0] + squares

        smooth_rows(x_ref, halo_tile(columns_ref), w_ref, store)
        for g in range(group):
            energy_ref[pl.ds(step * group + g, 1), :] = row_sums(total[0][g * block : (g + 1) * block, :])

    @pl.when(step == steps)
    def grams():
        core = lax.axis_index("pix") % 2
        first = lax.axis_index("ion") * blocks

        def one(s, carry):
            a = pairs_ref[0, s] - first
            b = jnp.clip(pairs_ref[1, s] - first, 0, blocks - 1)
            keep_ref[s], wide[s] = by_core(gram_of(held[a], held[b]), chips, core)
            return carry

        lax.fori_loop(0, slots, one, 0, unroll=4)
        give_ref[:slots] = wide[...].astype(jnp.bfloat16)


def cross_kernel(blocks, block, pairs_ref, down_ref, up_ref, down_columns_ref, up_columns_ref, w_ref, energy_ref,
                 smoothed_ref, keep_in, give_in, keep_ref, give_ref, near, own, table, keep_part, give_part, sems):
    del keep_in, give_in
    core = lax.axis_index("pix") % 2
    first_block = lax.axis_index("ion") * blocks
    slots = pairs_ref.shape[1]
    chips, share = keep_part.shape[1:3]
    units = 2 * table.shape[0] // block
    edge = REACH * block
    rows = blocks * block
    copies = [
        pltpu.make_async_copy(smoothed_ref.at[pl.ds(0, edge)], own.at[0], sems.at[0]),
        pltpu.make_async_copy(smoothed_ref.at[pl.ds(rows - edge, edge)], own.at[1], sems.at[1]),
    ]
    for copy in copies:
        copy.start()

    table[...] = jnp.zeros_like(table)
    table[REACH : REACH + blocks, :] = energy_ref[...]
    for side, (x_ref, columns_ref) in enumerate(((down_ref, down_columns_ref), (up_ref, up_columns_ref))):
        total = [None]

        def store(j, values):
            near[side, :, j * TILE : (j + 1) * TILE] = values.astype(jnp.bfloat16)
            squares = lane_pairs(values)
            total[0] = squares if j == 0 else total[0] + squares

        smooth_rows(x_ref, halo_tile(columns_ref), w_ref, store)
        for k in range(REACH):
            row = side * (REACH + blocks) + k
            table[row : row + 1, :] = row_sums(total[0][k * block : (k + 1) * block, :])
    for copy in copies:
        copy.wait()

    high, low = split(table[...])
    shape = (units, chips, share, LANES)
    keep_part[:units] = table[...].reshape(shape)
    give_part[:units] = high.reshape(shape)
    give_part[units:] = low.reshape(shape)
    copies = [
        pltpu.make_async_copy(keep_part.at[pl.ds(0, units)], keep_ref.at[pl.ds(slots, units)], sems.at[0]),
        pltpu.make_async_copy(give_part, give_ref.at[pl.ds(slots, 2 * units)], sems.at[1]),
    ]
    for copy in copies:
        copy.start()
    for copy in copies:
        copy.wait()

    def one(s, carry):
        a, b = pairs_ref[0, s] - first_block, pairs_ref[1, s] - first_block

        @pl.when((b < 0) | (b >= blocks))
        def crossing():
            side = (b >= 0).astype(jnp.int32)
            a_row = pl.multiple_of((a - side * (blocks - REACH)) * block, block)
            b_row = pl.multiple_of((b + REACH - side * (blocks + REACH)) * block, block)
            gram = gram_of(own[side, pl.ds(a_row, block), :], near[side, pl.ds(b_row, block), :])
            mine, other = by_core(gram, chips, core)
            keep_part[0] = mine
            give_part[0] = other.astype(jnp.bfloat16)
            first = pltpu.make_async_copy(keep_part.at[0], keep_ref.at[s], sems.at[0])
            second = pltpu.make_async_copy(give_part.at[0], give_ref.at[s], sems.at[1])
            first.start()
            second.start()
            first.wait()
            second.wait()

        return carry

    lax.fori_loop(0, slots, one, 0)


def fetch(sources, targets, sems):
    copies = [pltpu.make_async_copy(x, y, sems.at[k]) for k, (x, y) in enumerate(zip(sources, targets))]
    for copy in copies:
        copy.start()
    return copies


def chip_kernel(slots, units, keep_hbm, got_hbm, own_ref, *refs):
    out_refs, (keep_ref, got_ref, sems) = refs[:-3], refs[-3:]
    chip = lax.axis_index("pix") // 2
    chips, share = keep_ref.shape[1:3]
    shape = (units * chips, share, LANES)
    for copy in fetch((keep_hbm, got_hbm), (keep_ref, got_ref), sems):
        copy.wait()
    energies = keep_ref[slots:] + (
        got_ref[slots : slots + units].astype(jnp.float32) + got_ref[slots + units :].astype(jnp.float32)
    )
    high, low = split(energies)
    for d in range(chips):
        total = keep_ref[:slots, chip ^ d] + got_ref[:slots, chip ^ d].astype(jnp.float32)
        if d == 0:
            own_ref[:slots] = total
            own_ref[slots:] = energies.reshape(shape)
        else:
            out = out_refs[d - 1]
            out[:slots] = total.astype(jnp.bfloat16)
            out[slots : slots + units * chips] = high.reshape(shape)
            out[slots + units * chips :] = low.reshape(shape)


def score_kernel(blocks, place_of, pixel_count, pairs_ref, live_ref, rules_ref, *refs):
    chips = (len(refs) - 7) // 2
    sources, refs = refs[: chips + 2], refs[chips + 2 :]
    out_ref, own_ref, got_refs, table_ref, gram, inverse, sems = (
        refs[0], refs[1], refs[2 : chips + 1], refs[-4], refs[-3], refs[-2], refs[-1]
    )
    slots, share = gram.shape[:2]
    block = out_ref.shape[2]
    e_units = inverse.shape[0] // share
    half = table_ref.shape[0] // 2
    targets = (own_ref, *got_refs, table_ref.at[pl.ds(0, half)], table_ref.at[pl.ds(half, half)])
    copies = fetch(sources, targets, sems)
    pix, first = lax.axis_index("pix"), lax.axis_index("ion") * blocks
    for copy in copies[:-2]:
        copy.wait()
    total = own_ref[:slots]
    energies = own_ref[slots:]
    for got in got_refs:
        total = total + got[:slots].astype(jnp.float32)
        energies = energies + (
            got[slots : slots + e_units].astype(jnp.float32) + got[slots + e_units :].astype(jnp.float32)
        )
    gram[...] = total
    inverse[...] = (1.0 / jnp.sqrt(energies / pixel_count + 1e-06)).reshape(inverse.shape)
    lane = lax.broadcasted_iota(jnp.int32, (share, LANES), 1)
    mine = lane == lax.broadcasted_iota(jnp.int32, (share, LANES), 0) + pix * share
    for copy in copies[-2:]:
        copy.wait()

    def one(s, carry):
        a, b = pairs_ref[0, s], pairs_ref[1, s]
        inv_a = inverse[pl.ds(a - first + REACH, 1), :]
        inv_b = inverse[pl.ds(b - first + REACH, 1), :]
        inv_a = jnp.sum(jnp.where(mine, inv_a, 0.0), axis=1, keepdims=True)
        coloc = (gram[s] * inv_a * inv_b / pixel_count).astype(jnp.bfloat16)
        scores = jnp.zeros((share, block), jnp.float32)
        pieces = place_of(rules_ref[b])
        depth = block // len(pieces)
        for k, at in enumerate(pieces):
            matrix = table_ref[pl.ds(pl.multiple_of(at, depth), depth), :]
            part = coloc[:, k * depth : (k + 1) * depth]
            scores = scores + jnp.dot(part, matrix, preferred_element_type=jnp.float32)
        out_ref[s] = jnp.where(s < live_ref[0], scores, 0.0).astype(jnp.bfloat16)
        return carry

    lax.fori_loop(0, slots, one, 0, unroll=8)


def on_device(images, stencil, pairs, live, rule_of_block, adduct):
    rows, width = images.shape
    rules_here, block, _ = adduct.shape
    blocks = rows // block
    slots = pairs.shape[0]
    n_pix, n_ion = lax.axis_size("pix"), lax.axis_size("ion")
    pix, ion = lax.axis_index("pix"), lax.axis_index("ion")
    pixel_count = width * n_pix
    chips, share = n_pix // 2, block // n_pix
    core, chip = pix % 2, pix // 2
    edge = REACH * block

    def shifted(axis, size, up, value):
        steps = [(i, i + 1) if up else (i + 1, i) for i in range(size - 1)]
        return lax.ppermute(value, axis, steps)

    vmem = pl.BlockSpec(memory_space=pltpu.VMEM)
    smem = pl.BlockSpec(memory_space=pltpu.SMEM)
    hbm = pl.BlockSpec(memory_space=pl.ANY)
    edge_rows = jax.ShapeDtypeStruct((edge, width), images.dtype)
    edge_columns = jax.ShapeDtypeStruct((8, rows), images.dtype)
    top, bottom, head, tail = pl.pallas_call(
        cut_kernel,
        in_specs=[hbm],
        out_specs=[hbm, hbm, vmem, vmem],
        out_shape=[edge_rows, edge_rows, edge_columns, edge_columns],
        scratch_shapes=[
            pltpu.VMEM((2, rows, LANES), images.dtype),
            pltpu.VMEM((2, edge, width), images.dtype),
            pltpu.SemaphoreType.DMA((6,)),
        ],
        compiler_params=params(),
        cost_estimate=cost(0, 8 * edge * width),
        name="cut_edges",
    )(images)

    before = shifted("pix", n_pix, True, tail[6:])
    after = shifted("pix", n_pix, False, head[:2])
    down = shifted("ion", n_ion, True, bottom)
    up = shifted("ion", n_ion, False, top)
    columns = jnp.concatenate([after, jnp.zeros((4, rows), images.dtype), before], axis=0)
    down_columns = shifted("ion", n_ion, True, columns[:, rows - edge :])
    up_columns = shifted("ion", n_ion, False, columns[:, :edge])

    flat = adduct.reshape(rules_here * block, block)
    part = rules_here * block // n_pix
    mine = lax.dynamic_slice_in_dim(flat, pix * part, part, 0)
    axes = []
    for axis, size, index in (("ion", n_ion, ion), ("pix", n_pix, pix)):
        distances = [2**k for k in range(size.bit_length() - 1)]
        axes += [(axis, size, d) for d in (distances if axis == "ion" else distances[::-1])]
    for k, (axis, size, distance) in enumerate(axes):
        other = lax.ppermute(mine, axis, [(i, i ^ distance) for i in range(size)])
        if k < len(axes) - 1:
            mine = jnp.concatenate([mine, other], axis=0)

    def place_of(rule):
        here = {"ion": lax.axis_index("ion"), "pix": lax.axis_index("pix")}
        row = rule % rules_here * block
        pieces = []
        for offset in range(0, block, min(part, block)):
            from_ = {"ion": rule // rules_here, "pix": (row + offset) // part}
            at = (row + offset) % part
            for k, (axis, _, distance) in enumerate(axes):
                at = at + (((from_[axis] ^ here[axis]) // distance) % 2) * (part << k)
            pieces.append(at)
        return pieces

    weights = pl.pallas_call(
        weights_kernel,
        out_shape=jax.ShapeDtypeStruct((width // TILE, DEPTH, TILE), jnp.bfloat16),
        compiler_params=params(),
        cost_estimate=cost(0, width * DEPTH * 2),
        name="band_weights",
    )(stencil)

    table_pairs = pairs.T
    group = next(g for g in (8, 5, 4, 2, 1) if blocks % g == 0)
    steps = blocks // group
    units = -(-2 * (blocks + 2 * REACH) // block)
    half = (chips, share, LANES)
    keep_shape = (slots + units, *half)
    give_shape = (slots + 2 * units, *half)

    def rows_at(columns):
        return pl.BlockSpec((group * block, columns), lambda i, *_: (jnp.minimum(i, steps - 1), 0))

    smoothed, energy, keep, give = pl.pallas_call(
        functools.partial(main_kernel, steps, group, block),
        grid_spec=pltpu.PrefetchScalarGridSpec(
            num_scalar_prefetch=1,
            grid=(steps + 1,),
            in_specs=[
                rows_at(width),
                pl.BlockSpec((8, group * block), lambda i, *_: (0, jnp.minimum(i, steps - 1))),
                whole(weights.shape),
            ],
            out_specs=[rows_at(width), whole((blocks, LANES)), whole(keep_shape), whole(give_shape)],
            scratch_shapes=[
                pltpu.VMEM((blocks, block, width), jnp.bfloat16),
                pltpu.VMEM((slots, *half), jnp.float32),
            ],
        ),
        out_shape=[
            jax.ShapeDtypeStruct((rows, width), jnp.bfloat16),
            jax.ShapeDtypeStruct((blocks, LANES), jnp.float32),
            jax.ShapeDtypeStruct(keep_shape, jnp.float32),
            jax.ShapeDtypeStruct(give_shape, jnp.bfloat16),
        ],
        compiler_params=params(),
        cost_estimate=cost(2 * rows * width * DEPTH + 2 * slots * block * block * width, 4 * rows * width),
        name="smooth_and_gram",
    )(table_pairs, images, columns, weights)

    keep, give = pl.pallas_call(
        functools.partial(cross_kernel, blocks, block),
        in_specs=[smem] + [vmem] * 6 + [hbm] * 3,
        out_specs=[hbm, hbm],
        out_shape=[jax.ShapeDtypeStruct(keep_shape, jnp.float32), jax.ShapeDtypeStruct(give_shape, jnp.bfloat16)],
        input_output_aliases={8: 0, 9: 1},
        scratch_shapes=[
            pltpu.VMEM((2, edge, width), jnp.bfloat16),
            pltpu.VMEM((2, edge, width), jnp.bfloat16),
            pltpu.VMEM((units * block // 2, LANES), jnp.float32),
            pltpu.VMEM((units, *half), jnp.float32),
            pltpu.VMEM((2 * units, *half), jnp.bfloat16),
            pltpu.SemaphoreType.DMA((2,)),
        ],
        compiler_params=params(),
        cost_estimate=cost(4 * edge * width * DEPTH, 8 * edge * width),
        name="cross_grams",
    )(table_pairs, down, up, down_columns, up_columns, weights, energy, smoothed, keep, give)

    got = lax.ppermute(give, "pix", [(i, i ^ 1) for i in range(n_pix)])
    message = jax.ShapeDtypeStruct((slots + 2 * units * chips, share, LANES), jnp.bfloat16)
    own_rows = jax.ShapeDtypeStruct((slots + units * chips, share, LANES), jnp.float32)
    small = pltpu.CompilerParams(vmem_limit_bytes=16 * 1024 * 1024)
    own, *messages = pl.pallas_call(
        functools.partial(chip_kernel, slots, units),
        in_specs=[hbm, hbm],
        out_specs=[vmem] * chips,
        out_shape=[own_rows] + [message] * (chips - 1),
        scratch_shapes=[
            pltpu.VMEM(keep_shape, jnp.float32),
            pltpu.VMEM(give_shape, jnp.bfloat16),
            pltpu.SemaphoreType.DMA((2,)),
        ],
        compiler_params=small,
        name="chip_sums",
    )(keep, got)
    received = [
        lax.ppermute(m, "pix", [(i, i ^ (2 * (d + 1))) for i in range(n_pix)]) for d, m in enumerate(messages)
    ]

    scores = pl.pallas_call(
        functools.partial(score_kernel, blocks, place_of, pixel_count),
        in_specs=[smem] * 3 + [hbm] * (chips + 2),
        out_specs=vmem,
        out_shape=jax.ShapeDtypeStruct((slots, share, block), jnp.bfloat16),
        scratch_shapes=[
            pltpu.VMEM(own_rows.shape, jnp.float32),
            *[pltpu.VMEM(message.shape, jnp.bfloat16)] * (chips - 1),
            pltpu.VMEM((2 * mine.shape[0], block), jnp.bfloat16),
            pltpu.VMEM((slots, share, LANES), jnp.float32),
            pltpu.VMEM((units * block // 2, LANES), jnp.float32),
            pltpu.SemaphoreType.DMA((chips + 2,)),
        ],
        compiler_params=small,
        name="scores",
    )(table_pairs, live, rule_of_block, own, *received, mine, other)
    return (smoothed, scores)


def solution(mesh):
    return jax.shard_map(
        on_device,
        mesh=mesh,
        in_specs=(
            P("ion", "pix"),
            P(None, "pix"),
            P("ion", None),
            P("ion"),
            P(),
            P("ion", None, None),
        ),
        out_specs=(P("ion", "pix"), P("ion", "pix", None)),
        check_vma=False,
    )
```

```python
import functools

import jax
import jax.numpy as jnp
from jax import lax
from jax.experimental import pallas as pl
from jax.experimental.pallas import tpu as pltpu
from jax.sharding import PartitionSpec as P

REACH = 3
TAPS = 5
LANES = 128
HALF = LANES // 2
TILE = 2 * LANES
DEPTH = 6 * LANES
VMEM_BYTES = 58 * 1024 * 1024


def params():
    return pltpu.CompilerParams(vmem_limit_bytes=VMEM_BYTES)


def cost(flops, moved):
    return pl.CostEstimate(flops=flops, bytes_accessed=moved, transcendentals=0)


def whole(shape):
    return pl.BlockSpec(shape, lambda *_: (0,) * len(shape))


def split(values):
    high = values.astype(jnp.bfloat16)
    return high, (values - high.astype(jnp.float32)).astype(jnp.bfloat16)


def smooth_rows(x_ref, halo, w_ref, store):
    rows, width = x_ref.shape
    tiles = width // TILE
    first = lax.broadcasted_iota(jnp.int32, (rows, LANES), 1) < HALF
    for j in range(tiles):
        own = x_ref[:, j * TILE : (j + 1) * TILE]
        before = halo if j == 0 else x_ref[:, j * TILE - LANES : j * TILE]
        after = halo if j == tiles - 1 else x_ref[:, (j + 1) * TILE : (j + 1) * TILE + LANES]
        edge = jnp.where(first, after, before)
        window = jnp.concatenate([own, own, edge, edge], axis=1)
        store(j, jnp.dot(window, w_ref[j], preferred_element_type=jnp.float32))


def lane_pairs(values):
    squares = values * values
    return squares[:, :LANES] + squares[:, LANES:]


def row_sums(part):
    return jnp.sum(part.T, axis=0, keepdims=True)


def gram_of(left, right):
    return lax.dot_general(
        left, right, (((1,), (1,)), ((), ())), preferred_element_type=jnp.float32
    )


def by_core(gram, chips, core):
    parts = gram.reshape(chips, 2, gram.shape[0] // (2 * chips), gram.shape[1])
    return jnp.where(core == 0, parts[:, 0], parts[:, 1]), jnp.where(core == 0, parts[:, 1], parts[:, 0])


def write_weights(stencil_ref, out_ref):
    k = lax.broadcasted_iota(jnp.int32, (TILE, TILE), 0)
    n = lax.broadcasted_iota(jnp.int32, (TILE, TILE), 1)
    inner = k - n + 2
    k, n = k[:LANES], n[:LANES]
    outer = k - n + jnp.where(k < HALF, TILE + 2, 2 - LANES)
    for j in range(out_ref.shape[0]):
        taps = stencil_ref[:, j * TILE : (j + 1) * TILE]
        main = jnp.zeros((TILE, TILE), jnp.float32)
        edge = jnp.zeros((LANES, TILE), jnp.float32)
        for t in range(TAPS):
            main = jnp.where(inner == t, taps[t : t + 1, :], main)
            edge = jnp.where(outer == t, taps[t : t + 1, :], edge)
        out_ref[j, :TILE], out_ref[j, TILE : 2 * TILE] = split(main)
        out_ref[j, 2 * TILE : 2 * TILE + LANES], out_ref[j, 2 * TILE + LANES :] = split(edge)


def cut_kernel(images_ref, stencil_ref, top_ref, bottom_ref, head_ref, tail_ref, w_ref, strips, bands, sems):
    rows, width = images_ref.shape
    edge = top_ref.shape[0]
    reads = [
        pltpu.make_async_copy(images_ref.at[pl.ds(0, edge)], bands.at[0], sems.at[0]),
        pltpu.make_async_copy(images_ref.at[pl.ds(rows - edge, edge)], bands.at[1], sems.at[1]),
        pltpu.make_async_copy(images_ref.at[:, pl.ds(0, LANES)], strips.at[0], sems.at[2]),
        pltpu.make_async_copy(images_ref.at[:, pl.ds(width - LANES, LANES)], strips.at[1], sems.at[3]),
    ]
    writes = [
        pltpu.make_async_copy(bands.at[0], top_ref, sems.at[4]),
        pltpu.make_async_copy(bands.at[1], bottom_ref, sems.at[5]),
    ]
    for copy in reads:
        copy.start()
    write_weights(stencil_ref, w_ref)
    for k in range(2):
        reads[k].wait()
        writes[k].start()
    row = lax.broadcasted_iota(jnp.int32, (8, LANES), 0)
    lane = lax.broadcasted_iota(jnp.int32, (8, LANES), 1)
    for k, (out, shift) in enumerate(((head_ref, 0), (tail_ref, LANES - 2))):
        reads[2 + k].wait()
        pick = (lane == row + shift).astype(jnp.bfloat16)
        out[...] = gram_of(pick, strips[k])[:2].astype(jnp.bfloat16)
    for copy in writes:
        copy.wait()


def halo_tile(columns_ref):
    columns = columns_ref[...].astype(jnp.float32).T.astype(jnp.bfloat16)
    row = lax.broadcasted_iota(jnp.int32, (8, LANES), 0)
    lane = lax.broadcasted_iota(jnp.int32, (8, LANES), 1)
    place = (lane == row + jnp.where(row < 4, 0, LANES - 8)).astype(jnp.bfloat16)
    return jnp.dot(columns, place, preferred_element_type=jnp.float32).astype(jnp.bfloat16)


def main_kernel(steps, group, block, pairs_ref, x_ref, columns_ref, w_ref,
                out_ref, energy_ref, keep_ref, give_ref, held, wide):
    step = pl.program_id(0)
    blocks = steps * group
    slots, chips = wide.shape[:2]

    @pl.when(step < steps)
    def smooth():
        total = [None]

        def store(j, values):
            columns = slice(j * TILE, (j + 1) * TILE)
            rounded = values.astype(jnp.bfloat16)
            out_ref[:, columns] = rounded
            held[pl.ds(step * group, group), :, columns] = rounded.reshape(group, block, TILE)
            squares = lane_pairs(values)
            total[0] = squares if j == 0 else total[0] + squares

        smooth_rows(x_ref, halo_tile(columns_ref), w_ref, store)
        for g in range(group):
            energy_ref[pl.ds(step * group + g, 1), :] = row_sums(total[0][g * block : (g + 1) * block, :])

    @pl.when(step == steps)
    def grams():
        core = lax.axis_index("pix") % 2
        first = lax.axis_index("ion") * blocks

        def one(s, carry):
            a = pairs_ref[0, s] - first
            b = jnp.clip(pairs_ref[1, s] - first, 0, blocks - 1)
            keep_ref[s], wide[s] = by_core(gram_of(held[a], held[b]), chips, core)
            return carry

        lax.fori_loop(0, slots, one, 0, unroll=4)
        give_ref[:slots] = wide[...].astype(jnp.bfloat16)


def fetch(sources, targets, sems):
    copies = [pltpu.make_async_copy(x, y, sems.at[k]) for k, (x, y) in enumerate(zip(sources, targets))]
    for copy in copies:
        copy.start()
    return copies


def cross_kernel(blocks, block, pairs_ref, down_hbm, up_hbm, down_columns_hbm, up_columns_hbm, w_hbm, energy_hbm,
                 smoothed_hbm, keep_hbm, give_hbm, keep_ref, give_ref, x_ref, columns_ref, w_ref, energy_ref, own, near,
                 table, sems):
    core = lax.axis_index("pix") % 2
    first_block = lax.axis_index("ion") * blocks
    slots = pairs_ref.shape[1]
    chips, share = keep_ref.shape[1:3]
    units = keep_ref.shape[0] - slots
    edge = REACH * block
    rows = blocks * block
    low, high = pl.ds(0, edge), pl.ds(edge, edge)
    copies = fetch(
        (down_hbm, up_hbm, down_columns_hbm, up_columns_hbm, w_hbm, energy_hbm, smoothed_hbm.at[low],
         smoothed_hbm.at[pl.ds(rows - edge, edge)], keep_hbm, give_hbm),
        (x_ref.at[low], x_ref.at[high], columns_ref.at[:, low], columns_ref.at[:, high], w_ref, energy_ref, own.at[low],
         own.at[high], keep_ref, give_ref),
        sems,
    )
    for copy in copies[:6]:
        copy.wait()
    table[...] = jnp.zeros_like(table)
    table[REACH : REACH + blocks, :] = energy_ref[...]
    total = [None]

    def store(j, values):
        near[:, j * TILE : (j + 1) * TILE] = values.astype(jnp.bfloat16)
        squares = lane_pairs(values)
        total[0] = squares if j == 0 else total[0] + squares

    smooth_rows(x_ref, halo_tile(columns_ref), w_ref, store)
    for k in range(2 * REACH):
        row = k if k < REACH else k + blocks
        table[row : row + 1, :] = row_sums(total[0][k * block : (k + 1) * block, :])
    for copy in copies[6:]:
        copy.wait()

    upper, lower = split(table[...])
    shape = (units, chips, share, LANES)
    keep_ref[slots:] = table[...].reshape(shape)
    give_ref[slots : slots + units] = upper.reshape(shape)
    give_ref[slots + units :] = lower.reshape(shape)

    def one(s, carry):
        a, b = pairs_ref[0, s] - first_block, pairs_ref[1, s] - first_block

        @pl.when((b < 0) | (b >= blocks))
        def crossing():
            side = (b >= 0).astype(jnp.int32)
            a_row = pl.multiple_of((a - side * (blocks - 2 * REACH)) * block, block)
            b_row = pl.multiple_of((b + REACH - side * blocks) * block, block)
            gram = gram_of(own[pl.ds(a_row, block), :], near[pl.ds(b_row, block), :])
            mine, other = by_core(gram, chips, core)
            keep_ref[s] = mine
            give_ref[s] = other.astype(jnp.bfloat16)

        return carry

    lax.fori_loop(0, slots, one, 0)


def chip_kernel(slots, units, keep_hbm, got_hbm, own_ref, *refs):
    out_refs, (keep_ref, got_ref, sems) = refs[:-3], refs[-3:]
    chip = lax.axis_index("pix") // 2
    chips, share = keep_ref.shape[1:3]
    shape = (units * chips, share, LANES)
    for copy in fetch((keep_hbm, got_hbm), (keep_ref, got_ref), sems):
        copy.wait()
    energies = keep_ref[slots:] + (
        got_ref[slots : slots + units].astype(jnp.float32) + got_ref[slots + units :].astype(jnp.float32)
    )
    high, low = split(energies)
    for d in range(chips):
        total = keep_ref[:slots, chip ^ d] + got_ref[:slots, chip ^ d].astype(jnp.float32)
        if d == 0:
            own_ref[:slots] = total
            own_ref[slots:] = energies.reshape(shape)
        else:
            out = out_refs[d - 1]
            out[:slots] = total.astype(jnp.bfloat16)
            out[slots : slots + units * chips] = high.reshape(shape)
            out[slots + units * chips :] = low.reshape(shape)


def score_kernel(blocks, place_of, pixel_count, pairs_ref, live_ref, rules_ref, *refs):
    chips = (len(refs) - 9) // 2
    sources, out_ref, own_ref = refs[: chips + 2], refs[chips + 2], refs[chips + 3]
    got_refs, (table_ref, inverse, left, right, coloc, place, sems) = refs[chips + 4 : -7], refs[-7:]
    slots, share, block = out_ref.shape
    e_units = inverse.shape[0] // share
    half = table_ref.shape[0] // 2
    targets = (own_ref, *got_refs, table_ref.at[pl.ds(0, half)], table_ref.at[pl.ds(half, half)])
    copies = fetch(sources, targets, sems)
    pix, first = lax.axis_index("pix"), lax.axis_index("ion") * blocks
    pieces = place.shape[0]
    depth = block // pieces

    def find(s, carry):
        for k, at in enumerate(place_of(rules_ref[pairs_ref[1, s]])):
            place[k, s] = at
        return carry

    lax.fori_loop(0, slots, find, 0)
    for copy in copies[:-2]:
        copy.wait()
    gram = own_ref[:slots]
    energies = own_ref[slots:]
    for got in got_refs:
        gram = gram + got[:slots].astype(jnp.float32)
        energies = energies + (
            got[slots : slots + e_units].astype(jnp.float32) + got[slots + e_units :].astype(jnp.float32)
        )
    inverse[...] = (1.0 / jnp.sqrt(energies / pixel_count + 1e-06)).reshape(inverse.shape)

    def pick(s, carry):
        left[pl.ds(s, 1), :] = inverse[pl.ds(pairs_ref[0, s] - first + REACH, 1), :]
        right[pl.ds(s, 1), :] = inverse[pl.ds(pairs_ref[1, s] - first + REACH, 1), :]
        return carry

    lax.fori_loop(0, slots, pick, 0, unroll=8)
    lane = lax.broadcasted_iota(jnp.int32, (1, share, LANES), 2)
    mine = lane == lax.broadcasted_iota(jnp.int32, (1, share, LANES), 1) + pix * share
    inv_a = jnp.sum(jnp.where(mine, left[...][:, None, :], 0.0), axis=2, keepdims=True)
    coloc[...] = (gram * inv_a * right[...][:, None, :] / pixel_count).astype(jnp.bfloat16)
    for copy in copies[-2:]:
        copy.wait()

    def one(s, carry):
        scores = jnp.zeros((share, block), jnp.float32)
        for k in range(pieces):
            matrix = table_ref[pl.ds(pl.multiple_of(place[k, s], depth), depth), :]
            part = coloc[s, :, k * depth : (k + 1) * depth]
            scores = scores + jnp.dot(part, matrix, preferred_element_type=jnp.float32)
        out_ref[s] = jnp.where(s < live_ref[0], scores, 0.0).astype(jnp.bfloat16)
        return carry

    lax.fori_loop(0, slots, one, 0, unroll=16)


def on_device(images, stencil, pairs, live, rule_of_block, adduct):
    rows, width = images.shape
    rules_here, block, _ = adduct.shape
    blocks = rows // block
    slots = pairs.shape[0]
    n_pix, n_ion = lax.axis_size("pix"), lax.axis_size("ion")
    pix, ion = lax.axis_index("pix"), lax.axis_index("ion")
    pixel_count = width * n_pix
    chips, share = n_pix // 2, block // n_pix
    core, chip = pix % 2, pix // 2
    edge = REACH * block

    def shifted(axis, size, up, value):
        steps = [(i, i + 1) if up else (i + 1, i) for i in range(size - 1)]
        return lax.ppermute(value, axis, steps)

    vmem = pl.BlockSpec(memory_space=pltpu.VMEM)
    smem = pl.BlockSpec(memory_space=pltpu.SMEM)
    hbm = pl.BlockSpec(memory_space=pl.ANY)
    fixed = pl.BlockSpec(memory_space=pltpu.HBM)

    part = rules_here * block // n_pix
    mine = lax.dynamic_slice_in_dim(adduct.reshape(rules_here * block, block), pix * part, part, 0)
    turns = [lax.ppermute(mine, "ion", [(i, i ^ d) for i in range(n_ion)]) for d in range(1, n_ion)]

    edge_rows = jax.ShapeDtypeStruct((edge, width), images.dtype)
    edge_columns = jax.ShapeDtypeStruct((2, rows), images.dtype)
    top, bottom, head, tail, weights = pl.pallas_call(
        cut_kernel,
        in_specs=[hbm, vmem],
        out_specs=[hbm, hbm, vmem, vmem, vmem],
        out_shape=[
            edge_rows,
            edge_rows,
            edge_columns,
            edge_columns,
            jax.ShapeDtypeStruct((width // TILE, DEPTH, TILE), jnp.bfloat16),
        ],
        scratch_shapes=[
            pltpu.VMEM((2, rows, LANES), images.dtype),
            pltpu.VMEM((2, edge, width), images.dtype),
            pltpu.SemaphoreType.DMA((6,)),
        ],
        compiler_params=params(),
        cost_estimate=cost(0, 8 * edge * width),
        name="cut_edges",
    )(images, stencil)

    top, bottom, head, tail, *turns = lax.optimization_barrier((top, bottom, head, tail, *turns))
    mine = jnp.concatenate([mine, *turns], axis=0)

    before = shifted("pix", n_pix, True, tail)
    after = shifted("pix", n_pix, False, head)
    down = shifted("ion", n_ion, True, bottom)
    up = shifted("ion", n_ion, False, top)
    columns = jnp.concatenate([after, jnp.zeros((4, rows), images.dtype), before], axis=0)
    down_columns = shifted("ion", n_ion, True, columns[:, rows - edge :])
    up_columns = shifted("ion", n_ion, False, columns[:, :edge])

    distances = [n_pix >> k for k in range(1, n_pix.bit_length())]
    for distance in distances:
        other = lax.ppermute(mine, "pix", [(i, i ^ distance) for i in range(n_pix)])
        if distance > 1:
            mine = jnp.concatenate([mine, other], axis=0)

    def place_of(rule):
        row = rule % rules_here * block
        turn = (rule // rules_here) ^ lax.axis_index("ion")
        pieces = []
        for offset in range(0, block, min(part, block)):
            share_of = ((row + offset) // part) ^ lax.axis_index("pix")
            at = turn * part + (row + offset) % part
            for k, distance in enumerate(distances):
                at = at + (share_of // distance) % 2 * (n_ion * part << k)
            pieces.append(at)
        return pieces

    table_pairs = pairs.T
    group = next(g for g in (8, 5, 4, 2, 1) if blocks % g == 0)
    steps = blocks // group
    units = -(-2 * (blocks + 2 * REACH) // block)
    half = (chips, share, LANES)
    keep_shape = (slots + units, *half)
    give_shape = (slots + 2 * units, *half)

    def rows_at(columns):
        return pl.BlockSpec((group * block, columns), lambda i, *_: (jnp.minimum(i, steps - 1), 0))

    smoothed, energy, keep, give = pl.pallas_call(
        functools.partial(main_kernel, steps, group, block),
        grid_spec=pltpu.PrefetchScalarGridSpec(
            num_scalar_prefetch=1,
            grid=(steps + 1,),
            in_specs=[
                rows_at(width),
                pl.BlockSpec((8, group * block), lambda i, *_: (0, jnp.minimum(i, steps - 1))),
                whole(weights.shape),
            ],
            out_specs=[rows_at(width), whole((blocks, LANES)), whole(keep_shape), whole(give_shape)],
            scratch_shapes=[
                pltpu.VMEM((blocks, block, width), jnp.bfloat16),
                pltpu.VMEM((slots, *half), jnp.float32),
            ],
        ),
        out_shape=[
            jax.ShapeDtypeStruct((rows, width), jnp.bfloat16),
            jax.ShapeDtypeStruct((blocks, LANES), jnp.float32),
            jax.ShapeDtypeStruct(keep_shape, jnp.float32),
            jax.ShapeDtypeStruct(give_shape, jnp.bfloat16),
        ],
        compiler_params=params(),
        cost_estimate=cost(2 * rows * width * DEPTH + 2 * slots * block * block * width, 4 * rows * width),
        name="smooth_and_gram",
    )(table_pairs, images, columns, weights)

    keep, give = pl.pallas_call(
        functools.partial(cross_kernel, blocks, block),
        in_specs=[smem] + [hbm] * 4 + [fixed] * 5,
        out_specs=[vmem, vmem],
        out_shape=[jax.ShapeDtypeStruct(keep_shape, jnp.float32), jax.ShapeDtypeStruct(give_shape, jnp.bfloat16)],
        scratch_shapes=[
            pltpu.VMEM((2 * edge, width), jnp.bfloat16),
            pltpu.VMEM((8, 2 * edge), jnp.bfloat16),
            pltpu.VMEM(weights.shape, jnp.bfloat16),
            pltpu.VMEM((blocks, LANES), jnp.float32),
            pltpu.VMEM((2 * edge, width), jnp.bfloat16),
            pltpu.VMEM((2 * edge, width), jnp.bfloat16),
            pltpu.VMEM((units * block // 2, LANES), jnp.float32),
            pltpu.SemaphoreType.DMA((10,)),
        ],
        compiler_params=params(),
        cost_estimate=cost(4 * edge * width * DEPTH, 8 * edge * width),
        name="cross_grams",
    )(table_pairs, down, up, down_columns, up_columns, weights, energy, smoothed, keep, give)

    got = lax.ppermute(give, "pix", [(i, i ^ 1) for i in range(n_pix)])
    message = jax.ShapeDtypeStruct((slots + 2 * units * chips, share, LANES), jnp.bfloat16)
    own_rows = jax.ShapeDtypeStruct((slots + units * chips, share, LANES), jnp.float32)
    small = pltpu.CompilerParams(vmem_limit_bytes=16 * 1024 * 1024)
    own, *messages = pl.pallas_call(
        functools.partial(chip_kernel, slots, units),
        in_specs=[fixed, hbm],
        out_specs=[vmem] * chips,
        out_shape=[own_rows] + [message] * (chips - 1),
        scratch_shapes=[
            pltpu.VMEM(keep_shape, jnp.float32),
            pltpu.VMEM(give_shape, jnp.bfloat16),
            pltpu.SemaphoreType.DMA((2,)),
        ],
        compiler_params=small,
        name="chip_sums",
    )(keep, got)
    received = [
        lax.ppermute(m, "pix", [(i, i ^ (2 * (d + 1))) for i in range(n_pix)]) for d, m in enumerate(messages)
    ]

    scores = pl.pallas_call(
        functools.partial(score_kernel, blocks, place_of, pixel_count),
        in_specs=[smem] * 3 + [hbm] * (chips + 2),
        out_specs=vmem,
        out_shape=jax.ShapeDtypeStruct((slots, share, block), jnp.bfloat16),
        scratch_shapes=[
            pltpu.VMEM(own_rows.shape, jnp.float32),
            *[pltpu.VMEM(message.shape, jnp.bfloat16)] * (chips - 1),
            pltpu.VMEM((2 * mine.shape[0], block), jnp.bfloat16),
            pltpu.VMEM((units * block // 2, LANES), jnp.float32),
            pltpu.VMEM((slots, LANES), jnp.float32),
            pltpu.VMEM((slots, LANES), jnp.float32),
            pltpu.VMEM((slots, share, LANES), jnp.bfloat16),
            pltpu.SMEM((-(-block // part), slots), jnp.int32),
            pltpu.SemaphoreType.DMA((chips + 2,)),
        ],
        compiler_params=small,
        name="scores",
    )(table_pairs, live, rule_of_block, own, *received, mine, other)
    return (smoothed, scores)


def solution(mesh):
    return jax.shard_map(
        on_device,
        mesh=mesh,
        in_specs=(
            P("ion", "pix"),
            P(None, "pix"),
            P("ion", None),
            P("ion"),
            P(),
            P("ion", None, None),
        ),
        out_specs=(P("ion", "pix"), P("ion", "pix", None)),
        check_vma=False,
    )
```

```python
import functools

import jax
import jax.numpy as jnp
from jax import lax
from jax.experimental import pallas as pl
from jax.experimental.pallas import tpu as pltpu
from jax.sharding import PartitionSpec as P

REACH = 3
TAPS = 5
LANES = 128
HALF = LANES // 2
TILE = 2 * LANES
DEPTH = 3 * LANES
VMEM_BYTES = 58 * 1024 * 1024


def params():
    return pltpu.CompilerParams(vmem_limit_bytes=VMEM_BYTES)


def cost(flops, moved):
    return pl.CostEstimate(flops=flops, bytes_accessed=moved, transcendentals=0)


def whole(shape):
    return pl.BlockSpec(shape, lambda *_: (0,) * len(shape))


def split(values):
    high = values.astype(jnp.bfloat16)
    return high, (values - high.astype(jnp.float32)).astype(jnp.bfloat16)


def smooth_rows(x_ref, halo, w_ref, store):
    rows, width = x_ref.shape
    tiles = width // TILE
    first = lax.broadcasted_iota(jnp.int32, (rows, LANES), 1) < HALF
    for j in range(tiles):
        own = x_ref[:, j * TILE : (j + 1) * TILE]
        before = halo if j == 0 else x_ref[:, j * TILE - LANES : j * TILE]
        after = halo if j == tiles - 1 else x_ref[:, (j + 1) * TILE : (j + 1) * TILE + LANES]
        edge = jnp.where(first, after, before)
        window = jnp.concatenate([own, edge], axis=1)
        store(j, jnp.dot(window, w_ref[j], preferred_element_type=jnp.float32))


def lane_pairs(values):
    squares = values * values
    return squares[:, :LANES] + squares[:, LANES:]


def row_sums(part):
    return jnp.sum(part.T, axis=0, keepdims=True)


def gram_of(left, right):
    return lax.dot_general(
        left, right, (((1,), (1,)), ((), ())), preferred_element_type=jnp.float32
    )


def by_core(gram, chips, core):
    parts = gram.reshape(chips, 2, gram.shape[0] // (2 * chips), gram.shape[1])
    even, odd = parts[:, 0].astype(jnp.bfloat16), parts[:, 1].astype(jnp.bfloat16)
    return jnp.where(core == 0, even, odd), jnp.where(core == 0, odd, even)


def write_weights(stencil_ref, out_ref):
    out_ref[...] = jnp.zeros_like(out_ref)
    strip = 16
    places = [(0, LANES, 0, 2), (LANES, LANES, LANES, 2)]
    places += [(LANES - strip, strip, LANES, 2), (LANES, strip, 0, 2)]
    places += [(TILE + LANES - strip, strip, 0, 2 - LANES - TILE), (TILE, strip, LANES, 2)]
    for k0, rows, n0, shift in places:
        k = lax.broadcasted_iota(jnp.int32, (rows, LANES), 0) + k0
        tap = k - lax.broadcasted_iota(jnp.int32, (rows, LANES), 1) - n0 + shift
        for j in range(out_ref.shape[0]):
            taps = stencil_ref[:, j * TILE + n0 : j * TILE + n0 + LANES]
            w = jnp.zeros((rows, LANES), jnp.float32)
            for t in range(TAPS):
                w = jnp.where(tap == t, taps[t : t + 1, :], w)
            out_ref[j, k0 : k0 + rows, n0 : n0 + LANES] = w.astype(jnp.bfloat16)


def cut_kernel(images_ref, stencil_ref, top_ref, bottom_ref, head_ref, tail_ref, w_ref, strips, bands, sems):
    rows, width = images_ref.shape
    edge = top_ref.shape[0]
    reads = [
        pltpu.make_async_copy(images_ref.at[pl.ds(0, edge)], bands.at[0], sems.at[0]),
        pltpu.make_async_copy(images_ref.at[pl.ds(rows - edge, edge)], bands.at[1], sems.at[1]),
        pltpu.make_async_copy(images_ref.at[:, pl.ds(0, LANES)], strips.at[0], sems.at[2]),
        pltpu.make_async_copy(images_ref.at[:, pl.ds(width - LANES, LANES)], strips.at[1], sems.at[3]),
    ]
    writes = [
        pltpu.make_async_copy(bands.at[0], top_ref, sems.at[4]),
        pltpu.make_async_copy(bands.at[1], bottom_ref, sems.at[5]),
    ]
    for copy in reads:
        copy.start()
    write_weights(stencil_ref, w_ref)
    for k in range(2):
        reads[k].wait()
        writes[k].start()
    row = lax.broadcasted_iota(jnp.int32, (8, LANES), 0)
    lane = lax.broadcasted_iota(jnp.int32, (8, LANES), 1)
    for k, (out, shift) in enumerate(((head_ref, 0), (tail_ref, LANES - 2))):
        reads[2 + k].wait()
        pick = (lane == row + shift).astype(jnp.bfloat16)
        out[...] = gram_of(pick, strips[k])[:2].astype(jnp.bfloat16)
    for copy in writes:
        copy.wait()


def halo_tile(columns_ref):
    columns = columns_ref[...].astype(jnp.float32).T.astype(jnp.bfloat16)
    row = lax.broadcasted_iota(jnp.int32, (8, LANES), 0)
    lane = lax.broadcasted_iota(jnp.int32, (8, LANES), 1)
    place = (lane == row + jnp.where(row < 4, 0, LANES - 8)).astype(jnp.bfloat16)
    return jnp.dot(columns, place, preferred_element_type=jnp.float32).astype(jnp.bfloat16)


def main_kernel(steps, group, block, pairs_ref, x_ref, columns_ref, w_ref,
                out_ref, energy_ref, keep_ref, give_ref, held):
    step = pl.program_id(0)
    blocks = steps * group
    chips = keep_ref.shape[1]
    slots = pairs_ref.shape[1]

    @pl.when(step < steps)
    def smooth():
        total = [None]

        def store(j, values):
            columns = slice(j * TILE, (j + 1) * TILE)
            rounded = values.astype(jnp.bfloat16)
            out_ref[:, columns] = rounded
            held[pl.ds(step * group, group), :, columns] = rounded.reshape(group, block, TILE)
            squares = lane_pairs(values)
            total[0] = squares if j == 0 else total[0] + squares

        smooth_rows(x_ref, halo_tile(columns_ref), w_ref, store)
        for g in range(group):
            energy_ref[pl.ds(step * group + g, 1), :] = row_sums(total[0][g * block : (g + 1) * block, :])

    @pl.when(step == steps)
    def grams():
        core = lax.axis_index("pix") % 2
        first = lax.axis_index("ion") * blocks

        def one(s, carry):
            a = pairs_ref[0, s] - first
            b = jnp.clip(pairs_ref[1, s] - first, 0, blocks - 1)
            keep_ref[s], give_ref[s] = by_core(gram_of(held[a], held[b]), chips, core)
            return carry

        lax.fori_loop(0, slots, one, 0, unroll=4)


def fetch(sources, targets, sems):
    copies = [pltpu.make_async_copy(x, y, sems.at[k]) for k, (x, y) in enumerate(zip(sources, targets))]
    for copy in copies:
        copy.start()
    return copies


def cross_kernel(blocks, block, pairs_ref, down_hbm, up_hbm, down_columns_hbm, up_columns_hbm, w_hbm, energy_hbm,
                 smoothed_hbm, keep_hbm, give_hbm, keep_ref, give_ref, x_ref, columns_ref, w_ref, energy_ref, own, near,
                 table, sems):
    core = lax.axis_index("pix") % 2
    first_block = lax.axis_index("ion") * blocks
    slots = pairs_ref.shape[1]
    chips, share = keep_ref.shape[1:3]
    units = (keep_ref.shape[0] - slots) // 2
    edge = REACH * block
    rows = blocks * block
    low, high = pl.ds(0, edge), pl.ds(edge, edge)
    copies = fetch(
        (down_hbm, up_hbm, down_columns_hbm, up_columns_hbm, w_hbm, energy_hbm, smoothed_hbm.at[low],
         smoothed_hbm.at[pl.ds(rows - edge, edge)], keep_hbm, give_hbm),
        (x_ref.at[low], x_ref.at[high], columns_ref.at[:, low], columns_ref.at[:, high], w_ref, energy_ref, own.at[low],
         own.at[high], keep_ref, give_ref),
        sems,
    )
    for copy in copies[:6]:
        copy.wait()
    table[...] = jnp.zeros_like(table)
    table[REACH : REACH + blocks, :] = energy_ref[...]
    total = [None]

    def store(j, values):
        near[:, j * TILE : (j + 1) * TILE] = values.astype(jnp.bfloat16)
        squares = lane_pairs(values)
        total[0] = squares if j == 0 else total[0] + squares

    smooth_rows(x_ref, halo_tile(columns_ref), w_ref, store)
    for k in range(2 * REACH):
        row = k if k < REACH else k + blocks
        table[row : row + 1, :] = row_sums(total[0][k * block : (k + 1) * block, :])
    for copy in copies[6:]:
        copy.wait()

    shape = (units, chips, share, LANES)
    upper, lower = split(table[...].reshape(shape))
    for ref in (keep_ref, give_ref):
        ref[slots : slots + units] = upper
        ref[slots + units :] = lower

    def one(s, carry):
        a, b = pairs_ref[0, s] - first_block, pairs_ref[1, s] - first_block

        @pl.when((b < 0) | (b >= blocks))
        def crossing():
            side = (b >= 0).astype(jnp.int32)
            a_row = pl.multiple_of((a - side * (blocks - 2 * REACH)) * block, block)
            b_row = pl.multiple_of((b + REACH - side * blocks) * block, block)
            gram = gram_of(own[pl.ds(a_row, block), :], near[pl.ds(b_row, block), :])
            keep_ref[s], give_ref[s] = by_core(gram, chips, core)

        return carry

    lax.fori_loop(0, slots, one, 0)


def chip_kernel(slots, units, keep_hbm, got_hbm, own_ref, *refs):
    out_refs, (keep_ref, got_ref, sems) = refs[:-3], refs[-3:]
    chip = lax.axis_index("pix") // 2
    chips, share = keep_ref.shape[1:3]
    shape = (units * chips, share, LANES)
    for copy in fetch((keep_hbm, got_hbm), (keep_ref, got_ref), sems):
        copy.wait()
    energies = 0.0
    for ref in (keep_ref, got_ref):
        energies = energies + (
            ref[slots : slots + units].astype(jnp.float32) + ref[slots + units :].astype(jnp.float32)
        )
    high, low = split(energies)
    for d in range(chips):
        total = keep_ref[:slots, chip ^ d].astype(jnp.float32) + got_ref[:slots, chip ^ d].astype(jnp.float32)
        if d == 0:
            own_ref[:slots] = total
            own_ref[slots:] = energies.reshape(shape)
        else:
            out = out_refs[d - 1]
            out[:slots] = total.astype(jnp.bfloat16)
            out[slots : slots + units * chips] = high.reshape(shape)
            out[slots + units * chips :] = low.reshape(shape)


def score_kernel(blocks, place_of, pixel_count, pairs_ref, live_ref, rules_ref, *refs):
    chips = (len(refs) - 9) // 2
    sources, out_ref, own_ref = refs[: chips + 2], refs[chips + 2], refs[chips + 3]
    got_refs, (table_ref, inverse, left, right, coloc, place, sems) = refs[chips + 4 : -7], refs[-7:]
    slots, share, block = out_ref.shape
    e_units = inverse.shape[0] // share
    half = table_ref.shape[0] // 2
    targets = (own_ref, *got_refs, table_ref.at[pl.ds(0, half)], table_ref.at[pl.ds(half, half)])
    copies = fetch(sources, targets, sems)
    pix, first = lax.axis_index("pix"), lax.axis_index("ion") * blocks
    pieces = place.shape[0]
    depth = block // pieces

    def find(s, carry):
        for k, at in enumerate(place_of(rules_ref[pairs_ref[1, s]])):
            place[k, s] = at
        return carry

    lax.fori_loop(0, slots, find, 0)
    for copy in copies[:-2]:
        copy.wait()
    gram = own_ref[:slots]
    energies = own_ref[slots:]
    for got in got_refs:
        gram = gram + got[:slots].astype(jnp.float32)
        energies = energies + (
            got[slots : slots + e_units].astype(jnp.float32) + got[slots + e_units :].astype(jnp.float32)
        )
    inverse[...] = (1.0 / jnp.sqrt(energies / pixel_count + 1e-06)).reshape(inverse.shape)

    def pick(s, carry):
        left[pl.ds(s, 1), :] = inverse[pl.ds(pairs_ref[0, s] - first + REACH, 1), :]
        right[pl.ds(s, 1), :] = inverse[pl.ds(pairs_ref[1, s] - first + REACH, 1), :]
        return carry

    lax.fori_loop(0, slots, pick, 0, unroll=8)
    lane = lax.broadcasted_iota(jnp.int32, (1, share, LANES), 2)
    mine = lane == lax.broadcasted_iota(jnp.int32, (1, share, LANES), 1) + pix * share
    inv_a = jnp.sum(jnp.where(mine, left[...][:, None, :], 0.0), axis=2, keepdims=True)
    coloc[...] = (gram * inv_a * right[...][:, None, :] / pixel_count).astype(jnp.bfloat16)
    for copy in copies[-2:]:
        copy.wait()

    def one(s, carry):
        scores = jnp.zeros((share, block), jnp.float32)
        for k in range(pieces):
            matrix = table_ref[pl.ds(pl.multiple_of(place[k, s], depth), depth), :]
            part = coloc[s, :, k * depth : (k + 1) * depth]
            scores = scores + jnp.dot(part, matrix, preferred_element_type=jnp.float32)
        out_ref[s] = jnp.where(s < live_ref[0], scores, 0.0).astype(jnp.bfloat16)
        return carry

    lax.fori_loop(0, slots, one, 0, unroll=16)


def on_device(images, stencil, pairs, live, rule_of_block, adduct):
    rows, width = images.shape
    rules_here, block, _ = adduct.shape
    blocks = rows // block
    slots = pairs.shape[0]
    n_pix, n_ion = lax.axis_size("pix"), lax.axis_size("ion")
    pix, ion = lax.axis_index("pix"), lax.axis_index("ion")
    pixel_count = width * n_pix
    chips, share = n_pix // 2, block // n_pix
    core, chip = pix % 2, pix // 2
    edge = REACH * block

    def shifted(axis, size, up, value):
        steps = [(i, i + 1) if up else (i + 1, i) for i in range(size - 1)]
        return lax.ppermute(value, axis, steps)

    vmem = pl.BlockSpec(memory_space=pltpu.VMEM)
    smem = pl.BlockSpec(memory_space=pltpu.SMEM)
    hbm = pl.BlockSpec(memory_space=pl.ANY)
    fixed = pl.BlockSpec(memory_space=pltpu.HBM)

    part = rules_here * block // n_pix
    mine = lax.dynamic_slice_in_dim(adduct.reshape(rules_here * block, block), pix * part, part, 0)
    turns = [lax.ppermute(mine, "ion", [(i, i ^ d) for i in range(n_ion)]) for d in range(1, n_ion)]

    edge_rows = jax.ShapeDtypeStruct((edge, width), images.dtype)
    edge_columns = jax.ShapeDtypeStruct((2, rows), images.dtype)
    top, bottom, head, tail, weights = pl.pallas_call(
        cut_kernel,
        in_specs=[hbm, vmem],
        out_specs=[hbm, hbm, vmem, vmem, vmem],
        out_shape=[
            edge_rows,
            edge_rows,
            edge_columns,
            edge_columns,
            jax.ShapeDtypeStruct((width // TILE, DEPTH, TILE), jnp.bfloat16),
        ],
        scratch_shapes=[
            pltpu.VMEM((2, rows, LANES), images.dtype),
            pltpu.VMEM((2, edge, width), images.dtype),
            pltpu.SemaphoreType.DMA((6,)),
        ],
        compiler_params=params(),
        cost_estimate=cost(0, 8 * edge * width),
        name="cut_edges",
    )(images, stencil)

    top, bottom, head, tail, *turns = lax.optimization_barrier((top, bottom, head, tail, *turns))
    mine = jnp.concatenate([mine, *turns], axis=0)

    down = shifted("ion", n_ion, True, bottom)
    up = shifted("ion", n_ion, False, top)
    before = shifted("pix", n_pix, True, tail)
    after = shifted("pix", n_pix, False, head)
    columns = jnp.concatenate([after, jnp.zeros((4, rows), images.dtype), before], axis=0)
    down_columns = shifted("ion", n_ion, True, columns[:, rows - edge :])
    up_columns = shifted("ion", n_ion, False, columns[:, :edge])

    distances = [n_pix >> k for k in range(1, n_pix.bit_length())]
    for distance in distances:
        other = lax.ppermute(mine, "pix", [(i, i ^ distance) for i in range(n_pix)])
        if distance > 1:
            mine = jnp.concatenate([mine, other], axis=0)

    def place_of(rule):
        row = (rule & (rules_here - 1)) * block
        turn = (rule >> (rules_here.bit_length() - 1)) ^ lax.axis_index("ion")
        pieces = []
        for offset in range(0, block, min(part, block)):
            share_of = ((row + offset) >> (part.bit_length() - 1)) ^ lax.axis_index("pix")
            at = turn * part + ((row + offset) & (part - 1))
            for k, distance in enumerate(distances):
                at = at + jnp.where((share_of & distance) != 0, n_ion * part << k, 0)
            pieces.append(at)
        return pieces

    table_pairs = pairs.T
    group = next(g for g in (8, 5, 4, 2, 1) if blocks % g == 0)
    steps = blocks // group
    units = -(-2 * (blocks + 2 * REACH) // block)
    half = (chips, share, LANES)
    half_shape = (slots + 2 * units, *half)
    both_halves = [jax.ShapeDtypeStruct(half_shape, jnp.bfloat16)] * 2

    def rows_at(columns):
        return pl.BlockSpec((group * block, columns), lambda i, *_: (jnp.minimum(i, steps - 1), 0))

    smoothed, energy, keep, give = pl.pallas_call(
        functools.partial(main_kernel, steps, group, block),
        grid_spec=pltpu.PrefetchScalarGridSpec(
            num_scalar_prefetch=1,
            grid=(steps + 1,),
            in_specs=[
                rows_at(width),
                pl.BlockSpec((8, group * block), lambda i, *_: (0, jnp.minimum(i, steps - 1))),
                whole(weights.shape),
            ],
            out_specs=[rows_at(width), whole((blocks, LANES)), whole(half_shape), whole(half_shape)],
            scratch_shapes=[pltpu.VMEM((blocks, block, width), jnp.bfloat16)],
        ),
        out_shape=[
            jax.ShapeDtypeStruct((rows, width), jnp.bfloat16),
            jax.ShapeDtypeStruct((blocks, LANES), jnp.float32),
            *both_halves,
        ],
        compiler_params=params(),
        cost_estimate=cost(2 * rows * width * DEPTH + 2 * slots * block * block * width, 4 * rows * width),
        name="smooth_and_gram",
    )(table_pairs, images, columns, weights)

    keep, give = pl.pallas_call(
        functools.partial(cross_kernel, blocks, block),
        in_specs=[smem] + [hbm] * 4 + [fixed] * 5,
        out_specs=[vmem, vmem],
        out_shape=both_halves,
        scratch_shapes=[
            pltpu.VMEM((2 * edge, width), jnp.bfloat16),
            pltpu.VMEM((8, 2 * edge), jnp.bfloat16),
            pltpu.VMEM(weights.shape, jnp.bfloat16),
            pltpu.VMEM((blocks, LANES), jnp.float32),
            pltpu.VMEM((2 * edge, width), jnp.bfloat16),
            pltpu.VMEM((2 * edge, width), jnp.bfloat16),
            pltpu.VMEM((units * block // 2, LANES), jnp.float32),
            pltpu.SemaphoreType.DMA((10,)),
        ],
        compiler_params=params(),
        cost_estimate=cost(4 * edge * width * DEPTH, 8 * edge * width),
        name="cross_grams",
    )(table_pairs, down, up, down_columns, up_columns, weights, energy, smoothed, keep, give)

    got = lax.ppermute(give, "pix", [(i, i ^ 1) for i in range(n_pix)])
    message = jax.ShapeDtypeStruct((slots + 2 * units * chips, share, LANES), jnp.bfloat16)
    own_rows = jax.ShapeDtypeStruct((slots + units * chips, share, LANES), jnp.float32)
    small = pltpu.CompilerParams(vmem_limit_bytes=16 * 1024 * 1024)
    own, *messages = pl.pallas_call(
        functools.partial(chip_kernel, slots, units),
        in_specs=[fixed, hbm],
        out_specs=[vmem] * chips,
        out_shape=[own_rows] + [message] * (chips - 1),
        scratch_shapes=[
            pltpu.VMEM(half_shape, jnp.bfloat16),
            pltpu.VMEM(half_shape, jnp.bfloat16),
            pltpu.SemaphoreType.DMA((2,)),
        ],
        compiler_params=small,
        name="chip_sums",
    )(keep, got)
    received = [
        lax.ppermute(m, "pix", [(i, i ^ (2 * (d + 1))) for i in range(n_pix)]) for d, m in enumerate(messages)
    ]

    scores = pl.pallas_call(
        functools.partial(score_kernel, blocks, place_of, pixel_count),
        in_specs=[smem] * 3 + [hbm] * (chips + 2),
        out_specs=vmem,
        out_shape=jax.ShapeDtypeStruct((slots, share, block), jnp.bfloat16),
        scratch_shapes=[
            pltpu.VMEM(own_rows.shape, jnp.float32),
            *[pltpu.VMEM(message.shape, jnp.bfloat16)] * (chips - 1),
            pltpu.VMEM((2 * mine.shape[0], block), jnp.bfloat16),
            pltpu.VMEM((units * block // 2, LANES), jnp.float32),
            pltpu.VMEM((slots, LANES), jnp.float32),
            pltpu.VMEM((slots, LANES), jnp.float32),
            pltpu.VMEM((slots, share, LANES), jnp.bfloat16),
            pltpu.SMEM((-(-block // part), slots), jnp.int32),
            pltpu.SemaphoreType.DMA((chips + 2,)),
        ],
        compiler_params=small,
        name="scores",
    )(table_pairs, live, rule_of_block, own, *received, mine, other)
    return (smoothed, scores)


def solution(mesh):
    return jax.shard_map(
        on_device,
        mesh=mesh,
        in_specs=(
            P("ion", "pix"),
            P(None, "pix"),
            P("ion", None),
            P("ion"),
            P(),
            P("ion", None, None),
        ),
        out_specs=(P("ion", "pix"), P("ion", "pix", None)),
        check_vma=False,
    )
```

```python
import functools

import jax
import jax.numpy as jnp
from jax import lax
from jax.experimental import pallas as pl
from jax.experimental.pallas import tpu as pltpu
from jax.sharding import PartitionSpec as P

REACH = 3
TAPS = 5
LANES = 128
HALF = LANES // 2
TILE = 2 * LANES
DEPTH = 3 * LANES
EXTRA = 16
VMEM_BYTES = 58 * 1024 * 1024


def params():
    return pltpu.CompilerParams(vmem_limit_bytes=VMEM_BYTES)


def cost(flops, moved):
    return pl.CostEstimate(flops=flops, bytes_accessed=moved, transcendentals=0)


def whole(shape):
    return pl.BlockSpec(shape, lambda *_: (0,) * len(shape))


def fetch(sources, targets, sems):
    copies = [pltpu.make_async_copy(x, y, sems.at[k]) for k, (x, y) in enumerate(zip(sources, targets))]
    for copy in copies:
        copy.start()
    return copies


def split(values):
    high = values.astype(jnp.bfloat16)
    return high, (values - high.astype(jnp.float32)).astype(jnp.bfloat16)


def smooth_rows(x_ref, halo, w_ref, store):
    rows, width = x_ref.shape
    tiles = width // TILE
    first = lax.broadcasted_iota(jnp.int32, (rows, LANES), 1) < HALF
    last = None
    for j in range(tiles):
        own = x_ref[:, j * TILE : (j + 1) * TILE]
        before = halo if j == 0 else x_ref[:, j * TILE - LANES : j * TILE]
        after = halo if j == tiles - 1 else x_ref[:, (j + 1) * TILE : (j + 1) * TILE + LANES]
        window = jnp.concatenate([own, jnp.where(first, after, before)], axis=1)
        values = jnp.dot(window, w_ref[j], preferred_element_type=jnp.float32)
        if j > 0:
            store(j - 1, last)
        last = values
    store(tiles - 1, last)


def lane_pairs(values):
    squares = values * values
    return squares[:, :LANES] + squares[:, LANES:]


def row_sums(part):
    return jnp.sum(part.T, axis=0, keepdims=True)


def gram_of(left, right):
    return lax.dot_general(
        left, right, (((1,), (1,)), ((), ())), preferred_element_type=jnp.float32
    )


def by_core(gram, chips, core):
    parts = gram.reshape(chips, 2, gram.shape[0] // (2 * chips), gram.shape[1])
    even, odd = parts[:, 0].astype(jnp.bfloat16), parts[:, 1].astype(jnp.bfloat16)
    return jnp.where(core == 0, even, odd), jnp.where(core == 0, odd, even)


def write_weights(stencil_ref, out_ref):
    out_ref[...] = jnp.zeros_like(out_ref)
    strip = 16
    places = [(0, LANES, 0, 2), (LANES, LANES, LANES, 2)]
    places += [(LANES - strip, strip, LANES, 2), (LANES, strip, 0, 2)]
    places += [(TILE + LANES - strip, strip, 0, 2 - LANES - TILE), (TILE, strip, LANES, 2)]
    for k0, rows, n0, shift in places:
        k = lax.broadcasted_iota(jnp.int32, (rows, LANES), 0) + k0
        tap = k - lax.broadcasted_iota(jnp.int32, (rows, LANES), 1) - n0 + shift
        for j in range(out_ref.shape[0]):
            taps = stencil_ref[:, j * TILE + n0 : j * TILE + n0 + LANES]
            w = jnp.zeros((rows, LANES), jnp.float32)
            for t in range(TAPS):
                w = jnp.where(tap == t, taps[t : t + 1, :], w)
            out_ref[j, k0 : k0 + rows, n0 : n0 + LANES] = w.astype(jnp.bfloat16)


def columns_kernel(images_ref, stencil_ref, head_ref, tail_ref, w_ref, strips, sems):
    width = images_ref.shape[1]
    copies = fetch((images_ref.at[:, pl.ds(0, LANES)], images_ref.at[:, pl.ds(width - LANES, LANES)]),
                   (strips.at[0], strips.at[1]), sems)
    write_weights(stencil_ref, w_ref)
    row = lax.broadcasted_iota(jnp.int32, (8, LANES), 0)
    lane = lax.broadcasted_iota(jnp.int32, (8, LANES), 1)
    for k, (out, shift) in enumerate(((head_ref, 0), (tail_ref, LANES - 2))):
        copies[k].wait()
        pick = (lane == row + shift).astype(jnp.bfloat16)
        out[...] = gram_of(pick, strips[k])[:2].astype(jnp.bfloat16)


def message_kernel(images_ref, columns_ref, top_ref, bottom_ref, bands, sems):
    rows = images_ref.shape[0]
    edge = bands.shape[1] - EXTRA
    copies = fetch((images_ref.at[pl.ds(0, edge)], images_ref.at[pl.ds(rows - edge, edge)]),
                   (bands.at[0, pl.ds(0, edge)], bands.at[1, pl.ds(0, edge)]), sems)
    bands[:, edge:, :] = jnp.zeros((2, EXTRA, bands.shape[2]), bands.dtype)
    bands[0, edge : edge + 8, :edge] = columns_ref[:, :edge]
    bands[1, edge : edge + 8, :edge] = columns_ref[:, rows - edge :]
    writes = []
    for k, out in enumerate((top_ref, bottom_ref)):
        copies[k].wait()
        writes += [pltpu.make_async_copy(bands.at[k], out, sems.at[2 + k])]
        writes[k].start()
    for copy in writes:
        copy.wait()


def halo_tile(columns_ref):
    columns = columns_ref[...].astype(jnp.float32).T.astype(jnp.bfloat16)
    row = lax.broadcasted_iota(jnp.int32, (8, LANES), 0)
    lane = lax.broadcasted_iota(jnp.int32, (8, LANES), 1)
    place = (lane == row + jnp.where(row < 4, 0, LANES - 8)).astype(jnp.bfloat16)
    return jnp.dot(columns, place, preferred_element_type=jnp.float32).astype(jnp.bfloat16)


def main_kernel(steps, group, block, pairs_ref, x_ref, columns_ref, w_ref,
                out_hbm, energy_ref, keep_ref, give_ref, held, sems):
    step = pl.program_id(0)
    blocks = steps * group
    chips = keep_ref.shape[1]
    slots = pairs_ref.shape[1]

    def copy_out(k):
        here = pl.ds(k * group, group)
        return pltpu.make_async_copy(held.at[here], out_hbm.at[here], sems.at[k])

    @pl.when(step < steps)
    def smooth():
        total = [None]

        def store(j, values):
            columns = slice(j * TILE, (j + 1) * TILE)
            rounded = values.astype(jnp.bfloat16).reshape(group, block, TILE)
            held[pl.ds(step * group, group), :, columns] = rounded
            squares = lane_pairs(values)
            total[0] = squares if j == 0 else total[0] + squares

        smooth_rows(x_ref, halo_tile(columns_ref), w_ref, store)
        copy_out(step).start()
        for g in range(group):
            energy_ref[pl.ds(step * group + g, 1), :] = row_sums(total[0][g * block : (g + 1) * block, :])

    @pl.when(step == steps)
    def grams():
        core = lax.axis_index("pix") % 2
        first = lax.axis_index("ion") * blocks

        def one(s, carry):
            a = pairs_ref[0, s] - first
            b = jnp.clip(pairs_ref[1, s] - first, 0, blocks - 1)
            keep_ref[s], give_ref[s] = by_core(gram_of(held[a], held[b]), chips, core)
            return carry

        lax.fori_loop(0, slots, one, 0, unroll=4)
        for k in range(steps):
            copy_out(k).wait()


def cross_kernel(blocks, block, pairs_ref, down_hbm, up_hbm, w_hbm, energy_hbm, smoothed_hbm, keep_hbm,
                 give_hbm, keep_ref, give_ref, x_ref, columns_ref, w_ref, energy_ref, own, near, table, sems):
    core = lax.axis_index("pix") % 2
    first_block = lax.axis_index("ion") * blocks
    slots = pairs_ref.shape[1]
    chips, share = keep_ref.shape[1:3]
    units = (keep_ref.shape[0] - slots) // 2
    edge = REACH * block
    rows = blocks * block
    low, high = pl.ds(0, edge), pl.ds(edge, edge)
    copies = fetch(
        (down_hbm.at[low], up_hbm.at[low], down_hbm.at[pl.ds(edge, EXTRA), low], up_hbm.at[pl.ds(edge, EXTRA), low], w_hbm,
         energy_hbm, smoothed_hbm.at[low], smoothed_hbm.at[pl.ds(rows - edge, edge)], keep_hbm, give_hbm),
        (x_ref.at[low], x_ref.at[high], columns_ref.at[:, low], columns_ref.at[:, high], w_ref, energy_ref, own.at[low],
         own.at[high], keep_ref, give_ref),
        sems,
    )
    for copy in copies[:6]:
        copy.wait()
    table[...] = jnp.zeros_like(table)
    table[REACH : REACH + blocks, :] = energy_ref[...]
    total = [None]

    def store(j, values):
        near[:, j * TILE : (j + 1) * TILE] = values.astype(jnp.bfloat16)
        squares = lane_pairs(values)
        total[0] = squares if j == 0 else total[0] + squares

    smooth_rows(x_ref, halo_tile(columns_ref.at[:8]), w_ref, store)
    for k in range(2 * REACH):
        row = k if k < REACH else k + blocks
        table[row : row + 1, :] = row_sums(total[0][k * block : (k + 1) * block, :])
    for copy in copies[6:]:
        copy.wait()

    shape = (units, chips, share, LANES)
    upper, lower = split(table[...].reshape(shape))
    for ref in (keep_ref, give_ref):
        ref[slots : slots + units] = upper
        ref[slots + units :] = lower

    def one(s, carry):
        a, b = pairs_ref[0, s] - first_block, pairs_ref[1, s] - first_block

        @pl.when((b < 0) | (b >= blocks))
        def crossing():
            side = (b >= 0).astype(jnp.int32)
            a_row = pl.multiple_of((a - side * (blocks - 2 * REACH)) * block, block)
            b_row = pl.multiple_of((b + REACH - side * blocks) * block, block)
            gram = gram_of(own[pl.ds(a_row, block), :], near[pl.ds(b_row, block), :])
            keep_ref[s], give_ref[s] = by_core(gram, chips, core)

        return carry

    lax.fori_loop(0, slots, one, 0)


def chip_kernel(slots, units, keep_hbm, got_hbm, own_ref, *refs):
    out_refs, (keep_ref, got_ref, sems) = refs[:-3], refs[-3:]
    chip = lax.axis_index("pix") // 2
    chips, share = keep_ref.shape[1:3]
    shape = (units * chips, share, LANES)
    for copy in fetch((keep_hbm, got_hbm), (keep_ref, got_ref), sems):
        copy.wait()
    energies = 0.0
    for ref in (keep_ref, got_ref):
        energies = energies + (
            ref[slots : slots + units].astype(jnp.float32) + ref[slots + units :].astype(jnp.float32)
        )
    high, low = split(energies)
    for d in range(chips):
        total = keep_ref[:slots, chip ^ d].astype(jnp.float32) + got_ref[:slots, chip ^ d].astype(jnp.float32)
        if d == 0:
            own_ref[:slots] = total
            own_ref[slots:] = energies.reshape(shape)
        else:
            out = out_refs[d - 1]
            out[:slots] = total.astype(jnp.bfloat16)
            out[slots : slots + units * chips] = high.reshape(shape)
            out[slots + units * chips :] = low.reshape(shape)


def score_kernel(blocks, place_of, pixel_count, pairs_ref, live_ref, rules_ref, *refs):
    chips = (len(refs) - 9) // 2
    sources, out_ref, own_ref = refs[: chips + 2], refs[chips + 2], refs[chips + 3]
    got_refs, (table_ref, inverse, left, right, coloc, place, sems) = refs[chips + 4 : -7], refs[-7:]
    slots, share, block = out_ref.shape
    e_units = inverse.shape[0] // share
    half = table_ref.shape[0] // 2
    targets = (own_ref, *got_refs, table_ref.at[pl.ds(0, half)], table_ref.at[pl.ds(half, half)])
    copies = fetch(sources, targets, sems)
    pix, first = lax.axis_index("pix"), lax.axis_index("ion") * blocks
    pieces = place.shape[0]
    depth = block // pieces

    def find(s, carry):
        for k, at in enumerate(place_of(rules_ref[pairs_ref[1, s]])):
            place[k, s] = at
        return carry

    lax.fori_loop(0, slots, find, 0)
    for copy in copies[:-2]:
        copy.wait()
    gram = own_ref[:slots]
    energies = own_ref[slots:]
    for got in got_refs:
        gram = gram + got[:slots].astype(jnp.float32)
        energies = energies + (
            got[slots : slots + e_units].astype(jnp.float32) + got[slots + e_units :].astype(jnp.float32)
        )
    inverse[...] = (1.0 / jnp.sqrt(energies / pixel_count + 1e-06)).reshape(inverse.shape)

    def pick(s, carry):
        left[pl.ds(s, 1), :] = inverse[pl.ds(pairs_ref[0, s] - first + REACH, 1), :]
        right[pl.ds(s, 1), :] = inverse[pl.ds(pairs_ref[1, s] - first + REACH, 1), :]
        return carry

    lax.fori_loop(0, slots, pick, 0, unroll=8)
    lane = lax.broadcasted_iota(jnp.int32, (1, share, LANES), 2)
    mine = lane == lax.broadcasted_iota(jnp.int32, (1, share, LANES), 1) + pix * share
    inv_a = jnp.sum(jnp.where(mine, left[...][:, None, :], 0.0), axis=2, keepdims=True)
    coloc[...] = (gram * inv_a * right[...][:, None, :] / pixel_count).astype(jnp.bfloat16)
    for copy in copies[-2:]:
        copy.wait()

    def one(s, carry):
        scores = jnp.zeros((share, block), jnp.float32)
        for k in range(pieces):
            matrix = table_ref[pl.ds(pl.multiple_of(place[k, s], depth), depth), :]
            part = coloc[s, :, k * depth : (k + 1) * depth]
            scores = scores + jnp.dot(part, matrix, preferred_element_type=jnp.float32)
        out_ref[s] = jnp.where(s < live_ref[0], scores, 0.0).astype(jnp.bfloat16)
        return carry

    lax.fori_loop(0, slots, one, 0, unroll=slots)


def on_device(images, stencil, pairs, live, rule_of_block, adduct):
    rows, width = images.shape
    rules_here, block, _ = adduct.shape
    blocks = rows // block
    slots = pairs.shape[0]
    n_pix, n_ion = lax.axis_size("pix"), lax.axis_size("ion")
    pix, ion = lax.axis_index("pix"), lax.axis_index("ion")
    pixel_count = width * n_pix
    chips, share = n_pix // 2, block // n_pix
    core, chip = pix % 2, pix // 2
    edge = REACH * block

    def shifted(axis, size, up, value):
        steps = [(i, i + 1) if up else (i + 1, i) for i in range(size - 1)]
        return lax.ppermute(value, axis, steps)

    vmem = pl.BlockSpec(memory_space=pltpu.VMEM)
    smem = pl.BlockSpec(memory_space=pltpu.SMEM)
    hbm = pl.BlockSpec(memory_space=pl.ANY)
    fixed = pl.BlockSpec(memory_space=pltpu.HBM)

    part = rules_here * block // n_pix
    mine = lax.dynamic_slice_in_dim(adduct.reshape(rules_here * block, block), pix * part, part, 0)

    def turned(value, distance):
        other = lax.ppermute(value, "ion", [(i, i ^ distance) for i in range(n_ion)])
        return jnp.concatenate([value, other], axis=0)

    mine = turned(mine, 1)

    edge_columns = jax.ShapeDtypeStruct((2, rows), images.dtype)
    head, tail, weights = pl.pallas_call(
        columns_kernel,
        in_specs=[hbm, vmem],
        out_specs=[vmem, vmem, vmem],
        out_shape=[
            edge_columns,
            edge_columns,
            jax.ShapeDtypeStruct((width // TILE, DEPTH, TILE), jnp.bfloat16),
        ],
        scratch_shapes=[pltpu.VMEM((2, rows, LANES), images.dtype), pltpu.SemaphoreType.DMA((2,))],
        compiler_params=params(),
        cost_estimate=cost(0, 4 * rows * LANES),
        name="columns",
    )(images, stencil)
    head, tail, mine = lax.optimization_barrier((head, tail, mine))
    before = shifted("pix", n_pix, True, tail)
    after = shifted("pix", n_pix, False, head)
    for k in range(1, n_ion.bit_length() - 1):
        mine = turned(mine, 2**k)
    columns = jnp.concatenate([after, jnp.zeros((4, rows), images.dtype), before], axis=0)

    message = jax.ShapeDtypeStruct((edge + EXTRA, width), images.dtype)
    top, bottom = pl.pallas_call(
        message_kernel,
        in_specs=[hbm, vmem],
        out_specs=[hbm, hbm],
        out_shape=[message, message],
        scratch_shapes=[pltpu.VMEM((2, edge + EXTRA, width), images.dtype), pltpu.SemaphoreType.DMA((4,))],
        compiler_params=params(),
        cost_estimate=cost(0, 8 * edge * width),
        name="edge_messages",
    )(images, columns)
    top, bottom, mine = lax.optimization_barrier((top, bottom, mine))
    down = shifted("ion", n_ion, True, bottom)
    up = shifted("ion", n_ion, False, top)

    distances = [n_pix >> k for k in range(1, n_pix.bit_length())]
    for distance in distances:
        other = lax.ppermute(mine, "pix", [(i, i ^ distance) for i in range(n_pix)])
        if distance > 1:
            mine = jnp.concatenate([mine, other], axis=0)

    def place_of(rule):
        row = (rule & (rules_here - 1)) * block
        turn = (rule >> (rules_here.bit_length() - 1)) ^ lax.axis_index("ion")
        pieces = []
        for offset in range(0, block, min(part, block)):
            share_of = ((row + offset) >> (part.bit_length() - 1)) ^ lax.axis_index("pix")
            at = turn * part + ((row + offset) & (part - 1))
            for k, distance in enumerate(distances):
                at = at + jnp.where((share_of & distance) != 0, n_ion * part << k, 0)
            pieces.append(at)
        return pieces

    table_pairs = pairs.T
    group = next(g for g in (8, 5, 4, 2, 1) if blocks % g == 0)
    steps = blocks // group
    units = -(-2 * (blocks + 2 * REACH) // block)
    half = (chips, share, LANES)
    half_shape = (slots + 2 * units, *half)
    both_halves = [jax.ShapeDtypeStruct(half_shape, jnp.bfloat16)] * 2

    def rows_at(columns):
        return pl.BlockSpec((group * block, columns), lambda i, *_: (jnp.minimum(i, steps - 1), 0))

    smoothed, energy, keep, give = pl.pallas_call(
        functools.partial(main_kernel, steps, group, block),
        grid_spec=pltpu.PrefetchScalarGridSpec(
            num_scalar_prefetch=1,
            grid=(steps + 1,),
            in_specs=[
                rows_at(width),
                pl.BlockSpec((8, group * block), lambda i, *_: (0, jnp.minimum(i, steps - 1))),
                whole(weights.shape),
            ],
            out_specs=[hbm, whole((blocks, LANES)), whole(half_shape), whole(half_shape)],
            scratch_shapes=[pltpu.VMEM((blocks, block, width), jnp.bfloat16), pltpu.SemaphoreType.DMA((steps,))],
        ),
        out_shape=[
            jax.ShapeDtypeStruct((blocks, block, width), jnp.bfloat16),
            jax.ShapeDtypeStruct((blocks, LANES), jnp.float32),
            *both_halves,
        ],
        compiler_params=params(),
        cost_estimate=cost(2 * rows * width * DEPTH + 2 * slots * block * block * width, 4 * rows * width),
        name="smooth_and_gram",
    )(table_pairs, images, columns, weights)
    smoothed = smoothed.reshape(rows, width)

    keep, give = pl.pallas_call(
        functools.partial(cross_kernel, blocks, block),
        in_specs=[smem] + [hbm] * 2 + [fixed] * 5,
        out_specs=[vmem, vmem],
        out_shape=both_halves,
        scratch_shapes=[
            pltpu.VMEM((2 * edge, width), jnp.bfloat16),
            pltpu.VMEM((EXTRA, 2 * edge), jnp.bfloat16),
            pltpu.VMEM(weights.shape, jnp.bfloat16),
            pltpu.VMEM((blocks, LANES), jnp.float32),
            pltpu.VMEM((2 * edge, width), jnp.bfloat16),
            pltpu.VMEM((2 * edge, width), jnp.bfloat16),
            pltpu.VMEM((units * block // 2, LANES), jnp.float32),
            pltpu.SemaphoreType.DMA((10,)),
        ],
        compiler_params=params(),
        cost_estimate=cost(4 * edge * width * DEPTH, 8 * edge * width),
        name="cross_grams",
    )(table_pairs, down, up, weights, energy, smoothed, keep, give)

    got = lax.ppermute(give, "pix", [(i, i ^ 1) for i in range(n_pix)])
    message = jax.ShapeDtypeStruct((slots + 2 * units * chips, share, LANES), jnp.bfloat16)
    own_rows = jax.ShapeDtypeStruct((slots + units * chips, share, LANES), jnp.float32)
    small = pltpu.CompilerParams(vmem_limit_bytes=16 * 1024 * 1024)
    own, *messages = pl.pallas_call(
        functools.partial(chip_kernel, slots, units),
        in_specs=[fixed, hbm],
        out_specs=[vmem] * chips,
        out_shape=[own_rows] + [message] * (chips - 1),
        scratch_shapes=[
            pltpu.VMEM(half_shape, jnp.bfloat16),
            pltpu.VMEM(half_shape, jnp.bfloat16),
            pltpu.SemaphoreType.DMA((2,)),
        ],
        compiler_params=small,
        name="chip_sums",
    )(keep, got)
    received = [
        lax.ppermute(m, "pix", [(i, i ^ (2 * (d + 1))) for i in range(n_pix)]) for d, m in enumerate(messages)
    ]

    scores = pl.pallas_call(
        functools.partial(score_kernel, blocks, place_of, pixel_count),
        in_specs=[smem] * 3 + [hbm] * (chips + 2),
        out_specs=vmem,
        out_shape=jax.ShapeDtypeStruct((slots, share, block), jnp.bfloat16),
        scratch_shapes=[
            pltpu.VMEM(own_rows.shape, jnp.float32),
            *[pltpu.VMEM(message.shape, jnp.bfloat16)] * (chips - 1),
            pltpu.VMEM((2 * mine.shape[0], block), jnp.bfloat16),
            pltpu.VMEM((units * block // 2, LANES), jnp.float32),
            pltpu.VMEM((slots, LANES), jnp.float32),
            pltpu.VMEM((slots, LANES), jnp.float32),
            pltpu.VMEM((slots, share, LANES), jnp.bfloat16),
            pltpu.SMEM((-(-block // part), slots), jnp.int32),
            pltpu.SemaphoreType.DMA((chips + 2,)),
        ],
        compiler_params=small,
        name="scores",
    )(table_pairs, live, rule_of_block, own, *received, mine, other)
    return (smoothed, scores)


def solution(mesh):
    return jax.shard_map(
        on_device,
        mesh=mesh,
        in_specs=(
            P("ion", "pix"),
            P(None, "pix"),
            P("ion", None),
            P("ion"),
            P(),
            P("ion", None, None),
        ),
        out_specs=(P("ion", "pix"), P("ion", "pix", None)),
        check_vma=False,
    )
```

```python
import functools

import jax
import jax.numpy as jnp
from jax import lax
from jax.experimental import pallas as pl
from jax.experimental.pallas import tpu as pltpu
from jax.sharding import PartitionSpec as P

REACH = 3
TAPS = 5
LANES = 128
HALF = LANES // 2
TILE = 2 * LANES
DEPTH = 3 * LANES
VMEM_BYTES = 58 * 1024 * 1024


def params():
    return pltpu.CompilerParams(vmem_limit_bytes=VMEM_BYTES)


def cost(flops, moved):
    return pl.CostEstimate(flops=flops, bytes_accessed=moved, transcendentals=0)


def whole(shape):
    return pl.BlockSpec(shape, lambda *_: (0,) * len(shape))


def fetch(sources, targets, sems):
    copies = [pltpu.make_async_copy(x, y, sems.at[k]) for k, (x, y) in enumerate(zip(sources, targets))]
    for copy in copies:
        copy.start()
    return copies


def split(values):
    high = values.astype(jnp.bfloat16)
    return high, (values - high.astype(jnp.float32)).astype(jnp.bfloat16)


def smooth_rows(x_ref, halo, w_ref, store):
    rows, width = x_ref.shape
    tiles = width // TILE
    first = lax.broadcasted_iota(jnp.int32, (rows, LANES), 1) < HALF
    last = None
    for j in range(tiles):
        own = x_ref[:, j * TILE : (j + 1) * TILE]
        before = halo if j == 0 else x_ref[:, j * TILE - LANES : j * TILE]
        after = halo if j == tiles - 1 else x_ref[:, (j + 1) * TILE : (j + 1) * TILE + LANES]
        window = jnp.concatenate([own, jnp.where(first, after, before)], axis=1)
        values = jnp.dot(window, w_ref[j], preferred_element_type=jnp.float32)
        if j > 0:
            store(j - 1, last)
        last = values
    store(tiles - 1, last)


def lane_pairs(values):
    squares = values * values
    return squares[:, :LANES] + squares[:, LANES:]


def row_sums(part):
    return jnp.sum(part.T, axis=0, keepdims=True)


def gram_of(left, right):
    return lax.dot_general(
        left, right, (((1,), (1,)), ((), ())), preferred_element_type=jnp.float32
    )


def by_core(gram, chips, core):
    parts = gram.reshape(chips, 2, gram.shape[0] // (2 * chips), gram.shape[1])
    even, odd = parts[:, 0].astype(jnp.bfloat16), parts[:, 1].astype(jnp.bfloat16)
    return jnp.where(core == 0, even, odd), jnp.where(core == 0, odd, even)


def write_weights(stencil_ref, out_ref):
    out_ref[...] = jnp.zeros_like(out_ref)
    strip = 16
    places = [(0, LANES, 0, 2), (LANES, LANES, LANES, 2)]
    places += [(LANES - strip, strip, LANES, 2), (LANES, strip, 0, 2)]
    places += [(TILE + LANES - strip, strip, 0, 2 - LANES - TILE), (TILE, strip, LANES, 2)]
    for k0, rows, n0, shift in places:
        k = lax.broadcasted_iota(jnp.int32, (rows, LANES), 0) + k0
        tap = k - lax.broadcasted_iota(jnp.int32, (rows, LANES), 1) - n0 + shift
        for j in range(out_ref.shape[0]):
            taps = stencil_ref[:, j * TILE + n0 : j * TILE + n0 + LANES]
            w = jnp.zeros((rows, LANES), jnp.float32)
            for t in range(TAPS):
                w = jnp.where(tap == t, taps[t : t + 1, :], w)
            out_ref[j, k0 : k0 + rows, n0 : n0 + LANES] = w.astype(jnp.bfloat16)


def columns_kernel(images_ref, stencil_ref, near_ref, far_ref, w_ref, strips, sems):
    width = images_ref.shape[1]
    copies = fetch((images_ref.at[:, pl.ds(0, LANES)], images_ref.at[:, pl.ds(width - LANES, LANES)]),
                   (strips.at[0], strips.at[1]), sems)
    write_weights(stencil_ref, w_ref)
    row = lax.broadcasted_iota(jnp.int32, (8, LANES), 0)
    lane = lax.broadcasted_iota(jnp.int32, (8, LANES), 1)
    sides = []
    for k, shift in enumerate((0, LANES - 2)):
        copies[k].wait()
        pick = (lane == row + shift).astype(jnp.bfloat16)
        sides.append(gram_of(pick, strips[k])[:2])
    head, tail = sides
    odd = lax.axis_index("pix") % 2 == 1
    near_ref[...] = jnp.where(odd, head, tail).astype(jnp.bfloat16)
    far_ref[...] = jnp.where(odd, tail, head).astype(jnp.bfloat16)


def rows_kernel(images_ref, near_ref, far_ref, bands, sems):
    rows, edge = images_ref.shape[0], near_ref.shape[0]
    odd = lax.axis_index("ion") % 2
    reads = fetch(
        [images_ref.at[pl.ds(pl.multiple_of(k * (rows - edge), edge // REACH), edge)] for k in (1 - odd, odd)],
        [bands.at[0], bands.at[1]],
        sems,
    )
    writes = [
        pltpu.make_async_copy(bands.at[k], out, sems.at[2 + k]) for k, out in enumerate((near_ref, far_ref))
    ]
    for read, write in zip(reads, writes):
        read.wait()
        write.start()
    for write in writes:
        write.wait()


def halo_tile(columns_ref):
    columns = columns_ref[...].astype(jnp.float32).T.astype(jnp.bfloat16)
    row = lax.broadcasted_iota(jnp.int32, (8, LANES), 0)
    lane = lax.broadcasted_iota(jnp.int32, (8, LANES), 1)
    place = (lane == row + jnp.where(row < 4, 0, LANES - 8)).astype(jnp.bfloat16)
    return jnp.dot(columns, place, preferred_element_type=jnp.float32).astype(jnp.bfloat16)


def main_kernel(steps, group, block, pairs_ref, x_ref, columns_ref, w_ref,
                out_hbm, energy_ref, keep_ref, give_ref, held, sems):
    step = pl.program_id(0)
    blocks = steps * group
    chips = keep_ref.shape[1]
    slots = pairs_ref.shape[1]

    def copy_out(k):
        here = pl.ds(k * group, group)
        return pltpu.make_async_copy(held.at[here], out_hbm.at[here], sems.at[k])

    @pl.when(step < steps)
    def smooth():
        total = [None]

        def store(j, values):
            columns = slice(j * TILE, (j + 1) * TILE)
            rounded = values.astype(jnp.bfloat16).reshape(group, block, TILE)
            held[pl.ds(step * group, group), :, columns] = rounded
            squares = lane_pairs(values)
            total[0] = squares if j == 0 else total[0] + squares

        smooth_rows(x_ref, halo_tile(columns_ref), w_ref, store)
        copy_out(step).start()
        for g in range(group):
            energy_ref[pl.ds(step * group + g, 1), :] = row_sums(total[0][g * block : (g + 1) * block, :])

    @pl.when(step == steps)
    def grams():
        core = lax.axis_index("pix") % 2
        first = lax.axis_index("ion") * blocks

        def one(s, carry):
            a = pairs_ref[0, s] - first
            b = jnp.clip(pairs_ref[1, s] - first, 0, blocks - 1)
            keep_ref[s], give_ref[s] = by_core(gram_of(held[a], held[b]), chips, core)
            return carry

        lax.fori_loop(0, slots, one, 0, unroll=4)
        for k in range(steps):
            copy_out(k).wait()


def cross_kernel(blocks, block, pairs_ref, near_hbm, far_hbm, near_columns_hbm, far_columns_hbm, w_hbm, energy_hbm, smoothed_hbm, keep_hbm,
                 give_hbm, keep_ref, give_ref, x_ref, columns_ref, w_ref, energy_ref, own, other, table, sems):
    core = lax.axis_index("pix") % 2
    first_block = lax.axis_index("ion") * blocks
    slots = pairs_ref.shape[1]
    chips, share = keep_ref.shape[1:3]
    units = (keep_ref.shape[0] - slots) // 2
    edge = REACH * block
    rows = blocks * block
    low, high = pl.ds(0, edge), pl.ds(edge, edge)
    odd = lax.axis_index("ion") % 2
    near, far = (pl.ds(pl.multiple_of(k * edge, edge), edge) for k in (1 - odd, odd))
    copies = fetch(
        (near_hbm, far_hbm, near_columns_hbm, far_columns_hbm, w_hbm, energy_hbm, smoothed_hbm.at[low],
         smoothed_hbm.at[pl.ds(rows - edge, edge)], keep_hbm, give_hbm),
        (x_ref.at[near], x_ref.at[far], columns_ref.at[:, near], columns_ref.at[:, far], w_ref, energy_ref, own.at[low],
         own.at[high], keep_ref, give_ref),
        sems,
    )
    for copy in copies[:6]:
        copy.wait()
    table[...] = jnp.zeros_like(table)
    table[REACH : REACH + blocks, :] = energy_ref[...]
    total = [None]

    def store(j, values):
        other[:, j * TILE : (j + 1) * TILE] = values.astype(jnp.bfloat16)
        squares = lane_pairs(values)
        total[0] = squares if j == 0 else total[0] + squares

    smooth_rows(x_ref, halo_tile(columns_ref), w_ref, store)
    for k in range(2 * REACH):
        row = k if k < REACH else k + blocks
        table[row : row + 1, :] = row_sums(total[0][k * block : (k + 1) * block, :])
    for copy in copies[6:]:
        copy.wait()

    shape = (units, chips, share, LANES)
    upper, lower = split(table[...].reshape(shape))
    for ref in (keep_ref, give_ref):
        ref[slots : slots + units] = upper
        ref[slots + units :] = lower

    def one(s, carry):
        a, b = pairs_ref[0, s] - first_block, pairs_ref[1, s] - first_block

        @pl.when((b < 0) | (b >= blocks))
        def crossing():
            side = (b >= 0).astype(jnp.int32)
            a_row = pl.multiple_of((a - side * (blocks - 2 * REACH)) * block, block)
            b_row = pl.multiple_of((b + REACH - side * blocks) * block, block)
            gram = gram_of(own[pl.ds(a_row, block), :], other[pl.ds(b_row, block), :])
            keep_ref[s], give_ref[s] = by_core(gram, chips, core)

        return carry

    lax.fori_loop(0, slots, one, 0)


def chip_kernel(slots, units, keep_hbm, got_hbm, own_ref, *refs):
    out_refs, (keep_ref, got_ref, sems) = refs[:-3], refs[-3:]
    chip = lax.axis_index("pix") // 2
    chips, share = keep_ref.shape[1:3]
    shape = (units * chips, share, LANES)
    for copy in fetch((keep_hbm, got_hbm), (keep_ref, got_ref), sems):
        copy.wait()
    energies = 0.0
    for ref in (keep_ref, got_ref):
        energies = energies + (
            ref[slots : slots + units].astype(jnp.float32) + ref[slots + units :].astype(jnp.float32)
        )
    high, low = split(energies)
    for d in range(chips):
        total = keep_ref[:slots, chip ^ d].astype(jnp.float32) + got_ref[:slots, chip ^ d].astype(jnp.float32)
        if d == 0:
            own_ref[:slots] = total
            own_ref[slots:] = energies.reshape(shape)
        else:
            out = out_refs[d - 1]
            out[:slots] = total.astype(jnp.bfloat16)
            out[slots : slots + units * chips] = high.reshape(shape)
            out[slots + units * chips :] = low.reshape(shape)


def score_kernel(blocks, place_of, pixel_count, pairs_ref, live_ref, rules_ref, *refs):
    chips = (len(refs) - 9) // 2
    sources, out_ref, own_ref = refs[: chips + 2], refs[chips + 2], refs[chips + 3]
    got_refs, (table_ref, inverse, left, right, coloc, place, sems) = refs[chips + 4 : -7], refs[-7:]
    slots, share, block = out_ref.shape
    e_units = inverse.shape[0] // share
    half = table_ref.shape[0] // 2
    targets = (own_ref, *got_refs, table_ref.at[pl.ds(0, half)], table_ref.at[pl.ds(half, half)])
    copies = fetch(sources, targets, sems)
    pix, first = lax.axis_index("pix"), lax.axis_index("ion") * blocks
    pieces = place.shape[0]
    depth = block // pieces

    def find(s, carry):
        for k, at in enumerate(place_of(rules_ref[pairs_ref[1, s]])):
            place[k, s] = at
        return carry

    lax.fori_loop(0, slots, find, 0)
    for copy in copies[:-2]:
        copy.wait()
    gram = own_ref[:slots]
    energies = own_ref[slots:]
    for got in got_refs:
        gram = gram + got[:slots].astype(jnp.float32)
        energies = energies + (
            got[slots : slots + e_units].astype(jnp.float32) + got[slots + e_units :].astype(jnp.float32)
        )
    inverse[...] = (1.0 / jnp.sqrt(energies / pixel_count + 1e-06)).reshape(inverse.shape)

    def pick(s, carry):
        left[pl.ds(s, 1), :] = inverse[pl.ds(pairs_ref[0, s] - first + REACH, 1), :]
        right[pl.ds(s, 1), :] = inverse[pl.ds(pairs_ref[1, s] - first + REACH, 1), :]
        return carry

    lax.fori_loop(0, slots, pick, 0, unroll=8)
    lane = lax.broadcasted_iota(jnp.int32, (1, share, LANES), 2)
    mine = lane == lax.broadcasted_iota(jnp.int32, (1, share, LANES), 1) + pix * share
    inv_a = jnp.sum(jnp.where(mine, left[...][:, None, :], 0.0), axis=2, keepdims=True)
    coloc[...] = (gram * inv_a * right[...][:, None, :] / pixel_count).astype(jnp.bfloat16)
    for copy in copies[-2:]:
        copy.wait()

    def one(s, carry):
        scores = jnp.zeros((share, block), jnp.float32)
        for k in range(pieces):
            matrix = table_ref[pl.ds(pl.multiple_of(place[k, s], depth), depth), :]
            part = coloc[s, :, k * depth : (k + 1) * depth]
            scores = scores + jnp.dot(part, matrix, preferred_element_type=jnp.float32)
        out_ref[s] = jnp.where(s < live_ref[0], scores, 0.0).astype(jnp.bfloat16)
        return carry

    lax.fori_loop(0, slots, one, 0, unroll=slots)


def on_device(images, stencil, pairs, live, rule_of_block, adduct):
    rows, width = images.shape
    rules_here, block, _ = adduct.shape
    blocks = rows // block
    slots = pairs.shape[0]
    n_pix, n_ion = lax.axis_size("pix"), lax.axis_size("ion")
    pix, ion = lax.axis_index("pix"), lax.axis_index("ion")
    pixel_count = width * n_pix
    chips, share = n_pix // 2, block // n_pix
    core, chip = pix % 2, pix // 2
    edge = REACH * block

    def swapped(axis, size, near, far):
        pairs_of = [[(i, i + 1) for i in range(first, size - 1, 2)] for first in (0, 1)]
        return [
            lax.ppermute(value, axis, both + [(j, i) for i, j in both]) for value, both in zip((near, far), pairs_of)
        ]

    vmem = pl.BlockSpec(memory_space=pltpu.VMEM)
    smem = pl.BlockSpec(memory_space=pltpu.SMEM)
    hbm = pl.BlockSpec(memory_space=pl.ANY)
    fixed = pl.BlockSpec(memory_space=pltpu.HBM)

    part = rules_here * block // n_pix
    mine = lax.dynamic_slice_in_dim(adduct.reshape(rules_here * block, block), pix * part, part, 0)
    turns = [lax.ppermute(mine, "ion", [(i, i ^ d) for i in range(n_ion)]) for d in range(1, n_ion)]

    edge_rows = jax.ShapeDtypeStruct((edge, width), images.dtype)
    near, far = pl.pallas_call(
        rows_kernel,
        in_specs=[hbm],
        out_specs=[hbm, hbm],
        out_shape=[edge_rows, edge_rows],
        scratch_shapes=[pltpu.VMEM((2, edge, width), images.dtype), pltpu.SemaphoreType.DMA((4,))],
        compiler_params=params(),
        cost_estimate=cost(0, 8 * edge * width),
        name="edge_rows",
    )(images)
    near, far, *turns = lax.optimization_barrier((near, far, *turns))
    near_rows, far_rows = swapped("ion", n_ion, near, far)
    mine = jnp.concatenate([mine, *turns], axis=0)

    edge_columns = jax.ShapeDtypeStruct((2, rows), images.dtype)
    images_later, near, far = lax.optimization_barrier((images, near, far))
    near, far, weights = pl.pallas_call(
        columns_kernel,
        in_specs=[hbm, vmem],
        out_specs=[vmem, vmem, vmem],
        out_shape=[
            edge_columns,
            edge_columns,
            jax.ShapeDtypeStruct((width // TILE, DEPTH, TILE), jnp.bfloat16),
        ],
        scratch_shapes=[pltpu.VMEM((2, rows, LANES), images.dtype), pltpu.SemaphoreType.DMA((2,))],
        compiler_params=params(),
        cost_estimate=cost(0, 4 * rows * LANES),
        name="columns",
    )(images_later, stencil)
    near, far = swapped("pix", n_pix, near, far)
    odd = pix % 2 == 1
    after, before = jnp.where(odd, far, near), jnp.where(odd, near, far)
    columns = jnp.concatenate([after, jnp.zeros((4, rows), images.dtype), before], axis=0)
    first, last = columns[:, :edge], columns[:, rows - edge :]
    odd = ion % 2 == 1
    near_columns, far_columns = swapped("ion", n_ion, jnp.where(odd, first, last), jnp.where(odd, last, first))

    distances = [n_pix >> k for k in range(1, n_pix.bit_length())]
    for distance in distances:
        other = lax.ppermute(mine, "pix", [(i, i ^ distance) for i in range(n_pix)])
        if distance > 1:
            mine = jnp.concatenate([mine, other], axis=0)

    def place_of(rule):
        row = (rule & (rules_here - 1)) * block
        turn = (rule >> (rules_here.bit_length() - 1)) ^ lax.axis_index("ion")
        pieces = []
        for offset in range(0, block, min(part, block)):
            share_of = ((row + offset) >> (part.bit_length() - 1)) ^ lax.axis_index("pix")
            at = turn * part + ((row + offset) & (part - 1))
            for k, distance in enumerate(distances):
                at = at + jnp.where((share_of & distance) != 0, n_ion * part << k, 0)
            pieces.append(at)
        return pieces

    table_pairs = pairs.T
    group = next(g for g in (8, 5, 4, 2, 1) if blocks % g == 0)
    steps = blocks // group
    units = -(-2 * (blocks + 2 * REACH) // block)
    half = (chips, share, LANES)
    half_shape = (slots + 2 * units, *half)
    both_halves = [jax.ShapeDtypeStruct(half_shape, jnp.bfloat16)] * 2

    def rows_at(columns):
        return pl.BlockSpec((group * block, columns), lambda i, *_: (jnp.minimum(i, steps - 1), 0))

    smoothed, energy, keep, give = pl.pallas_call(
        functools.partial(main_kernel, steps, group, block),
        grid_spec=pltpu.PrefetchScalarGridSpec(
            num_scalar_prefetch=1,
            grid=(steps + 1,),
            in_specs=[
                rows_at(width),
                pl.BlockSpec((8, group * block), lambda i, *_: (0, jnp.minimum(i, steps - 1))),
                whole(weights.shape),
            ],
            out_specs=[hbm, whole((blocks, LANES)), whole(half_shape), whole(half_shape)],
            scratch_shapes=[pltpu.VMEM((blocks, block, width), jnp.bfloat16), pltpu.SemaphoreType.DMA((steps,))],
        ),
        out_shape=[
            jax.ShapeDtypeStruct((blocks, block, width), jnp.bfloat16),
            jax.ShapeDtypeStruct((blocks, LANES), jnp.float32),
            *both_halves,
        ],
        compiler_params=params(),
        cost_estimate=cost(2 * rows * width * DEPTH + 2 * slots * block * block * width, 4 * rows * width),
        name="smooth_and_gram",
    )(table_pairs, images, columns, weights)
    smoothed = smoothed.reshape(rows, width)

    keep, give = pl.pallas_call(
        functools.partial(cross_kernel, blocks, block),
        in_specs=[smem] + [hbm] * 4 + [fixed] * 5,
        out_specs=[vmem, vmem],
        out_shape=both_halves,
        scratch_shapes=[
            pltpu.VMEM((2 * edge, width), jnp.bfloat16),
            pltpu.VMEM((8, 2 * edge), jnp.bfloat16),
            pltpu.VMEM(weights.shape, jnp.bfloat16),
            pltpu.VMEM((blocks, LANES), jnp.float32),
            pltpu.VMEM((2 * edge, width), jnp.bfloat16),
            pltpu.VMEM((2 * edge, width), jnp.bfloat16),
            pltpu.VMEM((units * block // 2, LANES), jnp.float32),
            pltpu.SemaphoreType.DMA((10,)),
        ],
        compiler_params=params(),
        cost_estimate=cost(4 * edge * width * DEPTH, 8 * edge * width),
        name="cross_grams",
    )(table_pairs, near_rows, far_rows, near_columns, far_columns, weights, energy, smoothed, keep, give)

    got = lax.ppermute(give, "pix", [(i, i ^ 1) for i in range(n_pix)])
    message = jax.ShapeDtypeStruct((slots + 2 * units * chips, share, LANES), jnp.bfloat16)
    own_rows = jax.ShapeDtypeStruct((slots + units * chips, share, LANES), jnp.float32)
    small = pltpu.CompilerParams(vmem_limit_bytes=16 * 1024 * 1024)
    own, *messages = pl.pallas_call(
        functools.partial(chip_kernel, slots, units),
        in_specs=[fixed, hbm],
        out_specs=[vmem] * chips,
        out_shape=[own_rows] + [message] * (chips - 1),
        scratch_shapes=[
            pltpu.VMEM(half_shape, jnp.bfloat16),
            pltpu.VMEM(half_shape, jnp.bfloat16),
            pltpu.SemaphoreType.DMA((2,)),
        ],
        compiler_params=small,
        name="chip_sums",
    )(keep, got)
    received = [
        lax.ppermute(m, "pix", [(i, i ^ (2 * (d + 1))) for i in range(n_pix)]) for d, m in enumerate(messages)
    ]

    scores = pl.pallas_call(
        functools.partial(score_kernel, blocks, place_of, pixel_count),
        in_specs=[smem] * 3 + [hbm] * (chips + 2),
        out_specs=vmem,
        out_shape=jax.ShapeDtypeStruct((slots, share, block), jnp.bfloat16),
        scratch_shapes=[
            pltpu.VMEM(own_rows.shape, jnp.float32),
            *[pltpu.VMEM(message.shape, jnp.bfloat16)] * (chips - 1),
            pltpu.VMEM((2 * mine.shape[0], block), jnp.bfloat16),
            pltpu.VMEM((units * block // 2, LANES), jnp.float32),
            pltpu.VMEM((slots, LANES), jnp.float32),
            pltpu.VMEM((slots, LANES), jnp.float32),
            pltpu.VMEM((slots, share, LANES), jnp.bfloat16),
            pltpu.SMEM((-(-block // part), slots), jnp.int32),
            pltpu.SemaphoreType.DMA((chips + 2,)),
        ],
        compiler_params=small,
        name="scores",
    )(table_pairs, live, rule_of_block, own, *received, mine, other)
    return (smoothed, scores)


def solution(mesh):
    return jax.shard_map(
        on_device,
        mesh=mesh,
        in_specs=(
            P("ion", "pix"),
            P(None, "pix"),
            P("ion", None),
            P("ion"),
            P(),
            P("ion", None, None),
        ),
        out_specs=(P("ion", "pix"), P("ion", "pix", None)),
        check_vma=False,
    )
```

```python
import functools

import jax
import jax.numpy as jnp
from jax import lax
from jax.experimental import pallas as pl
from jax.experimental.pallas import tpu as pltpu
from jax.sharding import PartitionSpec as P

REACH = 3
TAPS = 5
LANES = 128
HALF = LANES // 2
TILE = 2 * LANES
DEPTH = 3 * LANES
VMEM_BYTES = 58 * 1024 * 1024


def params():
    return pltpu.CompilerParams(vmem_limit_bytes=VMEM_BYTES)


def cost(flops, moved):
    return pl.CostEstimate(flops=flops, bytes_accessed=moved, transcendentals=0)


def whole(shape):
    return pl.BlockSpec(shape, lambda *_: (0,) * len(shape))


def fetch(sources, targets, sems):
    copies = [pltpu.make_async_copy(x, y, sems.at[k]) for k, (x, y) in enumerate(zip(sources, targets))]
    for copy in copies:
        copy.start()
    return copies


def smooth_rows(x_ref, halo, w_ref, store):
    rows, width = x_ref.shape
    tiles = width // TILE
    first = lax.broadcasted_iota(jnp.int32, (rows, LANES), 1) < HALF

    def tile(j):
        own = x_ref[:, j * TILE : (j + 1) * TILE]
        before = halo if j == 0 else x_ref[:, j * TILE - LANES : j * TILE]
        after = halo if j == tiles - 1 else x_ref[:, (j + 1) * TILE : (j + 1) * TILE + LANES]
        window = jnp.concatenate([own, jnp.where(first, after, before)], axis=1)
        return jnp.dot(window, w_ref[j], preferred_element_type=jnp.float32)

    total = None
    for j in range(0, tiles, 2):
        squares = None
        for k, values in enumerate([tile(j), tile(j + 1)]):
            store(j + k, values.astype(jnp.bfloat16))
            values = values * values
            values = values[:, :LANES] + values[:, LANES:]
            squares = values if k == 0 else squares + values
        total = squares if j == 0 else total + squares
    return total


def row_sums(part):
    return jnp.sum(part.T, axis=0, keepdims=True)


def gram_of(left, right):
    return lax.dot_general(
        left, right, (((1,), (1,)), ((), ())), preferred_element_type=jnp.float32
    )


def by_core(gram, chips, core):
    parts = gram.reshape(chips, 2, gram.shape[0] // (2 * chips), gram.shape[1])
    even, odd = parts[:, 0].astype(jnp.bfloat16), parts[:, 1].astype(jnp.bfloat16)
    return jnp.where(core == 0, even, odd), jnp.where(core == 0, odd, even)


def write_weights(stencil_ref, out_ref):
    out_ref[...] = jnp.zeros_like(out_ref)
    strip = 16
    places = [(0, LANES, 0, 2), (LANES, LANES, LANES, 2)]
    places += [(LANES - strip, strip, LANES, 2), (LANES, strip, 0, 2)]
    places += [(TILE + LANES - strip, strip, 0, 2 - LANES - TILE), (TILE, strip, LANES, 2)]
    for k0, rows, n0, shift in places:
        k = lax.broadcasted_iota(jnp.int32, (rows, LANES), 0) + k0
        tap = k - lax.broadcasted_iota(jnp.int32, (rows, LANES), 1) - n0 + shift
        for j in range(out_ref.shape[0]):
            taps = stencil_ref[:, j * TILE + n0 : j * TILE + n0 + LANES]
            w = jnp.zeros((rows, LANES), jnp.float32)
            for t in range(TAPS):
                w = jnp.where(tap == t, taps[t : t + 1, :], w)
            out_ref[j, k0 : k0 + rows, n0 : n0 + LANES] = w.astype(jnp.bfloat16)


def cut_kernel(images_ref, stencil_ref, near_rows, far_rows, near_columns, far_columns, w_ref, bands, strips, sems):
    rows, width = images_ref.shape
    edge = near_rows.shape[0]
    odd = lax.axis_index("ion") % 2
    starts = [pl.multiple_of(k * (rows - edge), edge // REACH) for k in (1 - odd, odd)]
    reads = fetch(
        [images_ref.at[pl.ds(start, edge)] for start in starts]
        + [images_ref.at[:, pl.ds(start, LANES)] for start in (0, width - LANES)],
        [bands.at[0], bands.at[1], strips.at[0], strips.at[1]],
        sems,
    )
    writes = [
        pltpu.make_async_copy(bands.at[k], out, sems.at[4 + k]) for k, out in enumerate((near_rows, far_rows))
    ]
    write_weights(stencil_ref, w_ref)
    for read, write in zip(reads, writes):
        read.wait()
        write.start()
    row = lax.broadcasted_iota(jnp.int32, (8, LANES), 0)
    lane = lax.broadcasted_iota(jnp.int32, (8, LANES), 1)
    sides = []
    for k, shift in enumerate((0, LANES - 2)):
        reads[2 + k].wait()
        pick = (lane == row + shift).astype(jnp.bfloat16)
        sides.append(gram_of(pick, strips[k])[:2])
    head, tail = sides
    odd = lax.axis_index("pix") % 2 == 1
    near_columns[...] = jnp.where(odd, head, tail).astype(jnp.bfloat16)
    far_columns[...] = jnp.where(odd, tail, head).astype(jnp.bfloat16)
    for write in writes:
        write.wait()


def halo_tile(columns_ref):
    columns = columns_ref[...].astype(jnp.float32).T.astype(jnp.bfloat16)
    row = lax.broadcasted_iota(jnp.int32, (8, LANES), 0)
    lane = lax.broadcasted_iota(jnp.int32, (8, LANES), 1)
    place = (lane == row + jnp.where(row < 4, 0, LANES - 8)).astype(jnp.bfloat16)
    return jnp.dot(columns, place, preferred_element_type=jnp.float32).astype(jnp.bfloat16)


def main_kernel(steps, group, block, pairs_ref, x_ref, columns_ref, w_ref,
                out_hbm, energy_ref, keep_ref, give_ref, held, sems):
    step = pl.program_id(0)
    blocks = steps * group
    chips = keep_ref.shape[1]
    slots = pairs_ref.shape[1]

    def copy_out(k):
        here = pl.ds(k * group, group)
        return pltpu.make_async_copy(held.at[here], out_hbm.at[here], sems.at[k])

    @pl.when(step < steps)
    def smooth():
        def store(j, values):
            held[pl.ds(step * group, group), :, j * TILE : (j + 1) * TILE] = values.reshape(group, block, TILE)

        total = smooth_rows(x_ref, halo_tile(columns_ref), w_ref, store)
        copy_out(step).start()
        for g in range(group):
            energy_ref[pl.ds(step * group + g, 1), :] = row_sums(total[g * block : (g + 1) * block, :])

    @pl.when(step == steps)
    def grams():
        core = lax.axis_index("pix") % 2
        first = lax.axis_index("ion") * blocks

        def one(s, carry):
            a = pairs_ref[0, s] - first
            b = jnp.clip(pairs_ref[1, s] - first, 0, blocks - 1)
            keep_ref[s], give_ref[s] = by_core(gram_of(held[a], held[b]), chips, core)
            return carry

        lax.fori_loop(0, slots, one, 0, unroll=4)
        for k in range(steps):
            copy_out(k).wait()


def cross_kernel(blocks, block, pairs_ref, near_hbm, far_hbm, near_columns_hbm, far_columns_hbm, w_hbm, energy_hbm, smoothed_hbm, keep_hbm,
                 give_hbm, keep_ref, give_ref, x_ref, columns_ref, w_ref, energy_ref, own, other, table, sems):
    core = lax.axis_index("pix") % 2
    first_block = lax.axis_index("ion") * blocks
    slots = pairs_ref.shape[1]
    chips, share = keep_ref.shape[1:3]
    units = keep_ref.shape[0] - slots
    edge = REACH * block
    rows = blocks * block
    low, high = pl.ds(0, edge), pl.ds(edge, edge)
    odd = lax.axis_index("ion") % 2
    near, far = (pl.ds(pl.multiple_of(k * edge, edge), edge) for k in (1 - odd, odd))
    copies = fetch(
        (near_hbm, far_hbm, near_columns_hbm, far_columns_hbm, w_hbm, energy_hbm, smoothed_hbm.at[low],
         smoothed_hbm.at[pl.ds(rows - edge, edge)], keep_hbm, give_hbm),
        (x_ref.at[near], x_ref.at[far], columns_ref.at[:, near], columns_ref.at[:, far], w_ref, energy_ref, own.at[low],
         own.at[high], keep_ref, give_ref),
        sems,
    )
    for copy in copies[:6]:
        copy.wait()
    table[...] = jnp.zeros_like(table)
    table[REACH : REACH + blocks, :] = energy_ref[...]
    def store(j, values):
        other[:, j * TILE : (j + 1) * TILE] = values

    total = smooth_rows(x_ref, halo_tile(columns_ref), w_ref, store)
    for k in range(2 * REACH):
        row = k if k < REACH else k + blocks
        table[row : row + 1, :] = row_sums(total[k * block : (k + 1) * block, :])
    for copy in copies[6:]:
        copy.wait()

    shape = (units, chips, share, LANES)
    for ref in (keep_ref, give_ref):
        ref[slots:] = table[...].reshape(shape).astype(jnp.bfloat16)

    def one(s, carry):
        a, b = pairs_ref[0, s] - first_block, pairs_ref[1, s] - first_block

        @pl.when((b < 0) | (b >= blocks))
        def crossing():
            side = (b >= 0).astype(jnp.int32)
            a_row = pl.multiple_of((a - side * (blocks - 2 * REACH)) * block, block)
            b_row = pl.multiple_of((b + REACH - side * blocks) * block, block)
            gram = gram_of(own[pl.ds(a_row, block), :], other[pl.ds(b_row, block), :])
            keep_ref[s], give_ref[s] = by_core(gram, chips, core)

        return carry

    lax.fori_loop(0, slots, one, 0)


def chip_kernel(slots, units, keep_hbm, got_hbm, own_ref, *refs):
    out_refs, (keep_ref, got_ref, sems) = refs[:-3], refs[-3:]
    chip = lax.axis_index("pix") // 2
    chips, share = keep_ref.shape[1:3]
    shape = (units * chips, share, LANES)
    for copy in fetch((keep_hbm, got_hbm), (keep_ref, got_ref), sems):
        copy.wait()
    energies = (keep_ref[slots:].astype(jnp.float32) + got_ref[slots:].astype(jnp.float32)).reshape(shape)
    for d in range(chips):
        total = keep_ref[:slots, chip ^ d].astype(jnp.float32) + got_ref[:slots, chip ^ d].astype(jnp.float32)
        if d == 0:
            own_ref[:slots] = total
            own_ref[slots:] = energies
        else:
            out = out_refs[d - 1]
            out[:slots] = total.astype(jnp.bfloat16)
            out[slots:] = energies.astype(jnp.bfloat16)


def score_kernel(blocks, place_of, pixel_count, pairs_ref, live_ref, rules_ref, *refs):
    chips = (len(refs) - 9) // 2
    sources, out_ref, own_ref = refs[: chips + 2], refs[chips + 2], refs[chips + 3]
    got_refs, (table_ref, inverse, left, right, coloc, place, sems) = refs[chips + 4 : -7], refs[-7:]
    slots, share, block = out_ref.shape
    half = table_ref.shape[0] // 2
    targets = (own_ref, *got_refs, table_ref.at[pl.ds(0, half)], table_ref.at[pl.ds(half, half)])
    copies = fetch(sources, targets, sems)
    pix, first = lax.axis_index("pix"), lax.axis_index("ion") * blocks
    pieces = place.shape[0]
    depth = block // pieces

    def find(s, carry):
        for k, at in enumerate(place_of(rules_ref[pairs_ref[1, s]])):
            place[k, s] = at
        return carry

    lax.fori_loop(0, slots, find, 0)
    for copy in copies[:-2]:
        copy.wait()
    gram = own_ref[:slots]
    energies = own_ref[slots:]
    for got in got_refs:
        gram = gram + got[:slots].astype(jnp.float32)
        energies = energies + got[slots:].astype(jnp.float32)
    inverse[...] = (1.0 / jnp.sqrt(energies / pixel_count + 1e-06)).reshape(inverse.shape)

    def pick(s, carry):
        left[pl.ds(s, 1), :] = inverse[pl.ds(pairs_ref[0, s] - first + REACH, 1), :]
        right[pl.ds(s, 1), :] = inverse[pl.ds(pairs_ref[1, s] - first + REACH, 1), :]
        return carry

    lax.fori_loop(0, slots, pick, 0, unroll=8)
    lane = lax.broadcasted_iota(jnp.int32, (1, share, LANES), 2)
    mine = lane == lax.broadcasted_iota(jnp.int32, (1, share, LANES), 1) + pix * share
    inv_a = jnp.sum(jnp.where(mine, left[...][:, None, :], 0.0), axis=2, keepdims=True)
    coloc[...] = (gram * inv_a * right[...][:, None, :] / pixel_count).astype(jnp.bfloat16)
    for copy in copies[-2:]:
        copy.wait()

    def one(s, carry):
        scores = jnp.zeros((share, block), jnp.float32)
        for k in range(pieces):
            matrix = table_ref[pl.ds(pl.multiple_of(place[k, s], depth), depth), :]
            part = coloc[s, :, k * depth : (k + 1) * depth]
            scores = scores + jnp.dot(part, matrix, preferred_element_type=jnp.float32)
        out_ref[s] = jnp.where(s < live_ref[0], scores, 0.0).astype(jnp.bfloat16)
        return carry

    lax.fori_loop(0, slots, one, 0, unroll=slots)


def on_device(images, stencil, pairs, live, rule_of_block, adduct):
    rows, width = images.shape
    rules_here, block, _ = adduct.shape
    blocks = rows // block
    slots = pairs.shape[0]
    n_pix, n_ion = lax.axis_size("pix"), lax.axis_size("ion")
    pix, ion = lax.axis_index("pix"), lax.axis_index("ion")
    pixel_count = width * n_pix
    chips, share = n_pix // 2, block // n_pix
    core, chip = pix % 2, pix // 2
    edge = REACH * block

    def swapped(axis, size, near, far):
        pairs_of = [[(i, i + 1) for i in range(first, size - 1, 2)] for first in (0, 1)]
        return [
            lax.ppermute(value, axis, both + [(j, i) for i, j in both]) for value, both in zip((near, far), pairs_of)
        ]

    vmem = pl.BlockSpec(memory_space=pltpu.VMEM)
    smem = pl.BlockSpec(memory_space=pltpu.SMEM)
    hbm = pl.BlockSpec(memory_space=pl.ANY)
    fixed = pl.BlockSpec(memory_space=pltpu.HBM)

    part = rules_here * block // n_pix
    mine = lax.dynamic_slice_in_dim(adduct.reshape(rules_here * block, block), pix * part, part, 0)
    turns = [lax.ppermute(mine, "ion", [(i, i ^ d) for i in range(n_ion)]) for d in range(1, n_ion)]

    edge_rows = jax.ShapeDtypeStruct((edge, width), images.dtype)
    edge_columns = jax.ShapeDtypeStruct((2, rows), images.dtype)
    near_rows, far_rows, near, far, weights = pl.pallas_call(
        cut_kernel,
        in_specs=[hbm, vmem],
        out_specs=[hbm, hbm, vmem, vmem, vmem],
        out_shape=[
            edge_rows,
            edge_rows,
            edge_columns,
            edge_columns,
            jax.ShapeDtypeStruct((width // TILE, DEPTH, TILE), jnp.bfloat16),
        ],
        scratch_shapes=[
            pltpu.VMEM((2, edge, width), images.dtype),
            pltpu.VMEM((2, rows, LANES), images.dtype),
            pltpu.SemaphoreType.DMA((6,)),
        ],
        compiler_params=params(),
        cost_estimate=cost(0, 8 * edge * width),
        name="cut_edges",
    )(images, stencil)
    near_rows, far_rows = swapped("ion", n_ion, near_rows, far_rows)
    near, far, *turns = lax.optimization_barrier((near, far, *turns))
    mine = jnp.concatenate([mine, *turns], axis=0)
    near, far = swapped("pix", n_pix, near, far)
    odd = pix % 2 == 1
    after, before = jnp.where(odd, far, near), jnp.where(odd, near, far)
    columns = jnp.concatenate([after, jnp.zeros((4, rows), images.dtype), before], axis=0)

    distances = [n_pix >> k for k in range(1, n_pix.bit_length())]

    def exchange(value, distance):
        return lax.ppermute(value, "pix", [(i, i ^ distance) for i in range(n_pix)])

    mine = jnp.concatenate([mine, exchange(mine, distances[0])], axis=0)

    def place_of(rule):
        row = (rule & (rules_here - 1)) * block
        turn = (rule >> (rules_here.bit_length() - 1)) ^ lax.axis_index("ion")
        pieces = []
        for offset in range(0, block, min(part, block)):
            share_of = ((row + offset) >> (part.bit_length() - 1)) ^ lax.axis_index("pix")
            at = turn * part + ((row + offset) & (part - 1))
            for k, distance in enumerate(distances):
                at = at + jnp.where((share_of & distance) != 0, n_ion * part << k, 0)
            pieces.append(at)
        return pieces

    table_pairs = pairs.T
    group = next(g for g in (8, 5, 4, 2, 1) if blocks % g == 0)
    steps = blocks // group
    units = -(-2 * (blocks + 2 * REACH) // block)
    half = (chips, share, LANES)
    half_shape = (slots + units, *half)
    both_halves = [jax.ShapeDtypeStruct(half_shape, jnp.bfloat16)] * 2

    def rows_at(columns):
        return pl.BlockSpec((group * block, columns), lambda i, *_: (jnp.minimum(i, steps - 1), 0))

    smoothed, energy, keep, give = pl.pallas_call(
        functools.partial(main_kernel, steps, group, block),
        grid_spec=pltpu.PrefetchScalarGridSpec(
            num_scalar_prefetch=1,
            grid=(steps + 1,),
            in_specs=[
                rows_at(width),
                pl.BlockSpec((8, group * block), lambda i, *_: (0, jnp.minimum(i, steps - 1))),
                whole(weights.shape),
            ],
            out_specs=[hbm, whole((blocks, LANES)), whole(half_shape), whole(half_shape)],
            scratch_shapes=[pltpu.VMEM((blocks, block, width), jnp.bfloat16), pltpu.SemaphoreType.DMA((steps,))],
        ),
        out_shape=[
            jax.ShapeDtypeStruct((blocks, block, width), jnp.bfloat16),
            jax.ShapeDtypeStruct((blocks, LANES), jnp.float32),
            *both_halves,
        ],
        compiler_params=params(),
        cost_estimate=cost(2 * rows * width * DEPTH + 2 * slots * block * block * width, 4 * rows * width),
        name="smooth_and_gram",
    )(table_pairs, images, columns, weights)
    smoothed = smoothed.reshape(rows, width)

    energy, columns, mine = lax.optimization_barrier((energy, columns, mine))
    first, last = columns[:, :edge], columns[:, rows - edge :]
    odd = ion % 2 == 1
    near_columns, far_columns = swapped("ion", n_ion, jnp.where(odd, first, last), jnp.where(odd, last, first))
    for distance in distances[1:-1]:
        mine = jnp.concatenate([mine, exchange(mine, distance)], axis=0)

    keep, give = pl.pallas_call(
        functools.partial(cross_kernel, blocks, block),
        in_specs=[smem] + [hbm] * 4 + [fixed] * 5,
        out_specs=[vmem, vmem],
        out_shape=both_halves,
        scratch_shapes=[
            pltpu.VMEM((2 * edge, width), jnp.bfloat16),
            pltpu.VMEM((8, 2 * edge), jnp.bfloat16),
            pltpu.VMEM(weights.shape, jnp.bfloat16),
            pltpu.VMEM((blocks, LANES), jnp.float32),
            pltpu.VMEM((2 * edge, width), jnp.bfloat16),
            pltpu.VMEM((2 * edge, width), jnp.bfloat16),
            pltpu.VMEM((units * block // 2, LANES), jnp.float32),
            pltpu.SemaphoreType.DMA((10,)),
        ],
        compiler_params=params(),
        cost_estimate=cost(4 * edge * width * DEPTH, 8 * edge * width),
        name="cross_grams",
    )(table_pairs, near_rows, far_rows, near_columns, far_columns, weights, energy, smoothed, keep, give)

    got = lax.ppermute(give, "pix", [(i, i ^ 1) for i in range(n_pix)])
    message = jax.ShapeDtypeStruct((slots + units * chips, share, LANES), jnp.bfloat16)
    own_rows = jax.ShapeDtypeStruct((slots + units * chips, share, LANES), jnp.float32)
    small = pltpu.CompilerParams(vmem_limit_bytes=16 * 1024 * 1024)
    own, *messages = pl.pallas_call(
        functools.partial(chip_kernel, slots, units),
        in_specs=[fixed, hbm],
        out_specs=[vmem] * chips,
        out_shape=[own_rows] + [message] * (chips - 1),
        scratch_shapes=[
            pltpu.VMEM(half_shape, jnp.bfloat16),
            pltpu.VMEM(half_shape, jnp.bfloat16),
            pltpu.SemaphoreType.DMA((2,)),
        ],
        compiler_params=small,
        name="chip_sums",
    )(keep, got)
    own, mine = lax.optimization_barrier((own, mine))
    other = exchange(mine, distances[-1])
    received = [
        lax.ppermute(m, "pix", [(i, i ^ (2 * (d + 1))) for i in range(n_pix)]) for d, m in enumerate(messages)
    ]

    scores = pl.pallas_call(
        functools.partial(score_kernel, blocks, place_of, pixel_count),
        in_specs=[smem] * 3 + [hbm] * (chips + 2),
        out_specs=vmem,
        out_shape=jax.ShapeDtypeStruct((slots, share, block), jnp.bfloat16),
        scratch_shapes=[
            pltpu.VMEM(own_rows.shape, jnp.float32),
            *[pltpu.VMEM(message.shape, jnp.bfloat16)] * (chips - 1),
            pltpu.VMEM((2 * mine.shape[0], block), jnp.bfloat16),
            pltpu.VMEM((units * block // 2, LANES), jnp.float32),
            pltpu.VMEM((slots, LANES), jnp.float32),
            pltpu.VMEM((slots, LANES), jnp.float32),
            pltpu.VMEM((slots, share, LANES), jnp.bfloat16),
            pltpu.SMEM((-(-block // part), slots), jnp.int32),
            pltpu.SemaphoreType.DMA((chips + 2,)),
        ],
        compiler_params=small,
        name="scores",
    )(table_pairs, live, rule_of_block, own, *received, mine, other)
    return (smoothed, scores)


def solution(mesh):
    return jax.shard_map(
        on_device,
        mesh=mesh,
        in_specs=(
            P("ion", "pix"),
            P(None, "pix"),
            P("ion", None),
            P("ion"),
            P(),
            P("ion", None, None),
        ),
        out_specs=(P("ion", "pix"), P("ion", "pix", None)),
        check_vma=False,
    )
```

```python
import functools

import jax
import jax.numpy as jnp
from jax import lax
from jax.experimental import pallas as pl
from jax.experimental.pallas import tpu as pltpu
from jax.sharding import PartitionSpec as P

REACH = 3
OUTER = REACH - 1
TAPS = 5
LANES = 128
HALF = LANES // 2
DEPTH = 2 * LANES
VMEM_BYTES = 58 * 1024 * 1024


def params():
    return pltpu.CompilerParams(vmem_limit_bytes=VMEM_BYTES)


def cost(flops, moved):
    return pl.CostEstimate(flops=flops, bytes_accessed=moved, transcendentals=0)


def whole(shape):
    return pl.BlockSpec(shape, lambda *_: (0,) * len(shape))


def fetch(sources, targets, sems):
    copies = [pltpu.make_async_copy(x, y, sems.at[k]) for k, (x, y) in enumerate(zip(sources, targets))]
    for copy in copies:
        copy.start()
    return copies


def smooth_rows(x_ref, halo, w_ref, store):
    rows, width = x_ref.shape
    tiles = width // LANES
    first = lax.broadcasted_iota(jnp.int32, (rows, LANES), 1) < HALF
    before, total, squares = None, None, None
    for j in range(-1, tiles):
        if j < 0:
            window = jnp.concatenate([halo, x_ref[:, :LANES]], axis=1)
        elif j == tiles - 1:
            window = jnp.concatenate([x_ref[:, j * LANES :], halo], axis=1)
        else:
            window = x_ref[:, j * LANES : (j + 2) * LANES]
        now = jnp.dot(window, w_ref[j + 1], preferred_element_type=jnp.float32)
        if j >= 0:
            values = jnp.where(first, before, now)
            store(j, values.astype(jnp.bfloat16))
            squares = values * values if j % 2 == 0 else squares + values * values
            if j % 2 == 1:
                total = squares if total is None else total + squares
        before = now
    return total


def row_sums(part):
    return jnp.sum(part.T, axis=0, keepdims=True)


def gram_of(left, right):
    return lax.dot_general(
        left, right, (((1,), (1,)), ((), ())), preferred_element_type=jnp.float32
    )


def by_core(gram, chips, core):
    parts = gram.reshape(chips, 2, gram.shape[0] // (2 * chips), gram.shape[1])
    even, odd = parts[:, 0].astype(jnp.bfloat16), parts[:, 1].astype(jnp.bfloat16)
    return jnp.where(core == 0, even, odd), jnp.where(core == 0, odd, even)


def write_weights(stencil_ref, out_ref):
    tiles = stencil_ref.shape[1] // LANES
    out_ref[...] = jnp.zeros_like(out_ref)
    k0, rows = 3 * LANES // 8, 5 * LANES // 4
    k = lax.broadcasted_iota(jnp.int32, (rows, LANES), 0) + k0
    lane = lax.broadcasted_iota(jnp.int32, (rows, LANES), 1)
    tap = k - lane + jnp.where(lane < HALF, 2 - LANES, 2)
    early = lax.broadcasted_iota(jnp.int32, (TAPS, LANES), 1) < HALF
    zeros = jnp.zeros((TAPS, LANES), jnp.float32)
    for j in range(-1, tiles):
        here = stencil_ref[:, j * LANES : (j + 1) * LANES] if j >= 0 else zeros
        after = stencil_ref[:, (j + 1) * LANES : (j + 2) * LANES] if j + 1 < tiles else zeros
        taps = jnp.where(early, after, here)
        w = jnp.zeros((rows, LANES), jnp.float32)
        for t in range(TAPS):
            w = jnp.where(tap == t, taps[t : t + 1, :], w)
        out_ref[j + 1, k0 : k0 + rows] = w.astype(jnp.bfloat16)


def cut_kernel(images_ref, stencil_ref, near_rows, far_rows, near_columns, far_columns, w_ref, bands, strips, sems):
    rows, width = images_ref.shape
    edge = near_rows.shape[0]
    odd = lax.axis_index("ion") % 2
    starts = [pl.multiple_of(k * (rows - edge), edge // OUTER) for k in (1 - odd, odd)]
    reads = fetch(
        [images_ref.at[pl.ds(start, edge)] for start in starts]
        + [images_ref.at[:, pl.ds(start, LANES)] for start in (0, width - LANES)],
        [bands.at[0], bands.at[1], strips.at[0], strips.at[1]],
        sems,
    )
    writes = [
        pltpu.make_async_copy(bands.at[k], out, sems.at[4 + k]) for k, out in enumerate((near_rows, far_rows))
    ]
    write_weights(stencil_ref, w_ref)
    for read, write in zip(reads, writes):
        read.wait()
        write.start()
    row = lax.broadcasted_iota(jnp.int32, (8, LANES), 0)
    lane = lax.broadcasted_iota(jnp.int32, (8, LANES), 1)
    sides = []
    for k, shift in enumerate((0, LANES - 2)):
        reads[2 + k].wait()
        pick = (lane == row + shift).astype(jnp.bfloat16)
        sides.append(gram_of(pick, strips[k])[:2])
    head, tail = sides
    odd = lax.axis_index("pix") % 2 == 1
    near_columns[...] = jnp.where(odd, head, tail).astype(jnp.bfloat16)
    far_columns[...] = jnp.where(odd, tail, head).astype(jnp.bfloat16)
    for write in writes:
        write.wait()


def halo_tile(columns_ref):
    columns = columns_ref[...].astype(jnp.float32).T.astype(jnp.bfloat16)
    row = lax.broadcasted_iota(jnp.int32, (8, LANES), 0)
    lane = lax.broadcasted_iota(jnp.int32, (8, LANES), 1)
    place = (lane == row + jnp.where(row < 4, 0, LANES - 8)).astype(jnp.bfloat16)
    return jnp.dot(columns, place, preferred_element_type=jnp.float32).astype(jnp.bfloat16)


def main_kernel(steps, group, block, pairs_ref, x_ref, columns_ref, w_ref,
                out_hbm, energy_ref, keep_ref, give_ref, held, sems):
    step = pl.program_id(0)
    blocks = steps * group
    chips = keep_ref.shape[1]
    slots = pairs_ref.shape[1]

    def copy_out(k):
        here = pl.ds(k * group, group)
        return pltpu.make_async_copy(held.at[here], out_hbm.at[here], sems.at[k])

    @pl.when(step < steps)
    def smooth():
        def store(j, values):
            held[pl.ds(step * group, group), :, j * LANES : (j + 1) * LANES] = values.reshape(group, block, LANES)

        total = smooth_rows(x_ref, halo_tile(columns_ref), w_ref, store)
        copy_out(step).start()
        for g in range(group):
            energy_ref[pl.ds(step * group + g, 1), :] = row_sums(total[g * block : (g + 1) * block, :])

    @pl.when(step == steps)
    def grams():
        core = lax.axis_index("pix") % 2
        first = lax.axis_index("ion") * blocks

        def one(s, carry):
            a = pairs_ref[0, s] - first
            b = jnp.clip(pairs_ref[1, s] - first, 0, blocks - 1)
            keep_ref[s], give_ref[s] = by_core(gram_of(held[a], held[b]), chips, core)
            return carry

        lax.fori_loop(0, slots, one, 0, unroll=4)
        for k in range(steps):
            copy_out(k).wait()


def cross_kernel(blocks, block, pairs_ref, near_hbm, far_hbm, near_edge_hbm, far_edge_hbm, w_hbm, energy_hbm,
                 smoothed_hbm, keep_hbm, give_hbm, keep_ref, give_ref, near_same, near_cross, far_same, far_cross,
                 x_ref, edge_ref, w_ref, energy_ref, own, other, table, sems):
    core = lax.axis_index("pix") % 2
    first_block = lax.axis_index("ion") * blocks
    slots = pairs_ref.shape[1]
    chips, share = keep_ref.shape[1:3]
    units = keep_ref.shape[0] - slots
    edge = OUTER * block
    reach = REACH * block
    rows = blocks * block
    odd = lax.axis_index("ion") % 2
    near, far = (pl.ds(pl.multiple_of(k * edge, edge), edge) for k in (1 - odd, odd))
    copies = fetch(
        (near_hbm, far_hbm, near_edge_hbm, far_edge_hbm, w_hbm, energy_hbm, smoothed_hbm.at[pl.ds(0, reach)],
         smoothed_hbm.at[pl.ds(rows - reach, reach)], keep_hbm, give_hbm),
        (x_ref.at[near], x_ref.at[far], edge_ref.at[:, near], edge_ref.at[:, far], w_ref, energy_ref,
         own.at[pl.ds(0, reach)], own.at[pl.ds(reach, reach)], keep_ref, give_ref),
        sems,
    )
    for copy in copies[:6]:
        copy.wait()
    table[...] = jnp.zeros_like(table)
    table[REACH : REACH + blocks, :] = energy_ref[...]

    def store(j, values):
        other[:, j * LANES : (j + 1) * LANES] = values

    total = smooth_rows(x_ref, halo_tile(edge_ref.at[:8]), w_ref, store)
    for k in range(2 * OUTER):
        row = k + 1 if k < OUTER else k + 1 + blocks
        table[row : row + 1, :] = row_sums(total[k * block : (k + 1) * block, :])
    for row, lane in ((0, 0), (2 * REACH + blocks - 1, edge)):
        table[row : row + 1, :] = edge_ref[8:, lane : lane + LANES].astype(jnp.float32)[:1]
    for copy in copies[6:]:
        copy.wait()

    shape = (units, chips, share, LANES)
    for ref in (keep_ref, give_ref):
        ref[slots:] = table[...].reshape(shape).astype(jnp.bfloat16)

    def one(s, carry):
        a, b = pairs_ref[0, s] - first_block, pairs_ref[1, s] - first_block

        @pl.when(((b < 0) & (b >= -OUTER)) | ((b >= blocks) & (b < blocks + OUTER)))
        def crossing():
            side = (b >= 0).astype(jnp.int32)
            a_row = pl.multiple_of((a - side * (blocks - 2 * REACH)) * block, block)
            b_row = pl.multiple_of((b + OUTER - side * blocks) * block, block)
            gram = gram_of(own[pl.ds(a_row, block), :], other[pl.ds(b_row, block), :])
            keep_ref[s], give_ref[s] = by_core(gram, chips, core)

        return carry

    lax.fori_loop(0, slots, one, 0)

    def piece(ref, k):
        return ref[k * block : (k + 1) * block, :]

    above = by_core(gram_of(piece(other, OUTER), piece(own, REACH)), chips, core)
    below = by_core(gram_of(piece(other, OUTER - 1), piece(own, REACH - 1)), chips, core)
    for k, (near_ref, far_ref) in enumerate(((near_same, far_same), (near_cross, far_cross))):
        near_ref[...] = jnp.where(odd == 1, below[k], above[k])
        far_ref[...] = jnp.where(odd == 1, above[k], below[k])


def chip_kernel(blocks, slots, units, pairs_ref, keep_hbm, got_hbm, *refs):
    third_hbm, own_ref, out_refs, (keep_ref, got_ref, third, sems) = refs[:4], refs[4], refs[5:-4], refs[-4:]
    chip = lax.axis_index("pix") // 2
    first_block = lax.axis_index("ion") * blocks
    odd = lax.axis_index("ion") % 2
    chips, share = keep_ref.shape[1:3]
    shape = (units * chips, share, LANES)
    targets = [keep_ref, got_ref] + [third.at[k] for k in range(4)]
    for copy in fetch((keep_hbm, got_hbm, *third_hbm), targets, sems):
        copy.wait()

    def one(s, carry):
        b = pairs_ref[1, s] - first_block

        @pl.when((b == -REACH) | (b == blocks + REACH - 1))
        def returned():
            above = (b > 0).astype(jnp.int32)
            place = jnp.where(above + odd == 1, 0, 2)
            keep_ref[s] = third[place]
            got_ref[s] = third[place + 1]

        return carry

    lax.fori_loop(0, slots, one, 0)
    energies = (keep_ref[slots:].astype(jnp.float32) + got_ref[slots:].astype(jnp.float32)).reshape(shape)
    for d in range(chips):
        total = keep_ref[:slots, chip ^ d].astype(jnp.float32) + got_ref[:slots, chip ^ d].astype(jnp.float32)
        if d == 0:
            own_ref[:slots] = total
            own_ref[slots:] = energies
        else:
            out = out_refs[d - 1]
            out[:slots] = total.astype(jnp.bfloat16)
            out[slots:] = energies.astype(jnp.bfloat16)


def score_kernel(blocks, place_of, pixel_count, pairs_ref, live_ref, rules_ref, *refs):
    chips = (len(refs) - 9) // 2
    sources, out_ref, own_ref = refs[: chips + 2], refs[chips + 2], refs[chips + 3]
    got_refs, (table_ref, inverse, left, right, coloc, place, sems) = refs[chips + 4 : -7], refs[-7:]
    slots, share, block = out_ref.shape
    half = table_ref.shape[0] // 2
    targets = (own_ref, *got_refs, table_ref.at[pl.ds(0, half)], table_ref.at[pl.ds(half, half)])
    copies = fetch(sources, targets, sems)
    pix, first = lax.axis_index("pix"), lax.axis_index("ion") * blocks
    pieces = place.shape[0]
    depth = block // pieces

    def find(s, carry):
        for k, at in enumerate(place_of(rules_ref[pairs_ref[1, s]])):
            place[k, s] = at
        return carry

    lax.fori_loop(0, slots, find, 0)
    for copy in copies[:-2]:
        copy.wait()
    gram = own_ref[:slots]
    energies = own_ref[slots:]
    for got in got_refs:
        gram = gram + got[:slots].astype(jnp.float32)
        energies = energies + got[slots:].astype(jnp.float32)
    inverse[...] = (1.0 / jnp.sqrt(energies / pixel_count + 1e-06)).reshape(inverse.shape)

    def pick(s, carry):
        left[pl.ds(s, 1), :] = inverse[pl.ds(pairs_ref[0, s] - first + REACH, 1), :]
        right[pl.ds(s, 1), :] = inverse[pl.ds(pairs_ref[1, s] - first + REACH, 1), :]
        return carry

    lax.fori_loop(0, slots, pick, 0, unroll=8)
    lane = lax.broadcasted_iota(jnp.int32, (1, share, LANES), 2)
    mine = lane == lax.broadcasted_iota(jnp.int32, (1, share, LANES), 1) + pix * share
    inv_a = jnp.sum(jnp.where(mine, left[...][:, None, :], 0.0), axis=2, keepdims=True)
    coloc[...] = (gram * inv_a * right[...][:, None, :] / pixel_count).astype(jnp.bfloat16)
    for copy in copies[-2:]:
        copy.wait()

    def one(s, carry):
        scores = jnp.zeros((share, block), jnp.float32)
        for k in range(pieces):
            matrix = table_ref[pl.ds(pl.multiple_of(place[k, s], depth), depth), :]
            part = coloc[s, :, k * depth : (k + 1) * depth]
            scores = scores + jnp.dot(part, matrix, preferred_element_type=jnp.float32)
        out_ref[s] = jnp.where(s < live_ref[0], scores, 0.0).astype(jnp.bfloat16)
        return carry

    lax.fori_loop(0, slots, one, 0, unroll=slots)


def on_device(images, stencil, pairs, live, rule_of_block, adduct):
    rows, width = images.shape
    rules_here, block, _ = adduct.shape
    blocks = rows // block
    slots = pairs.shape[0]
    n_pix, n_ion = lax.axis_size("pix"), lax.axis_size("ion")
    pix, ion = lax.axis_index("pix"), lax.axis_index("ion")
    pixel_count = width * n_pix
    chips, share = n_pix // 2, block // n_pix
    core, chip = pix % 2, pix // 2
    edge = OUTER * block

    def swapped(axis, size, near, far):
        pairs_of = [[(i, i + 1) for i in range(first, size - 1, 2)] for first in (0, 1)]
        return [
            lax.ppermute(value, axis, both + [(j, i) for i, j in both]) for value, both in zip((near, far), pairs_of)
        ]

    vmem = pl.BlockSpec(memory_space=pltpu.VMEM)
    smem = pl.BlockSpec(memory_space=pltpu.SMEM)
    hbm = pl.BlockSpec(memory_space=pl.ANY)
    fixed = pl.BlockSpec(memory_space=pltpu.HBM)

    part = rules_here * block // n_pix
    mine = lax.dynamic_slice_in_dim(adduct.reshape(rules_here * block, block), pix * part, part, 0)
    turns = [lax.ppermute(mine, "ion", [(i, i ^ d) for i in range(n_ion)]) for d in range(1, n_ion)]

    edge_rows = jax.ShapeDtypeStruct((edge, width), images.dtype)
    edge_columns = jax.ShapeDtypeStruct((2, rows), images.dtype)
    near_rows, far_rows, near, far, weights = pl.pallas_call(
        cut_kernel,
        in_specs=[hbm, vmem],
        out_specs=[hbm, hbm, vmem, vmem, vmem],
        out_shape=[
            edge_rows,
            edge_rows,
            edge_columns,
            edge_columns,
            jax.ShapeDtypeStruct((width // LANES + 1, DEPTH, LANES), jnp.bfloat16),
        ],
        scratch_shapes=[
            pltpu.VMEM((2, edge, width), images.dtype),
            pltpu.VMEM((2, rows, LANES), images.dtype),
            pltpu.SemaphoreType.DMA((6,)),
        ],
        compiler_params=params(),
        cost_estimate=cost(0, 8 * edge * width),
        name="cut_edges",
    )(images, stencil)
    near_rows, far_rows = swapped("ion", n_ion, near_rows, far_rows)
    near, far, *turns = lax.optimization_barrier((near, far, *turns))
    mine = jnp.concatenate([mine, *turns], axis=0)
    near, far = swapped("pix", n_pix, near, far)
    odd = pix % 2 == 1
    after, before = jnp.where(odd, far, near), jnp.where(odd, near, far)
    columns = jnp.concatenate([after, jnp.zeros((4, rows), images.dtype), before], axis=0)

    distances = [n_pix >> k for k in range(1, n_pix.bit_length())]

    def exchange(value, distance):
        return lax.ppermute(value, "pix", [(i, i ^ distance) for i in range(n_pix)])

    mine = jnp.concatenate([mine, exchange(mine, distances[0])], axis=0)

    def place_of(rule):
        row = (rule & (rules_here - 1)) * block
        turn = (rule >> (rules_here.bit_length() - 1)) ^ lax.axis_index("ion")
        pieces = []
        for offset in range(0, block, min(part, block)):
            share_of = ((row + offset) >> (part.bit_length() - 1)) ^ lax.axis_index("pix")
            at = turn * part + ((row + offset) & (part - 1))
            for k, distance in enumerate(distances):
                at = at + jnp.where((share_of & distance) != 0, n_ion * part << k, 0)
            pieces.append(at)
        return pieces

    table_pairs = pairs.T
    group = next(g for g in (8, 5, 4, 2, 1) if blocks % g == 0)
    steps = blocks // group
    units = -(-2 * (blocks + 2 * REACH) // block)
    half = (chips, share, LANES)
    half_shape = (slots + units, *half)
    both_halves = [jax.ShapeDtypeStruct(half_shape, jnp.bfloat16)] * 2

    def rows_at(columns):
        return pl.BlockSpec((group * block, columns), lambda i, *_: (jnp.minimum(i, steps - 1), 0))

    smoothed, energy, keep, give = pl.pallas_call(
        functools.partial(main_kernel, steps, group, block),
        grid_spec=pltpu.PrefetchScalarGridSpec(
            num_scalar_prefetch=1,
            grid=(steps + 1,),
            in_specs=[
                rows_at(width),
                pl.BlockSpec((8, group * block), lambda i, *_: (0, jnp.minimum(i, steps - 1))),
                whole(weights.shape),
            ],
            out_specs=[hbm, whole((blocks, LANES)), whole(half_shape), whole(half_shape)],
            scratch_shapes=[pltpu.VMEM((blocks, block, width), jnp.bfloat16), pltpu.SemaphoreType.DMA((steps,))],
        ),
        out_shape=[
            jax.ShapeDtypeStruct((blocks, block, width), jnp.bfloat16),
            jax.ShapeDtypeStruct((blocks, LANES), jnp.float32),
            *both_halves,
        ],
        compiler_params=params(),
        cost_estimate=cost(2 * rows * width * DEPTH + 2 * slots * block * block * width, 4 * rows * width),
        name="smooth_and_gram",
    )(table_pairs, images, columns, weights)
    smoothed = smoothed.reshape(rows, width)

    energy, columns, mine = lax.optimization_barrier((energy, columns, mine))
    third = jnp.pad(energy.astype(jnp.bfloat16), ((0, 0), (0, edge - LANES)))
    rest = jnp.zeros((7, edge), images.dtype)
    first = jnp.concatenate([columns[:, :edge], third[REACH - 1 : REACH], rest], axis=0)
    last = jnp.concatenate([columns[:, rows - edge :], third[blocks - REACH : blocks - REACH + 1], rest], axis=0)
    odd = ion % 2 == 1
    near_edge, far_edge = swapped("ion", n_ion, jnp.where(odd, first, last), jnp.where(odd, last, first))
    for distance in distances[1:-1]:
        mine = jnp.concatenate([mine, exchange(mine, distance)], axis=0)

    keep, give, *third = pl.pallas_call(
        functools.partial(cross_kernel, blocks, block),
        in_specs=[smem] + [hbm] * 4 + [fixed] * 5,
        out_specs=[vmem] * 6,
        out_shape=both_halves + [jax.ShapeDtypeStruct(half, jnp.bfloat16)] * 4,
        scratch_shapes=[
            pltpu.VMEM((2 * edge, width), jnp.bfloat16),
            pltpu.VMEM((16, 2 * edge), jnp.bfloat16),
            pltpu.VMEM(weights.shape, jnp.bfloat16),
            pltpu.VMEM((blocks, LANES), jnp.float32),
            pltpu.VMEM((2 * REACH * block, width), jnp.bfloat16),
            pltpu.VMEM((2 * edge, width), jnp.bfloat16),
            pltpu.VMEM((units * block // 2, LANES), jnp.float32),
            pltpu.SemaphoreType.DMA((10,)),
        ],
        compiler_params=params(),
        cost_estimate=cost(4 * edge * width * DEPTH, 8 * edge * width),
        name="cross_grams",
    )(table_pairs, near_rows, far_rows, near_edge, far_edge, weights, energy, smoothed, keep, give)

    got = lax.ppermute(give, "pix", [(i, i ^ 1) for i in range(n_pix)])

    def both_cores(same, cross, first):
        both = [(i, i + 1) for i in range(first, n_ion - 1, 2)]
        both += [(j, i) for i, j in both]
        crossing = [(p * n_ion + i, (p ^ 1) * n_ion + j) for p in range(n_pix) for i, j in both]
        return lax.ppermute(same, "ion", both), lax.ppermute(cross, ("pix", "ion"), crossing)

    third = both_cores(*third[:2], 0) + both_cores(*third[2:], 1)
    message = jax.ShapeDtypeStruct((slots + units * chips, share, LANES), jnp.bfloat16)
    own_rows = jax.ShapeDtypeStruct((slots + units * chips, share, LANES), jnp.float32)
    small = pltpu.CompilerParams(vmem_limit_bytes=16 * 1024 * 1024)
    own, *messages = pl.pallas_call(
        functools.partial(chip_kernel, blocks, slots, units),
        in_specs=[smem, fixed] + [hbm] * 5,
        out_specs=[vmem] * chips,
        out_shape=[own_rows] + [message] * (chips - 1),
        scratch_shapes=[
            pltpu.VMEM(half_shape, jnp.bfloat16),
            pltpu.VMEM(half_shape, jnp.bfloat16),
            pltpu.VMEM((4, *half), jnp.bfloat16),
            pltpu.SemaphoreType.DMA((6,)),
        ],
        compiler_params=small,
        name="chip_sums",
    )(table_pairs, keep, got, *third)
    own, mine = lax.optimization_barrier((own, mine))
    other = exchange(mine, distances[-1])
    received = [
        lax.ppermute(m, "pix", [(i, i ^ (2 * (d + 1))) for i in range(n_pix)]) for d, m in enumerate(messages)
    ]

    scores = pl.pallas_call(
        functools.partial(score_kernel, blocks, place_of, pixel_count),
        in_specs=[smem] * 3 + [hbm] * (chips + 2),
        out_specs=vmem,
        out_shape=jax.ShapeDtypeStruct((slots, share, block), jnp.bfloat16),
        scratch_shapes=[
            pltpu.VMEM(own_rows.shape, jnp.float32),
            *[pltpu.VMEM(message.shape, jnp.bfloat16)] * (chips - 1),
            pltpu.VMEM((2 * mine.shape[0], block), jnp.bfloat16),
            pltpu.VMEM((units * block // 2, LANES), jnp.float32),
            pltpu.VMEM((slots, LANES), jnp.float32),
            pltpu.VMEM((slots, LANES), jnp.float32),
            pltpu.VMEM((slots, share, LANES), jnp.bfloat16),
            pltpu.SMEM((-(-block // part), slots), jnp.int32),
            pltpu.SemaphoreType.DMA((chips + 2,)),
        ],
        compiler_params=small,
        name="scores",
    )(table_pairs, live, rule_of_block, own, *received, mine, other)
    return (smoothed, scores)


def solution(mesh):
    return jax.shard_map(
        on_device,
        mesh=mesh,
        in_specs=(
            P("ion", "pix"),
            P(None, "pix"),
            P("ion", None),
            P("ion"),
            P(),
            P("ion", None, None),
        ),
        out_specs=(P("ion", "pix"), P("ion", "pix", None)),
        check_vma=False,
    )
```

```python
import functools

import jax
import jax.numpy as jnp
from jax import lax
from jax.experimental import pallas as pl
from jax.experimental.pallas import tpu as pltpu
from jax.sharding import PartitionSpec as P

REACH = 3
TAPS = 5
LANES = 128
HALF = LANES // 2
DEPTH = 2 * LANES
VMEM_BYTES = 58 * 1024 * 1024


def params():
    return pltpu.CompilerParams(vmem_limit_bytes=VMEM_BYTES)


def cost(flops, moved):
    return pl.CostEstimate(flops=flops, bytes_accessed=moved, transcendentals=0)


def whole(shape):
    return pl.BlockSpec(shape, lambda *_: (0,) * len(shape))


def fetch(sources, targets, sems):
    copies = [pltpu.make_async_copy(x, y, sems.at[k]) for k, (x, y) in enumerate(zip(sources, targets))]
    for copy in copies:
        copy.start()
    return copies


def smooth_rows(x_ref, halo, w_ref, store):
    rows, width = x_ref.shape
    tiles = width // LANES
    first = lax.broadcasted_iota(jnp.int32, (rows, LANES), 1) < HALF
    before, total, squares = None, None, None
    for j in range(-1, tiles):
        if j < 0:
            window = jnp.concatenate([halo, x_ref[:, :LANES]], axis=1)
        elif j == tiles - 1:
            window = jnp.concatenate([x_ref[:, j * LANES :], halo], axis=1)
        else:
            window = x_ref[:, j * LANES : (j + 2) * LANES]
        now = jnp.dot(window, w_ref[j + 1], preferred_element_type=jnp.float32)
        if j >= 0:
            values = jnp.where(first, before, now)
            store(j, values.astype(jnp.bfloat16))
            squares = values * values if j % 2 == 0 else squares + values * values
            if j % 2 == 1:
                total = squares if total is None else total + squares
        before = now
    return total


def row_sums(part):
    return jnp.sum(part.T, axis=0, keepdims=True)


def gram_of(left, right):
    return lax.dot_general(
        left, right, (((1,), (1,)), ((), ())), preferred_element_type=jnp.float32
    )


def by_core(gram, chips, core):
    parts = gram.reshape(chips, 2, gram.shape[0] // (2 * chips), gram.shape[1])
    even, odd = parts[:, 0].astype(jnp.bfloat16), parts[:, 1].astype(jnp.bfloat16)
    return jnp.where(core == 0, even, odd), jnp.where(core == 0, odd, even)


def write_weights(stencil_ref, out_ref):
    tiles = stencil_ref.shape[1] // LANES
    out_ref[...] = jnp.zeros_like(out_ref)
    k0, rows = 3 * LANES // 8, 5 * LANES // 4
    k = lax.broadcasted_iota(jnp.int32, (rows, LANES), 0) + k0
    lane = lax.broadcasted_iota(jnp.int32, (rows, LANES), 1)
    tap = k - lane + jnp.where(lane < HALF, 2 - LANES, 2)
    early = lax.broadcasted_iota(jnp.int32, (TAPS, LANES), 1) < HALF
    zeros = jnp.zeros((TAPS, LANES), jnp.float32)
    for j in range(-1, tiles):
        here = stencil_ref[:, j * LANES : (j + 1) * LANES] if j >= 0 else zeros
        after = stencil_ref[:, (j + 1) * LANES : (j + 2) * LANES] if j + 1 < tiles else zeros
        taps = jnp.where(early, after, here)
        w = jnp.zeros((rows, LANES), jnp.float32)
        for t in range(TAPS):
            w = jnp.where(tap == t, taps[t : t + 1, :], w)
        out_ref[j + 1, k0 : k0 + rows] = w.astype(jnp.bfloat16)


def cut_kernel(images_ref, stencil_ref, near_rows, far_rows, near_columns, far_columns, w_ref, bands, strips, sems):
    rows, width = images_ref.shape
    edge = near_rows.shape[0]
    odd = lax.axis_index("ion") % 2
    starts = [pl.multiple_of(k * (rows - edge), edge // REACH) for k in (1 - odd, odd)]
    reads = fetch(
        [images_ref.at[pl.ds(start, edge)] for start in starts]
        + [images_ref.at[:, pl.ds(start, LANES)] for start in (0, width - LANES)],
        [bands.at[0], bands.at[1], strips.at[0], strips.at[1]],
        sems,
    )
    writes = [
        pltpu.make_async_copy(bands.at[k], out, sems.at[4 + k]) for k, out in enumerate((near_rows, far_rows))
    ]
    write_weights(stencil_ref, w_ref)
    for read, write in zip(reads, writes):
        read.wait()
        write.start()
    row = lax.broadcasted_iota(jnp.int32, (8, LANES), 0)
    lane = lax.broadcasted_iota(jnp.int32, (8, LANES), 1)
    sides = []
    for k, shift in enumerate((0, LANES - 2)):
        reads[2 + k].wait()
        pick = (lane == row + shift).astype(jnp.bfloat16)
        sides.append(gram_of(pick, strips[k])[:2])
    head, tail = sides
    odd = lax.axis_index("pix") % 2 == 1
    near_columns[...] = jnp.where(odd, head, tail).astype(jnp.bfloat16)
    far_columns[...] = jnp.where(odd, tail, head).astype(jnp.bfloat16)
    for write in writes:
        write.wait()


def halo_tile(columns_ref):
    columns = columns_ref[...].astype(jnp.float32).T.astype(jnp.bfloat16)
    row = lax.broadcasted_iota(jnp.int32, (8, LANES), 0)
    lane = lax.broadcasted_iota(jnp.int32, (8, LANES), 1)
    place = (lane == row + jnp.where(row < 4, 0, LANES - 8)).astype(jnp.bfloat16)
    return jnp.dot(columns, place, preferred_element_type=jnp.float32).astype(jnp.bfloat16)


def main_kernel(steps, group, block, pairs_ref, x_ref, columns_ref, w_ref,
                out_hbm, energy_ref, keep_ref, give_ref, held, sems):
    step = pl.program_id(0)
    blocks = steps * group
    chips = keep_ref.shape[1]
    slots = pairs_ref.shape[1]

    def copy_out(k):
        here = pl.ds(k * group, group)
        return pltpu.make_async_copy(held.at[here], out_hbm.at[here], sems.at[k])

    @pl.when(step < steps)
    def smooth():
        def store(j, values):
            held[pl.ds(step * group, group), :, j * LANES : (j + 1) * LANES] = values.reshape(group, block, LANES)

        total = smooth_rows(x_ref, halo_tile(columns_ref), w_ref, store)
        for g in range(group):
            energy_ref[pl.ds(step * group + g, 1), :] = row_sums(total[g * block : (g + 1) * block, :])

    @pl.when(step == steps)
    def grams():
        for k in range(steps):
            copy_out(k).start()
        core = lax.axis_index("pix") % 2
        first = lax.axis_index("ion") * blocks

        def one(s, carry):
            a = pairs_ref[0, s] - first
            b = jnp.clip(pairs_ref[1, s] - first, 0, blocks - 1)
            keep_ref[s], give_ref[s] = by_core(gram_of(held[a], held[b]), chips, core)
            return carry

        lax.fori_loop(0, slots, one, 0, unroll=4)
        for k in range(steps):
            copy_out(k).wait()


def cross_kernel(blocks, block, pairs_ref, near_hbm, far_hbm, near_columns_hbm, far_columns_hbm, w_hbm, energy_hbm, smoothed_hbm, keep_hbm,
                 give_hbm, keep_ref, give_ref, x_ref, columns_ref, w_ref, energy_ref, own, other, table, sems):
    core = lax.axis_index("pix") % 2
    first_block = lax.axis_index("ion") * blocks
    slots = pairs_ref.shape[1]
    chips, share = keep_ref.shape[1:3]
    units = keep_ref.shape[0] - slots
    edge = REACH * block
    rows = blocks * block
    low, high = pl.ds(0, edge), pl.ds(edge, edge)
    odd = lax.axis_index("ion") % 2
    near, far = (pl.ds(pl.multiple_of(k * edge, edge), edge) for k in (1 - odd, odd))
    copies = fetch(
        (near_hbm, far_hbm, near_columns_hbm, far_columns_hbm, w_hbm, energy_hbm, smoothed_hbm.at[low],
         smoothed_hbm.at[pl.ds(rows - edge, edge)], keep_hbm, give_hbm),
        (x_ref.at[near], x_ref.at[far], columns_ref.at[:, near], columns_ref.at[:, far], w_ref, energy_ref, own.at[low],
         own.at[high], keep_ref, give_ref),
        sems,
    )
    for copy in copies[:6]:
        copy.wait()
    table[...] = jnp.zeros_like(table)
    table[REACH : REACH + blocks, :] = energy_ref[...]
    def store(j, values):
        other[:, j * LANES : (j + 1) * LANES] = values

    total = smooth_rows(x_ref, halo_tile(columns_ref), w_ref, store)
    for k in range(2 * REACH):
        row = k if k < REACH else k + blocks
        table[row : row + 1, :] = row_sums(total[k * block : (k + 1) * block, :])
    for copy in copies[6:]:
        copy.wait()

    shape = (units, chips, share, LANES)
    for ref in (keep_ref, give_ref):
        ref[slots:] = table[...].reshape(shape).astype(jnp.bfloat16)

    def one(s, carry):
        a, b = pairs_ref[0, s] - first_block, pairs_ref[1, s] - first_block

        @pl.when((b < 0) | (b >= blocks))
        def crossing():
            side = (b >= 0).astype(jnp.int32)
            a_row = pl.multiple_of((a - side * (blocks - 2 * REACH)) * block, block)
            b_row = pl.multiple_of((b + REACH - side * blocks) * block, block)
            gram = gram_of(own[pl.ds(a_row, block), :], other[pl.ds(b_row, block), :])
            keep_ref[s], give_ref[s] = by_core(gram, chips, core)

        return carry

    lax.fori_loop(0, slots, one, 0)


def chip_kernel(slots, units, keep_hbm, got_hbm, own_ref, *refs):
    out_refs, (keep_ref, got_ref, sems) = refs[:-3], refs[-3:]
    chip = lax.axis_index("pix") // 2
    chips, share = keep_ref.shape[1:3]
    shape = (units * chips, share, LANES)
    for copy in fetch((keep_hbm, got_hbm), (keep_ref, got_ref), sems):
        copy.wait()
    energies = (keep_ref[slots:].astype(jnp.float32) + got_ref[slots:].astype(jnp.float32)).reshape(shape)
    for d in range(chips):
        total = keep_ref[:slots, chip ^ d].astype(jnp.float32) + got_ref[:slots, chip ^ d].astype(jnp.float32)
        if d == 0:
            own_ref[:slots] = total
            own_ref[slots:] = energies
        else:
            out = out_refs[d - 1]
            out[:slots] = total.astype(jnp.bfloat16)
            out[slots:] = energies.astype(jnp.bfloat16)


def score_kernel(blocks, place_of, pixel_count, pairs_ref, live_ref, rules_ref, *refs):
    chips = (len(refs) - 9) // 2
    sources, out_ref, own_ref = refs[: chips + 2], refs[chips + 2], refs[chips + 3]
    got_refs, (table_ref, inverse, left, right, coloc, place, sems) = refs[chips + 4 : -7], refs[-7:]
    slots, share, block = out_ref.shape
    half = table_ref.shape[0] // 2
    targets = (own_ref, *got_refs, table_ref.at[pl.ds(0, half)], table_ref.at[pl.ds(half, half)])
    copies = fetch(sources, targets, sems)
    pix, first = lax.axis_index("pix"), lax.axis_index("ion") * blocks
    pieces = place.shape[0]
    depth = block // pieces

    def find(s, carry):
        for k, at in enumerate(place_of(rules_ref[pairs_ref[1, s]])):
            place[k, s] = at
        return carry

    lax.fori_loop(0, slots, find, 0)
    for copy in copies[:-2]:
        copy.wait()
    gram = own_ref[:slots]
    energies = own_ref[slots:]
    for got in got_refs:
        gram = gram + got[:slots].astype(jnp.float32)
        energies = energies + got[slots:].astype(jnp.float32)
    inverse[...] = (1.0 / jnp.sqrt(energies / pixel_count + 1e-06)).reshape(inverse.shape)

    def pick(s, carry):
        left[pl.ds(s, 1), :] = inverse[pl.ds(pairs_ref[0, s] - first + REACH, 1), :]
        right[pl.ds(s, 1), :] = inverse[pl.ds(pairs_ref[1, s] - first + REACH, 1), :]
        return carry

    lax.fori_loop(0, slots, pick, 0, unroll=8)
    lane = lax.broadcasted_iota(jnp.int32, (1, share, LANES), 2)
    mine = lane == lax.broadcasted_iota(jnp.int32, (1, share, LANES), 1) + pix * share
    inv_a = jnp.sum(jnp.where(mine, left[...][:, None, :], 0.0), axis=2, keepdims=True)
    coloc[...] = (gram * inv_a * right[...][:, None, :] / pixel_count).astype(jnp.bfloat16)
    for copy in copies[-2:]:
        copy.wait()

    def one(s, carry):
        scores = jnp.zeros((share, block), jnp.float32)
        for k in range(pieces):
            matrix = table_ref[pl.ds(pl.multiple_of(place[k, s], depth), depth), :]
            part = coloc[s, :, k * depth : (k + 1) * depth]
            scores = scores + jnp.dot(part, matrix, preferred_element_type=jnp.float32)
        out_ref[s] = jnp.where(s < live_ref[0], scores, 0.0).astype(jnp.bfloat16)
        return carry

    lax.fori_loop(0, slots, one, 0, unroll=slots)


def on_device(images, stencil, pairs, live, rule_of_block, adduct):
    rows, width = images.shape
    rules_here, block, _ = adduct.shape
    blocks = rows // block
    slots = pairs.shape[0]
    n_pix, n_ion = lax.axis_size("pix"), lax.axis_size("ion")
    pix, ion = lax.axis_index("pix"), lax.axis_index("ion")
    pixel_count = width * n_pix
    chips, share = n_pix // 2, block // n_pix
    core, chip = pix % 2, pix // 2
    edge = REACH * block

    def swapped(axis, size, near, far):
        pairs_of = [[(i, i + 1) for i in range(first, size - 1, 2)] for first in (0, 1)]
        return [
            lax.ppermute(value, axis, both + [(j, i) for i, j in both]) for value, both in zip((near, far), pairs_of)
        ]

    vmem = pl.BlockSpec(memory_space=pltpu.VMEM)
    smem = pl.BlockSpec(memory_space=pltpu.SMEM)
    hbm = pl.BlockSpec(memory_space=pl.ANY)
    fixed = pl.BlockSpec(memory_space=pltpu.HBM)

    part = rules_here * block // n_pix
    mine = lax.dynamic_slice_in_dim(adduct.reshape(rules_here * block, block), pix * part, part, 0)
    turns = [lax.ppermute(mine, "ion", [(i, i ^ d) for i in range(n_ion)]) for d in range(1, n_ion)]

    edge_rows = jax.ShapeDtypeStruct((edge, width), images.dtype)
    edge_columns = jax.ShapeDtypeStruct((2, rows), images.dtype)
    near_rows, far_rows, near, far, weights = pl.pallas_call(
        cut_kernel,
        in_specs=[hbm, vmem],
        out_specs=[hbm, hbm, vmem, vmem, vmem],
        out_shape=[
            edge_rows,
            edge_rows,
            edge_columns,
            edge_columns,
            jax.ShapeDtypeStruct((width // LANES + 1, DEPTH, LANES), jnp.bfloat16),
        ],
        scratch_shapes=[
            pltpu.VMEM((2, edge, width), images.dtype),
            pltpu.VMEM((2, rows, LANES), images.dtype),
            pltpu.SemaphoreType.DMA((6,)),
        ],
        compiler_params=params(),
        cost_estimate=cost(0, 8 * edge * width),
        name="cut_edges",
    )(images, stencil)
    near_rows, far_rows = swapped("ion", n_ion, near_rows, far_rows)
    near, far, *turns = lax.optimization_barrier((near, far, *turns))
    mine = jnp.concatenate([mine, *turns], axis=0)
    near, far = swapped("pix", n_pix, near, far)
    odd = pix % 2 == 1
    after, before = jnp.where(odd, far, near), jnp.where(odd, near, far)
    columns = jnp.concatenate([after, jnp.zeros((4, rows), images.dtype), before], axis=0)
    first, last = columns[:, :edge], columns[:, rows - edge :]
    odd = ion % 2 == 1
    near_columns, far_columns = swapped("ion", n_ion, jnp.where(odd, first, last), jnp.where(odd, last, first))
    columns, near_columns, far_columns = lax.optimization_barrier((columns, near_columns, far_columns))

    distances = [n_pix >> k for k in range(1, n_pix.bit_length())]

    def exchange(value, distance):
        return lax.ppermute(value, "pix", [(i, i ^ distance) for i in range(n_pix)])

    mine = jnp.concatenate([mine, exchange(mine, distances[0])], axis=0)

    def place_of(rule):
        row = (rule & (rules_here - 1)) * block
        turn = (rule >> (rules_here.bit_length() - 1)) ^ lax.axis_index("ion")
        pieces = []
        for offset in range(0, block, min(part, block)):
            share_of = ((row + offset) >> (part.bit_length() - 1)) ^ lax.axis_index("pix")
            at = turn * part + ((row + offset) & (part - 1))
            for k, distance in enumerate(distances):
                at = at + jnp.where((share_of & distance) != 0, n_ion * part << k, 0)
            pieces.append(at)
        return pieces

    table_pairs = pairs.T
    group = next(g for g in (8, 5, 4, 2, 1) if blocks % g == 0)
    steps = blocks // group
    units = -(-2 * (blocks + 2 * REACH) // block)
    half = (chips, share, LANES)
    half_shape = (slots + units, *half)
    both_halves = [jax.ShapeDtypeStruct(half_shape, jnp.bfloat16)] * 2

    def rows_at(columns):
        return pl.BlockSpec((group * block, columns), lambda i, *_: (jnp.minimum(i, steps - 1), 0))

    smoothed, energy, keep, give = pl.pallas_call(
        functools.partial(main_kernel, steps, group, block),
        grid_spec=pltpu.PrefetchScalarGridSpec(
            num_scalar_prefetch=1,
            grid=(steps + 1,),
            in_specs=[
                rows_at(width),
                pl.BlockSpec((8, group * block), lambda i, *_: (0, jnp.minimum(i, steps - 1))),
                whole(weights.shape),
            ],
            out_specs=[hbm, whole((blocks, LANES)), whole(half_shape), whole(half_shape)],
            scratch_shapes=[pltpu.VMEM((blocks, block, width), jnp.bfloat16), pltpu.SemaphoreType.DMA((steps,))],
        ),
        out_shape=[
            jax.ShapeDtypeStruct((blocks, block, width), jnp.bfloat16),
            jax.ShapeDtypeStruct((blocks, LANES), jnp.float32),
            *both_halves,
        ],
        compiler_params=params(),
        cost_estimate=cost(2 * rows * width * DEPTH + 2 * slots * block * block * width, 4 * rows * width),
        name="smooth_and_gram",
    )(table_pairs, images, columns, weights)
    smoothed = smoothed.reshape(rows, width)

    energy, mine = lax.optimization_barrier((energy, mine))
    for distance in distances[1:-1]:
        mine = jnp.concatenate([mine, exchange(mine, distance)], axis=0)

    keep, give = pl.pallas_call(
        functools.partial(cross_kernel, blocks, block),
        in_specs=[smem] + [hbm] * 4 + [fixed] * 5,
        out_specs=[vmem, vmem],
        out_shape=both_halves,
        scratch_shapes=[
            pltpu.VMEM((2 * edge, width), jnp.bfloat16),
            pltpu.VMEM((8, 2 * edge), jnp.bfloat16),
            pltpu.VMEM(weights.shape, jnp.bfloat16),
            pltpu.VMEM((blocks, LANES), jnp.float32),
            pltpu.VMEM((2 * edge, width), jnp.bfloat16),
            pltpu.VMEM((2 * edge, width), jnp.bfloat16),
            pltpu.VMEM((units * block // 2, LANES), jnp.float32),
            pltpu.SemaphoreType.DMA((10,)),
        ],
        compiler_params=params(),
        cost_estimate=cost(4 * edge * width * DEPTH, 8 * edge * width),
        name="cross_grams",
    )(table_pairs, near_rows, far_rows, near_columns, far_columns, weights, energy, smoothed, keep, give)

    got = lax.ppermute(give, "pix", [(i, i ^ 1) for i in range(n_pix)])
    message = jax.ShapeDtypeStruct((slots + units * chips, share, LANES), jnp.bfloat16)
    own_rows = jax.ShapeDtypeStruct((slots + units * chips, share, LANES), jnp.float32)
    small = pltpu.CompilerParams(vmem_limit_bytes=16 * 1024 * 1024)
    own, *messages = pl.pallas_call(
        functools.partial(chip_kernel, slots, units),
        in_specs=[fixed, hbm],
        out_specs=[vmem] * chips,
        out_shape=[own_rows] + [message] * (chips - 1),
        scratch_shapes=[
            pltpu.VMEM(half_shape, jnp.bfloat16),
            pltpu.VMEM(half_shape, jnp.bfloat16),
            pltpu.SemaphoreType.DMA((2,)),
        ],
        compiler_params=small,
        name="chip_sums",
    )(keep, got)
    own, mine = lax.optimization_barrier((own, mine))
    other = exchange(mine, distances[-1])
    received = [
        lax.ppermute(m, "pix", [(i, i ^ (2 * (d + 1))) for i in range(n_pix)]) for d, m in enumerate(messages)
    ]

    scores = pl.pallas_call(
        functools.partial(score_kernel, blocks, place_of, pixel_count),
        in_specs=[smem] * 3 + [hbm] * (chips + 2),
        out_specs=vmem,
        out_shape=jax.ShapeDtypeStruct((slots, share, block), jnp.bfloat16),
        scratch_shapes=[
            pltpu.VMEM(own_rows.shape, jnp.float32),
            *[pltpu.VMEM(message.shape, jnp.bfloat16)] * (chips - 1),
            pltpu.VMEM((2 * mine.shape[0], block), jnp.bfloat16),
            pltpu.VMEM((units * block // 2, LANES), jnp.float32),
            pltpu.VMEM((slots, LANES), jnp.float32),
            pltpu.VMEM((slots, LANES), jnp.float32),
            pltpu.VMEM((slots, share, LANES), jnp.bfloat16),
            pltpu.SMEM((-(-block // part), slots), jnp.int32),
            pltpu.SemaphoreType.DMA((chips + 2,)),
        ],
        compiler_params=small,
        name="scores",
    )(table_pairs, live, rule_of_block, own, *received, mine, other)
    return (smoothed, scores)


def solution(mesh):
    return jax.shard_map(
        on_device,
        mesh=mesh,
        in_specs=(
            P("ion", "pix"),
            P(None, "pix"),
            P("ion", None),
            P("ion"),
            P(),
            P("ion", None, None),
        ),
        out_specs=(P("ion", "pix"), P("ion", "pix", None)),
        check_vma=False,
    )
```

```python
import functools

import jax
import jax.numpy as jnp
from jax import lax
from jax.experimental import pallas as pl
from jax.experimental.pallas import tpu as pltpu
from jax.sharding import PartitionSpec as P

REACH = 3
TAPS = 5
LANES = 128
HALF = LANES // 2
DEPTH = 2 * LANES
VMEM_BYTES = 58 * 1024 * 1024


def params():
    return pltpu.CompilerParams(vmem_limit_bytes=VMEM_BYTES)


def cost(flops, moved):
    return pl.CostEstimate(flops=flops, bytes_accessed=moved, transcendentals=0)


def whole(shape):
    return pl.BlockSpec(shape, lambda *_: (0,) * len(shape))


def fetch(sources, targets, sems):
    copies = [pltpu.make_async_copy(x, y, sems.at[k]) for k, (x, y) in enumerate(zip(sources, targets))]
    for copy in copies:
        copy.start()
    return copies


def smooth_rows(x_ref, halo, w_ref, store):
    rows, width = x_ref.shape
    tiles = width // LANES
    first = lax.broadcasted_iota(jnp.int32, (rows, LANES), 1) < HALF
    before, total, squares = None, None, None
    for j in range(-1, tiles):
        if j < 0:
            window = jnp.concatenate([halo, x_ref[:, :LANES]], axis=1)
        elif j == tiles - 1:
            window = jnp.concatenate([x_ref[:, j * LANES :], halo], axis=1)
        else:
            window = x_ref[:, j * LANES : (j + 2) * LANES]
        now = jnp.dot(window, w_ref[j + 1], preferred_element_type=jnp.float32)
        if j >= 0:
            values = jnp.where(first, before, now)
            store(j, values.astype(jnp.bfloat16))
            squares = values * values if j % 2 == 0 else squares + values * values
            if j % 2 == 1:
                total = squares if total is None else total + squares
        before = now
    return total


def row_sums(part):
    return jnp.sum(part.T, axis=0, keepdims=True)


def gram_of(left, right):
    return lax.dot_general(
        left, right, (((1,), (1,)), ((), ())), preferred_element_type=jnp.float32
    )


def by_core(gram, chips, core):
    parts = gram.reshape(chips, 2, gram.shape[0] // (2 * chips), gram.shape[1])
    even, odd = parts[:, 0].astype(jnp.bfloat16), parts[:, 1].astype(jnp.bfloat16)
    return jnp.where(core == 0, even, odd), jnp.where(core == 0, odd, even)


def write_weights(stencil_ref, out_ref):
    tiles = stencil_ref.shape[1] // LANES
    out_ref[...] = jnp.zeros_like(out_ref)
    k0, rows = 3 * LANES // 8, 5 * LANES // 4
    k = lax.broadcasted_iota(jnp.int32, (rows, LANES), 0) + k0
    lane = lax.broadcasted_iota(jnp.int32, (rows, LANES), 1)
    tap = k - lane + jnp.where(lane < HALF, 2 - LANES, 2)
    early = lax.broadcasted_iota(jnp.int32, (TAPS, LANES), 1) < HALF
    zeros = jnp.zeros((TAPS, LANES), jnp.float32)
    for j in range(-1, tiles):
        here = stencil_ref[:, j * LANES : (j + 1) * LANES] if j >= 0 else zeros
        after = stencil_ref[:, (j + 1) * LANES : (j + 2) * LANES] if j + 1 < tiles else zeros
        taps = jnp.where(early, after, here)
        w = jnp.zeros((rows, LANES), jnp.float32)
        for t in range(TAPS):
            w = jnp.where(tap == t, taps[t : t + 1, :], w)
        out_ref[j + 1, k0 : k0 + rows] = w.astype(jnp.bfloat16)


def cut_kernel(images_ref, stencil_ref, near_rows, far_rows, near_columns, far_columns, w_ref, bands, strips, sems):
    rows, width = images_ref.shape
    edge = near_rows.shape[0]
    odd = lax.axis_index("ion") % 2
    starts = [pl.multiple_of(k * (rows - edge), edge // REACH) for k in (1 - odd, odd)]
    reads = fetch(
        [images_ref.at[pl.ds(start, edge)] for start in starts]
        + [images_ref.at[:, pl.ds(start, LANES)] for start in (0, width - LANES)],
        [bands.at[0], bands.at[1], strips.at[0], strips.at[1]],
        sems,
    )
    writes = [
        pltpu.make_async_copy(bands.at[k], out, sems.at[4 + k]) for k, out in enumerate((near_rows, far_rows))
    ]
    write_weights(stencil_ref, w_ref)
    for read, write in zip(reads, writes):
        read.wait()
        write.start()
    row = lax.broadcasted_iota(jnp.int32, (8, LANES), 0)
    lane = lax.broadcasted_iota(jnp.int32, (8, LANES), 1)
    sides = []
    for k, shift in enumerate((0, LANES - 2)):
        reads[2 + k].wait()
        pick = (lane == row + shift).astype(jnp.bfloat16)
        sides.append(gram_of(pick, strips[k])[:2])
    head, tail = sides
    odd = lax.axis_index("pix") % 2 == 1
    near_columns[...] = jnp.where(odd, head, tail).astype(jnp.bfloat16)
    far_columns[...] = jnp.where(odd, tail, head).astype(jnp.bfloat16)
    for write in writes:
        write.wait()


def halo_tile(columns_ref):
    columns = columns_ref[...].astype(jnp.float32).T.astype(jnp.bfloat16)
    row = lax.broadcasted_iota(jnp.int32, (8, LANES), 0)
    lane = lax.broadcasted_iota(jnp.int32, (8, LANES), 1)
    place = (lane == row + jnp.where(row < 4, 0, LANES - 8)).astype(jnp.bfloat16)
    return jnp.dot(columns, place, preferred_element_type=jnp.float32).astype(jnp.bfloat16)


def main_kernel(steps, group, block, pairs_ref, x_ref, columns_ref, w_ref,
                out_hbm, energy_ref, keep_ref, give_ref, held, sems):
    step = pl.program_id(0)
    blocks = steps * group
    chips = keep_ref.shape[1]
    slots = pairs_ref.shape[1]

    def copy_out(k):
        here = pl.ds(k * group, group)
        return pltpu.make_async_copy(held.at[here], out_hbm.at[here], sems.at[k])

    @pl.when(step < steps)
    def smooth():
        def store(j, values):
            held[pl.ds(step * group, group), :, j * LANES : (j + 1) * LANES] = values.reshape(group, block, LANES)

        total = smooth_rows(x_ref, halo_tile(columns_ref), w_ref, store)
        for g in range(group):
            energy_ref[pl.ds(step * group + g, 1), :] = row_sums(total[g * block : (g + 1) * block, :])

    @pl.when(step == steps)
    def grams():
        for k in range(steps):
            copy_out(k).start()
        core = lax.axis_index("pix") % 2
        first = lax.axis_index("ion") * blocks

        def one(s, carry):
            a = pairs_ref[0, s] - first
            b = jnp.clip(pairs_ref[1, s] - first, 0, blocks - 1)
            keep_ref[s], give_ref[s] = by_core(gram_of(held[a], held[b]), chips, core)
            return carry

        lax.fori_loop(0, slots, one, 0, unroll=4)
        for k in range(steps):
            copy_out(k).wait()


def cross_kernel(blocks, block, pairs_ref, near_hbm, far_hbm, near_columns_hbm, far_columns_hbm, w_hbm, energy_hbm, smoothed_hbm, keep_hbm,
                 give_hbm, keep_ref, give_ref, x_ref, columns_ref, w_ref, energy_ref, own, other, table, sems):
    core = lax.axis_index("pix") % 2
    first_block = lax.axis_index("ion") * blocks
    slots = pairs_ref.shape[1]
    chips, share = keep_ref.shape[1:3]
    units = keep_ref.shape[0] - slots
    edge = REACH * block
    rows = blocks * block
    low, high = pl.ds(0, edge), pl.ds(edge, edge)
    odd = lax.axis_index("ion") % 2
    near, far = (pl.ds(pl.multiple_of(k * edge, edge), edge) for k in (1 - odd, odd))
    copies = fetch(
        (near_hbm, far_hbm, near_columns_hbm, far_columns_hbm, w_hbm, energy_hbm, smoothed_hbm.at[low],
         smoothed_hbm.at[pl.ds(rows - edge, edge)], keep_hbm, give_hbm),
        (x_ref.at[near], x_ref.at[far], columns_ref.at[:, near], columns_ref.at[:, far], w_ref, energy_ref, own.at[low],
         own.at[high], keep_ref, give_ref),
        sems,
    )
    for copy in copies[:6]:
        copy.wait()
    table[...] = jnp.zeros_like(table)
    table[REACH : REACH + blocks, :] = energy_ref[...]
    def store(j, values):
        other[:, j * LANES : (j + 1) * LANES] = values

    total = smooth_rows(x_ref, halo_tile(columns_ref), w_ref, store)
    for k in range(2 * REACH):
        row = k if k < REACH else k + blocks
        table[row : row + 1, :] = row_sums(total[k * block : (k + 1) * block, :])
    for copy in copies[6:]:
        copy.wait()

    shape = (units, chips, share, LANES)
    for ref in (keep_ref, give_ref):
        ref[slots:] = table[...].reshape(shape).astype(jnp.bfloat16)

    def one(s, carry):
        a, b = pairs_ref[0, s] - first_block, pairs_ref[1, s] - first_block

        @pl.when((b < 0) | (b >= blocks))
        def crossing():
            side = (b >= 0).astype(jnp.int32)
            a_row = pl.multiple_of((a - side * (blocks - 2 * REACH)) * block, block)
            b_row = pl.multiple_of((b + REACH - side * blocks) * block, block)
            gram = gram_of(own[pl.ds(a_row, block), :], other[pl.ds(b_row, block), :])
            keep_ref[s], give_ref[s] = by_core(gram, chips, core)

        return carry

    lax.fori_loop(0, slots, one, 0)


def chip_kernel(slots, units, keep_hbm, got_hbm, own_ref, *refs):
    out_refs, (keep_ref, got_ref, sems) = refs[:-3], refs[-3:]
    chip = lax.axis_index("pix") // 2
    chips, share = keep_ref.shape[1:3]
    shape = (units * chips, share, LANES)
    for copy in fetch((keep_hbm, got_hbm), (keep_ref, got_ref), sems):
        copy.wait()
    energies = (keep_ref[slots:].astype(jnp.float32) + got_ref[slots:].astype(jnp.float32)).reshape(shape)
    for d in range(chips):
        total = keep_ref[:slots, chip ^ d].astype(jnp.float32) + got_ref[:slots, chip ^ d].astype(jnp.float32)
        if d == 0:
            own_ref[:slots] = total
            own_ref[slots:] = energies
        else:
            out = out_refs[d - 1]
            out[:slots] = total.astype(jnp.bfloat16)
            out[slots:] = energies.astype(jnp.bfloat16)


def score_kernel(blocks, place_of, pixel_count, pairs_ref, live_ref, rules_ref, *refs):
    chips = (len(refs) - 9) // 2
    sources, out_ref, own_ref = refs[: chips + 2], refs[chips + 2], refs[chips + 3]
    got_refs, (table_ref, inverse, left, right, coloc, place, sems) = refs[chips + 4 : -7], refs[-7:]
    slots, share, block = out_ref.shape
    half = table_ref.shape[0] // 2
    targets = (own_ref, *got_refs, table_ref.at[pl.ds(0, half)], table_ref.at[pl.ds(half, half)])
    copies = fetch(sources, targets, sems)
    pix, first = lax.axis_index("pix"), lax.axis_index("ion") * blocks
    pieces = place.shape[0]
    depth = block // pieces

    def find(s, carry):
        for k, at in enumerate(place_of(rules_ref[pairs_ref[1, s]])):
            place[k, s] = at
        return carry

    lax.fori_loop(0, slots, find, 0)
    for copy in copies[:-2]:
        copy.wait()
    gram = own_ref[:slots]
    energies = own_ref[slots:]
    for got in got_refs:
        gram = gram + got[:slots].astype(jnp.float32)
        energies = energies + got[slots:].astype(jnp.float32)
    inverse[...] = (1.0 / jnp.sqrt(energies / pixel_count + 1e-06)).reshape(inverse.shape)

    def pick(s, carry):
        left[pl.ds(s, 1), :] = inverse[pl.ds(pairs_ref[0, s] - first + REACH, 1), :]
        right[pl.ds(s, 1), :] = inverse[pl.ds(pairs_ref[1, s] - first + REACH, 1), :]
        return carry

    lax.fori_loop(0, slots, pick, 0, unroll=8)
    lane = lax.broadcasted_iota(jnp.int32, (1, share, LANES), 2)
    mine = lane == lax.broadcasted_iota(jnp.int32, (1, share, LANES), 1) + pix * share
    inv_a = jnp.sum(jnp.where(mine, left[...][:, None, :], 0.0), axis=2, keepdims=True)
    coloc[...] = (gram * inv_a * right[...][:, None, :] / pixel_count).astype(jnp.bfloat16)
    for copy in copies[-2:]:
        copy.wait()

    def one(s, carry):
        scores = jnp.zeros((share, block), jnp.float32)
        for k in range(pieces):
            matrix = table_ref[pl.ds(pl.multiple_of(place[k, s], depth), depth), :]
            part = coloc[s, :, k * depth : (k + 1) * depth]
            scores = scores + jnp.dot(part, matrix, preferred_element_type=jnp.float32)
        out_ref[s] = jnp.where(s < live_ref[0], scores, 0.0).astype(jnp.bfloat16)
        return carry

    lax.fori_loop(0, slots, one, 0, unroll=slots)


def on_device(images, stencil, pairs, live, rule_of_block, adduct):
    rows, width = images.shape
    rules_here, block, _ = adduct.shape
    blocks = rows // block
    slots = pairs.shape[0]
    n_pix, n_ion = lax.axis_size("pix"), lax.axis_size("ion")
    pix, ion = lax.axis_index("pix"), lax.axis_index("ion")
    pixel_count = width * n_pix
    chips, share = n_pix // 2, block // n_pix
    core, chip = pix % 2, pix // 2
    edge = REACH * block

    def swapped(axis, size, near, far):
        pairs_of = [[(i, i + 1) for i in range(first, size - 1, 2)] for first in (0, 1)]
        return [
            lax.ppermute(value, axis, both + [(j, i) for i, j in both]) for value, both in zip((near, far), pairs_of)
        ]

    vmem = pl.BlockSpec(memory_space=pltpu.VMEM)
    smem = pl.BlockSpec(memory_space=pltpu.SMEM)
    hbm = pl.BlockSpec(memory_space=pl.ANY)
    fixed = pl.BlockSpec(memory_space=pltpu.HBM)

    part = rules_here * block // n_pix
    mine = lax.dynamic_slice_in_dim(adduct.reshape(rules_here * block, block), pix * part, part, 0)
    turns = [lax.ppermute(mine, "ion", [(i, i ^ d) for i in range(n_ion)]) for d in range(1, n_ion)]

    edge_rows = jax.ShapeDtypeStruct((edge, width), images.dtype)
    edge_columns = jax.ShapeDtypeStruct((2, rows), images.dtype)
    near_rows, far_rows, near, far, weights = pl.pallas_call(
        cut_kernel,
        in_specs=[hbm, vmem],
        out_specs=[hbm, hbm, vmem, vmem, vmem],
        out_shape=[
            edge_rows,
            edge_rows,
            edge_columns,
            edge_columns,
            jax.ShapeDtypeStruct((width // LANES + 1, DEPTH, LANES), jnp.bfloat16),
        ],
        scratch_shapes=[
            pltpu.VMEM((2, edge, width), images.dtype),
            pltpu.VMEM((2, rows, LANES), images.dtype),
            pltpu.SemaphoreType.DMA((6,)),
        ],
        compiler_params=params(),
        cost_estimate=cost(0, 8 * edge * width),
        name="cut_edges",
    )(images, stencil)
    near_rows, far_rows = swapped("ion", n_ion, near_rows, far_rows)
    near, far, *turns = lax.optimization_barrier((near, far, *turns))
    mine = jnp.concatenate([mine, *turns], axis=0)
    near, far, mine = lax.optimization_barrier((near, far, mine))
    near, far = swapped("pix", n_pix, near, far)
    odd = pix % 2 == 1
    after, before = jnp.where(odd, far, near), jnp.where(odd, near, far)
    columns = jnp.concatenate([after, jnp.zeros((4, rows), images.dtype), before], axis=0)
    first, last = columns[:, :edge], columns[:, rows - edge :]
    odd = ion % 2 == 1
    near_columns, far_columns = swapped("ion", n_ion, jnp.where(odd, first, last), jnp.where(odd, last, first))

    distances = [n_pix >> k for k in range(1, n_pix.bit_length())]

    def exchange(value, distance):
        return lax.ppermute(value, "pix", [(i, i ^ distance) for i in range(n_pix)])

    for distance in distances[:-1]:
        mine = jnp.concatenate([mine, exchange(mine, distance)], axis=0)

    def place_of(rule):
        row = (rule & (rules_here - 1)) * block
        turn = (rule >> (rules_here.bit_length() - 1)) ^ lax.axis_index("ion")
        pieces = []
        for offset in range(0, block, min(part, block)):
            share_of = ((row + offset) >> (part.bit_length() - 1)) ^ lax.axis_index("pix")
            at = turn * part + ((row + offset) & (part - 1))
            for k, distance in enumerate(distances):
                at = at + jnp.where((share_of & distance) != 0, n_ion * part << k, 0)
            pieces.append(at)
        return pieces

    table_pairs = pairs.T
    group = next(g for g in (8, 5, 4, 2, 1) if blocks % g == 0)
    steps = blocks // group
    units = -(-2 * (blocks + 2 * REACH) // block)
    half = (chips, share, LANES)
    half_shape = (slots + units, *half)
    both_halves = [jax.ShapeDtypeStruct(half_shape, jnp.bfloat16)] * 2

    def rows_at(columns):
        return pl.BlockSpec((group * block, columns), lambda i, *_: (jnp.minimum(i, steps - 1), 0))

    smoothed, energy, keep, give = pl.pallas_call(
        functools.partial(main_kernel, steps, group, block),
        grid_spec=pltpu.PrefetchScalarGridSpec(
            num_scalar_prefetch=1,
            grid=(steps + 1,),
            in_specs=[
                rows_at(width),
                pl.BlockSpec((8, group * block), lambda i, *_: (0, jnp.minimum(i, steps - 1))),
                whole(weights.shape),
            ],
            out_specs=[hbm, whole((blocks, LANES)), whole(half_shape), whole(half_shape)],
            scratch_shapes=[pltpu.VMEM((blocks, block, width), jnp.bfloat16), pltpu.SemaphoreType.DMA((steps,))],
        ),
        out_shape=[
            jax.ShapeDtypeStruct((blocks, block, width), jnp.bfloat16),
            jax.ShapeDtypeStruct((blocks, LANES), jnp.float32),
            *both_halves,
        ],
        compiler_params=params(),
        cost_estimate=cost(2 * rows * width * DEPTH + 2 * slots * block * block * width, 4 * rows * width),
        name="smooth_and_gram",
    )(table_pairs, images, columns, weights)
    smoothed = smoothed.reshape(rows, width)


    keep, give = pl.pallas_call(
        functools.partial(cross_kernel, blocks, block),
        in_specs=[smem] + [hbm] * 4 + [fixed] * 5,
        out_specs=[vmem, vmem],
        out_shape=both_halves,
        scratch_shapes=[
            pltpu.VMEM((2 * edge, width), jnp.bfloat16),
            pltpu.VMEM((8, 2 * edge), jnp.bfloat16),
            pltpu.VMEM(weights.shape, jnp.bfloat16),
            pltpu.VMEM((blocks, LANES), jnp.float32),
            pltpu.VMEM((2 * edge, width), jnp.bfloat16),
            pltpu.VMEM((2 * edge, width), jnp.bfloat16),
            pltpu.VMEM((units * block // 2, LANES), jnp.float32),
            pltpu.SemaphoreType.DMA((10,)),
        ],
        compiler_params=params(),
        cost_estimate=cost(4 * edge * width * DEPTH, 8 * edge * width),
        name="cross_grams",
    )(table_pairs, near_rows, far_rows, near_columns, far_columns, weights, energy, smoothed, keep, give)

    got = lax.ppermute(give, "pix", [(i, i ^ 1) for i in range(n_pix)])
    message = jax.ShapeDtypeStruct((slots + units * chips, share, LANES), jnp.bfloat16)
    own_rows = jax.ShapeDtypeStruct((slots + units * chips, share, LANES), jnp.float32)
    small = pltpu.CompilerParams(vmem_limit_bytes=16 * 1024 * 1024)
    own, *messages = pl.pallas_call(
        functools.partial(chip_kernel, slots, units),
        in_specs=[fixed, hbm],
        out_specs=[vmem] * chips,
        out_shape=[own_rows] + [message] * (chips - 1),
        scratch_shapes=[
            pltpu.VMEM(half_shape, jnp.bfloat16),
            pltpu.VMEM(half_shape, jnp.bfloat16),
            pltpu.SemaphoreType.DMA((2,)),
        ],
        compiler_params=small,
        name="chip_sums",
    )(keep, got)
    own, mine = lax.optimization_barrier((own, mine))
    other = exchange(mine, distances[-1])
    received = [
        lax.ppermute(m, "pix", [(i, i ^ (2 * (d + 1))) for i in range(n_pix)]) for d, m in enumerate(messages)
    ]

    scores = pl.pallas_call(
        functools.partial(score_kernel, blocks, place_of, pixel_count),
        in_specs=[smem] * 3 + [hbm] * (chips + 2),
        out_specs=vmem,
        out_shape=jax.ShapeDtypeStruct((slots, share, block), jnp.bfloat16),
        scratch_shapes=[
            pltpu.VMEM(own_rows.shape, jnp.float32),
            *[pltpu.VMEM(message.shape, jnp.bfloat16)] * (chips - 1),
            pltpu.VMEM((2 * mine.shape[0], block), jnp.bfloat16),
            pltpu.VMEM((units * block // 2, LANES), jnp.float32),
            pltpu.VMEM((slots, LANES), jnp.float32),
            pltpu.VMEM((slots, LANES), jnp.float32),
            pltpu.VMEM((slots, share, LANES), jnp.bfloat16),
            pltpu.SMEM((-(-block // part), slots), jnp.int32),
            pltpu.SemaphoreType.DMA((chips + 2,)),
        ],
        compiler_params=small,
        name="scores",
    )(table_pairs, live, rule_of_block, own, *received, mine, other)
    return (smoothed, scores)


def solution(mesh):
    return jax.shard_map(
        on_device,
        mesh=mesh,
        in_specs=(
            P("ion", "pix"),
            P(None, "pix"),
            P("ion", None),
            P("ion"),
            P(),
            P("ion", None, None),
        ),
        out_specs=(P("ion", "pix"), P("ion", "pix", None)),
        check_vma=False,
    )
```

```python
import functools

import jax
import jax.numpy as jnp
from jax import lax
from jax.experimental import pallas as pl
from jax.experimental.pallas import tpu as pltpu
from jax.sharding import PartitionSpec as P

REACH = 3
TAPS = 5
LANES = 128
HALF = LANES // 2
DEPTH = 2 * LANES
VMEM_BYTES = 58 * 1024 * 1024
MAIN_VMEM_BYTES = 125 * 1024 * 512


def params():
    return pltpu.CompilerParams(vmem_limit_bytes=VMEM_BYTES)


def cost(flops, moved):
    return pl.CostEstimate(flops=flops, bytes_accessed=moved, transcendentals=0)


def whole(shape):
    return pl.BlockSpec(shape, lambda *_: (0,) * len(shape))


def fetch(sources, targets, sems):
    copies = [pltpu.make_async_copy(x, y, sems.at[k]) for k, (x, y) in enumerate(zip(sources, targets))]
    for copy in copies:
        copy.start()
    return copies


def smooth_rows(x_ref, halo, w_ref, store):
    rows, width = x_ref.shape
    tiles = width // LANES
    first = lax.broadcasted_iota(jnp.int32, (rows, LANES), 1) < HALF
    before, total, squares = None, None, None
    for j in range(-1, tiles):
        if j < 0:
            window = jnp.concatenate([halo, x_ref[:, :LANES]], axis=1)
        elif j == tiles - 1:
            window = jnp.concatenate([x_ref[:, j * LANES :], halo], axis=1)
        else:
            window = x_ref[:, j * LANES : (j + 2) * LANES]
        now = jnp.dot(window, w_ref[j + 1], preferred_element_type=jnp.float32)
        if j >= 0:
            values = jnp.where(first, before, now)
            store(j, values.astype(jnp.bfloat16))
            squares = values * values if j % 2 == 0 else squares + values * values
            if j % 2 == 1:
                total = squares if total is None else total + squares
        before = now
    return total


def row_sums(part):
    return jnp.sum(part.T, axis=0, keepdims=True)


def gram_of(left, right):
    return lax.dot_general(
        left, right, (((1,), (1,)), ((), ())), preferred_element_type=jnp.float32
    )


def by_core(gram, chips, core):
    parts = gram.reshape(chips, 2, gram.shape[0] // (2 * chips), gram.shape[1])
    even, odd = parts[:, 0].astype(jnp.bfloat16), parts[:, 1].astype(jnp.bfloat16)
    return jnp.where(core == 0, even, odd), jnp.where(core == 0, odd, even)


def write_weights(stencil_ref, out_ref):
    tiles = stencil_ref.shape[1] // LANES
    out_ref[...] = jnp.zeros_like(out_ref)
    k0, rows = 3 * LANES // 8, 5 * LANES // 4
    k = lax.broadcasted_iota(jnp.int32, (rows, LANES), 0) + k0
    lane = lax.broadcasted_iota(jnp.int32, (rows, LANES), 1)
    tap = k - lane + jnp.where(lane < HALF, 2 - LANES, 2)
    early = lax.broadcasted_iota(jnp.int32, (TAPS, LANES), 1) < HALF
    zeros = jnp.zeros((TAPS, LANES), jnp.float32)
    for j in range(-1, tiles):
        here = stencil_ref[:, j * LANES : (j + 1) * LANES] if j >= 0 else zeros
        after = stencil_ref[:, (j + 1) * LANES : (j + 2) * LANES] if j + 1 < tiles else zeros
        taps = jnp.where(early, after, here)
        w = jnp.zeros((rows, LANES), jnp.float32)
        for t in range(TAPS):
            w = jnp.where(tap == t, taps[t : t + 1, :], w)
        out_ref[j + 1, k0 : k0 + rows] = w.astype(jnp.bfloat16)


def cut_kernel(images_ref, stencil_ref, near_rows, far_rows, near_columns, far_columns, w_ref, bands, strips, sems):
    rows, width = images_ref.shape
    edge = near_rows.shape[0]
    odd = lax.axis_index("ion") % 2
    starts = [pl.multiple_of(k * (rows - edge), edge // REACH) for k in (1 - odd, odd)]
    reads = fetch(
        [images_ref.at[pl.ds(start, edge)] for start in starts]
        + [images_ref.at[:, pl.ds(start, LANES)] for start in (0, width - LANES)],
        [bands.at[0], bands.at[1], strips.at[0], strips.at[1]],
        sems,
    )
    writes = [
        pltpu.make_async_copy(bands.at[k], out, sems.at[4 + k]) for k, out in enumerate((near_rows, far_rows))
    ]
    write_weights(stencil_ref, w_ref)
    for read, write in zip(reads, writes):
        read.wait()
        write.start()
    row = lax.broadcasted_iota(jnp.int32, (8, LANES), 0)
    lane = lax.broadcasted_iota(jnp.int32, (8, LANES), 1)
    sides = []
    for k, shift in enumerate((0, LANES - 2)):
        reads[2 + k].wait()
        pick = (lane == row + shift).astype(jnp.bfloat16)
        sides.append(gram_of(pick, strips[k])[:2])
    head, tail = sides
    odd = lax.axis_index("pix") % 2 == 1
    near_columns[...] = jnp.where(odd, head, tail).astype(jnp.bfloat16)
    far_columns[...] = jnp.where(odd, tail, head).astype(jnp.bfloat16)
    for write in writes:
        write.wait()


def halo_tile(columns_ref):
    columns = columns_ref[...].astype(jnp.float32).T.astype(jnp.bfloat16)
    row = lax.broadcasted_iota(jnp.int32, (8, LANES), 0)
    lane = lax.broadcasted_iota(jnp.int32, (8, LANES), 1)
    place = (lane == row + jnp.where(row < 4, 0, LANES - 8)).astype(jnp.bfloat16)
    return jnp.dot(columns, place, preferred_element_type=jnp.float32).astype(jnp.bfloat16)


def main_kernel(steps, group, block, pairs_ref, x_ref, columns_ref, w_ref,
                out_hbm, energy_ref, keep_ref, give_ref, held, sems):
    step = pl.program_id(0)
    blocks = steps * group
    chips = keep_ref.shape[1]
    slots = pairs_ref.shape[1]

    def copy_out(k):
        here = pl.ds(k * group, group)
        return pltpu.make_async_copy(held.at[here], out_hbm.at[here], sems.at[k])

    @pl.when(step < steps)
    def smooth():
        def store(j, values):
            held[pl.ds(step * group, group), :, j * LANES : (j + 1) * LANES] = values.reshape(group, block, LANES)

        total = smooth_rows(x_ref, halo_tile(columns_ref), w_ref, store)
        for g in range(group):
            energy_ref[pl.ds(step * group + g, 1), :] = row_sums(total[g * block : (g + 1) * block, :])

    @pl.when(step == steps)
    def grams():
        for k in range(steps):
            copy_out(k).start()
        core = lax.axis_index("pix") % 2
        first = lax.axis_index("ion") * blocks

        def one(s, carry):
            a = pairs_ref[0, s] - first
            b = jnp.clip(pairs_ref[1, s] - first, 0, blocks - 1)
            keep_ref[s], give_ref[s] = by_core(gram_of(held[a], held[b]), chips, core)
            return carry

        lax.fori_loop(0, slots, one, 0, unroll=4)
        for k in range(steps):
            copy_out(k).wait()


def cross_kernel(blocks, block, pairs_ref, near_hbm, far_hbm, near_columns_hbm, far_columns_hbm, w_hbm, energy_hbm, smoothed_hbm, keep_hbm,
                 give_hbm, keep_ref, give_ref, x_ref, columns_ref, w_ref, energy_ref, own, other, table, sems):
    core = lax.axis_index("pix") % 2
    first_block = lax.axis_index("ion") * blocks
    slots = pairs_ref.shape[1]
    chips, share = keep_ref.shape[1:3]
    units = keep_ref.shape[0] - slots
    edge = REACH * block
    rows = blocks * block
    low, high = pl.ds(0, edge), pl.ds(edge, edge)
    odd = lax.axis_index("ion") % 2
    near, far = (pl.ds(pl.multiple_of(k * edge, edge), edge) for k in (1 - odd, odd))
    copies = fetch(
        (near_hbm, far_hbm, near_columns_hbm, far_columns_hbm, w_hbm, energy_hbm, smoothed_hbm.at[low],
         smoothed_hbm.at[pl.ds(rows - edge, edge)], keep_hbm, give_hbm),
        (x_ref.at[near], x_ref.at[far], columns_ref.at[:, near], columns_ref.at[:, far], w_ref, energy_ref, own.at[low],
         own.at[high], keep_ref, give_ref),
        sems,
    )
    for copy in copies[:6]:
        copy.wait()
    table[...] = jnp.zeros_like(table)
    table[REACH : REACH + blocks, :] = energy_ref[...]
    def store(j, values):
        other[:, j * LANES : (j + 1) * LANES] = values

    total = smooth_rows(x_ref, halo_tile(columns_ref), w_ref, store)
    for k in range(2 * REACH):
        row = k if k < REACH else k + blocks
        table[row : row + 1, :] = row_sums(total[k * block : (k + 1) * block, :])
    for copy in copies[6:]:
        copy.wait()

    shape = (units, chips, share, LANES)
    for ref in (keep_ref, give_ref):
        ref[slots:] = table[...].reshape(shape).astype(jnp.bfloat16)

    def one(s, carry):
        a, b = pairs_ref[0, s] - first_block, pairs_ref[1, s] - first_block

        @pl.when((b < 0) | (b >= blocks))
        def crossing():
            side = (b >= 0).astype(jnp.int32)
            a_row = pl.multiple_of((a - side * (blocks - 2 * REACH)) * block, block)
            b_row = pl.multiple_of((b + REACH - side * blocks) * block, block)
            gram = gram_of(own[pl.ds(a_row, block), :], other[pl.ds(b_row, block), :])
            keep_ref[s], give_ref[s] = by_core(gram, chips, core)

        return carry

    lax.fori_loop(0, slots, one, 0)


def chip_kernel(slots, units, keep_hbm, got_hbm, own_ref, *refs):
    out_refs, (keep_ref, got_ref, sems) = refs[:-3], refs[-3:]
    chip = lax.axis_index("pix") // 2
    chips, share = keep_ref.shape[1:3]
    shape = (units * chips, share, LANES)
    for copy in fetch((keep_hbm, got_hbm), (keep_ref, got_ref), sems):
        copy.wait()
    energies = (keep_ref[slots:].astype(jnp.float32) + got_ref[slots:].astype(jnp.float32)).reshape(shape)
    for d in range(chips):
        total = keep_ref[:slots, chip ^ d].astype(jnp.float32) + got_ref[:slots, chip ^ d].astype(jnp.float32)
        if d == 0:
            own_ref[:slots] = total
            own_ref[slots:] = energies
        else:
            out = out_refs[d - 1]
            out[:slots] = total.astype(jnp.bfloat16)
            out[slots:] = energies.astype(jnp.bfloat16)


def score_kernel(blocks, place_of, pixel_count, pairs_ref, live_ref, rules_ref, *refs):
    chips = (len(refs) - 9) // 2
    sources, out_ref, own_ref = refs[: chips + 2], refs[chips + 2], refs[chips + 3]
    got_refs, (table_ref, inverse, left, right, coloc, place, sems) = refs[chips + 4 : -7], refs[-7:]
    slots, share, block = out_ref.shape
    half = table_ref.shape[0] // 2
    targets = (own_ref, *got_refs, table_ref.at[pl.ds(0, half)], table_ref.at[pl.ds(half, half)])
    copies = fetch(sources, targets, sems)
    pix, first = lax.axis_index("pix"), lax.axis_index("ion") * blocks
    pieces = place.shape[0]
    depth = block // pieces

    def find(s, carry):
        for k, at in enumerate(place_of(rules_ref[pairs_ref[1, s]])):
            place[k, s] = at
        return carry

    lax.fori_loop(0, slots, find, 0)
    for copy in copies[:-2]:
        copy.wait()
    gram = own_ref[:slots]
    energies = own_ref[slots:]
    for got in got_refs:
        gram = gram + got[:slots].astype(jnp.float32)
        energies = energies + got[slots:].astype(jnp.float32)
    inverse[...] = (1.0 / jnp.sqrt(energies / pixel_count + 1e-06)).reshape(inverse.shape)

    def pick(s, carry):
        left[pl.ds(s, 1), :] = inverse[pl.ds(pairs_ref[0, s] - first + REACH, 1), :]
        right[pl.ds(s, 1), :] = inverse[pl.ds(pairs_ref[1, s] - first + REACH, 1), :]
        return carry

    lax.fori_loop(0, slots, pick, 0, unroll=8)
    lane = lax.broadcasted_iota(jnp.int32, (1, share, LANES), 2)
    mine = lane == lax.broadcasted_iota(jnp.int32, (1, share, LANES), 1) + pix * share
    inv_a = jnp.sum(jnp.where(mine, left[...][:, None, :], 0.0), axis=2, keepdims=True)
    coloc[...] = (gram * inv_a * right[...][:, None, :] / pixel_count).astype(jnp.bfloat16)
    for copy in copies[-2:]:
        copy.wait()

    def matrix(s):
        rows = [table_ref[pl.ds(pl.multiple_of(place[k, s], depth), depth), :] for k in range(pieces)]
        return jnp.concatenate(rows, axis=0)

    for s in range(0, slots, 2):
        both = jnp.concatenate([matrix(s), matrix(s + 1)], axis=1)
        rows = coloc[s : s + 2].reshape(2 * share, block)
        scores = jnp.dot(rows, both, preferred_element_type=jnp.float32)
        for k in range(2):
            part = scores[k * share : (k + 1) * share, k * block : (k + 1) * block]
            out_ref[s + k] = jnp.where(s + k < live_ref[0], part, 0.0).astype(jnp.bfloat16)


def on_device(images, stencil, pairs, live, rule_of_block, adduct):
    rows, width = images.shape
    rules_here, block, _ = adduct.shape
    blocks = rows // block
    slots = pairs.shape[0]
    n_pix, n_ion = lax.axis_size("pix"), lax.axis_size("ion")
    pix, ion = lax.axis_index("pix"), lax.axis_index("ion")
    pixel_count = width * n_pix
    chips, share = n_pix // 2, block // n_pix
    core, chip = pix % 2, pix // 2
    edge = REACH * block

    def swapped(axis, size, near, far):
        pairs_of = [[(i, i + 1) for i in range(first, size - 1, 2)] for first in (0, 1)]
        return [
            lax.ppermute(value, axis, both + [(j, i) for i, j in both]) for value, both in zip((near, far), pairs_of)
        ]

    vmem = pl.BlockSpec(memory_space=pltpu.VMEM)
    smem = pl.BlockSpec(memory_space=pltpu.SMEM)
    hbm = pl.BlockSpec(memory_space=pl.ANY)
    fixed = pl.BlockSpec(memory_space=pltpu.HBM)

    part = rules_here * block // n_pix
    mine = lax.dynamic_slice_in_dim(adduct.reshape(rules_here * block, block), pix * part, part, 0)
    turns = [lax.ppermute(mine, "ion", [(i, i ^ d) for i in range(n_ion)]) for d in range(1, n_ion)]

    edge_rows = jax.ShapeDtypeStruct((edge, width), images.dtype)
    edge_columns = jax.ShapeDtypeStruct((2, rows), images.dtype)
    near_rows, far_rows, near, far, weights = pl.pallas_call(
        cut_kernel,
        in_specs=[hbm, vmem],
        out_specs=[hbm, hbm, vmem, vmem, vmem],
        out_shape=[
            edge_rows,
            edge_rows,
            edge_columns,
            edge_columns,
            jax.ShapeDtypeStruct((width // LANES + 1, DEPTH, LANES), jnp.bfloat16),
        ],
        scratch_shapes=[
            pltpu.VMEM((2, edge, width), images.dtype),
            pltpu.VMEM((2, rows, LANES), images.dtype),
            pltpu.SemaphoreType.DMA((6,)),
        ],
        compiler_params=params(),
        cost_estimate=cost(0, 8 * edge * width),
        name="cut_edges",
    )(images, stencil)
    near_rows, far_rows = swapped("ion", n_ion, near_rows, far_rows)
    near, far, *turns = lax.optimization_barrier((near, far, *turns))
    mine = jnp.concatenate([mine, *turns], axis=0)
    near, far, mine = lax.optimization_barrier((near, far, mine))
    near, far = swapped("pix", n_pix, near, far)
    odd = pix % 2 == 1
    after, before = jnp.where(odd, far, near), jnp.where(odd, near, far)
    columns = jnp.concatenate([after, jnp.zeros((4, rows), images.dtype), before], axis=0)
    first, last = columns[:, :edge], columns[:, rows - edge :]
    odd = ion % 2 == 1
    near_columns, far_columns = swapped("ion", n_ion, jnp.where(odd, first, last), jnp.where(odd, last, first))

    distances = [n_pix >> k for k in range(1, n_pix.bit_length())]

    def exchange(value, distance):
        return lax.ppermute(value, "pix", [(i, i ^ distance) for i in range(n_pix)])

    mine = jnp.concatenate([mine, exchange(mine, distances[0])], axis=0)

    def place_of(rule):
        row = (rule & (rules_here - 1)) * block
        turn = (rule >> (rules_here.bit_length() - 1)) ^ lax.axis_index("ion")
        pieces = []
        for offset in range(0, block, min(part, block)):
            share_of = ((row + offset) >> (part.bit_length() - 1)) ^ lax.axis_index("pix")
            at = turn * part + ((row + offset) & (part - 1))
            for k, distance in enumerate(distances):
                at = at + jnp.where((share_of & distance) != 0, n_ion * part << k, 0)
            pieces.append(at)
        return pieces

    table_pairs = pairs.T
    group = next(g for g in (8, 5, 4, 2, 1) if blocks % g == 0)
    steps = blocks // group
    units = -(-2 * (blocks + 2 * REACH) // block)
    half = (chips, share, LANES)
    half_shape = (slots + units, *half)
    both_halves = [jax.ShapeDtypeStruct(half_shape, jnp.bfloat16)] * 2

    def rows_at(columns):
        return pl.BlockSpec((group * block, columns), lambda i, *_: (jnp.minimum(i, steps - 1), 0))

    smoothed, energy, keep, give = pl.pallas_call(
        functools.partial(main_kernel, steps, group, block),
        grid_spec=pltpu.PrefetchScalarGridSpec(
            num_scalar_prefetch=1,
            grid=(steps + 1,),
            in_specs=[
                rows_at(width),
                pl.BlockSpec((8, group * block), lambda i, *_: (0, jnp.minimum(i, steps - 1))),
                whole(weights.shape),
            ],
            out_specs=[hbm, whole((blocks, LANES)), whole(half_shape), whole(half_shape)],
            scratch_shapes=[pltpu.VMEM((blocks, block, width), jnp.bfloat16), pltpu.SemaphoreType.DMA((steps,))],
        ),
        out_shape=[
            jax.ShapeDtypeStruct((blocks, block, width), jnp.bfloat16),
            jax.ShapeDtypeStruct((blocks, LANES), jnp.float32),
            *both_halves,
        ],
        compiler_params=pltpu.CompilerParams(vmem_limit_bytes=MAIN_VMEM_BYTES),
        cost_estimate=cost(2 * rows * width * DEPTH + 2 * slots * block * block * width, 4 * rows * width),
        name="smooth_and_gram",
    )(table_pairs, images, columns, weights)
    smoothed = smoothed.reshape(rows, width)
    received = (near_rows, far_rows, near_columns, far_columns)
    energy, mine, *received = lax.optimization_barrier((energy, mine, *received))
    for distance in distances[1:-1]:
        mine = jnp.concatenate([mine, exchange(mine, distance)], axis=0)

    keep, give = pl.pallas_call(
        functools.partial(cross_kernel, blocks, block),
        in_specs=[smem] + [hbm] * 4 + [fixed] * 5,
        out_specs=[vmem, vmem],
        out_shape=both_halves,
        scratch_shapes=[
            pltpu.VMEM((2 * edge, width), jnp.bfloat16),
            pltpu.VMEM((8, 2 * edge), jnp.bfloat16),
            pltpu.VMEM(weights.shape, jnp.bfloat16),
            pltpu.VMEM((blocks, LANES), jnp.float32),
            pltpu.VMEM((2 * edge, width), jnp.bfloat16),
            pltpu.VMEM((2 * edge, width), jnp.bfloat16),
            pltpu.VMEM((units * block // 2, LANES), jnp.float32),
            pltpu.SemaphoreType.DMA((10,)),
        ],
        compiler_params=params(),
        cost_estimate=cost(4 * edge * width * DEPTH, 8 * edge * width),
        name="cross_grams",
    )(table_pairs, *received, weights, energy, smoothed, keep, give)

    got = lax.ppermute(give, "pix", [(i, i ^ 1) for i in range(n_pix)])
    message = jax.ShapeDtypeStruct((slots + units * chips, share, LANES), jnp.bfloat16)
    own_rows = jax.ShapeDtypeStruct((slots + units * chips, share, LANES), jnp.float32)
    small = pltpu.CompilerParams(vmem_limit_bytes=16 * 1024 * 1024)
    own, *messages = pl.pallas_call(
        functools.partial(chip_kernel, slots, units),
        in_specs=[fixed, hbm],
        out_specs=[vmem] * chips,
        out_shape=[own_rows] + [message] * (chips - 1),
        scratch_shapes=[
            pltpu.VMEM(half_shape, jnp.bfloat16),
            pltpu.VMEM(half_shape, jnp.bfloat16),
            pltpu.SemaphoreType.DMA((2,)),
        ],
        compiler_params=small,
        name="chip_sums",
    )(keep, got)
    own, mine = lax.optimization_barrier((own, mine))
    other = exchange(mine, distances[-1])
    received = [
        lax.ppermute(m, "pix", [(i, i ^ (2 * (d + 1))) for i in range(n_pix)]) for d, m in enumerate(messages)
    ]

    scores = pl.pallas_call(
        functools.partial(score_kernel, blocks, place_of, pixel_count),
        in_specs=[smem] * 3 + [hbm] * (chips + 2),
        out_specs=vmem,
        out_shape=jax.ShapeDtypeStruct((slots, share, block), jnp.bfloat16),
        scratch_shapes=[
            pltpu.VMEM(own_rows.shape, jnp.float32),
            *[pltpu.VMEM(message.shape, jnp.bfloat16)] * (chips - 1),
            pltpu.VMEM((2 * mine.shape[0], block), jnp.bfloat16),
            pltpu.VMEM((units * block // 2, LANES), jnp.float32),
            pltpu.VMEM((slots, LANES), jnp.float32),
            pltpu.VMEM((slots, LANES), jnp.float32),
            pltpu.VMEM((slots, share, LANES), jnp.bfloat16),
            pltpu.SMEM((-(-block // part), slots), jnp.int32),
            pltpu.SemaphoreType.DMA((chips + 2,)),
        ],
        compiler_params=small,
        name="scores",
    )(table_pairs, live, rule_of_block, own, *received, mine, other)
    return (smoothed, scores)


def solution(mesh):
    return jax.shard_map(
        on_device,
        mesh=mesh,
        in_specs=(
            P("ion", "pix"),
            P(None, "pix"),
            P("ion", None),
            P("ion"),
            P(),
            P("ion", None, None),
        ),
        out_specs=(P("ion", "pix"), P("ion", "pix", None)),
        check_vma=False,
    )
```

```python
import functools

import jax
import jax.numpy as jnp
from jax import lax
from jax.experimental import pallas as pl
from jax.experimental.pallas import tpu as pltpu
from jax.sharding import PartitionSpec as P

REACH = 3
TAPS = 5
LANES = 128
HALF = LANES // 2
DEPTH = 2 * LANES
VMEM_BYTES = 58 * 1024 * 1024
MAIN_VMEM_BYTES = 125 * 1024 * 512


def params():
    return pltpu.CompilerParams(vmem_limit_bytes=VMEM_BYTES)


def cost(flops, moved):
    return pl.CostEstimate(flops=flops, bytes_accessed=moved, transcendentals=0)


def whole(shape):
    return pl.BlockSpec(shape, lambda *_: (0,) * len(shape))


def fetch(sources, targets, sems):
    copies = [pltpu.make_async_copy(x, y, sems.at[k]) for k, (x, y) in enumerate(zip(sources, targets))]
    for copy in copies:
        copy.start()
    return copies


def smooth_rows(x_ref, halo, w_ref, store):
    rows, width = x_ref.shape
    tiles = width // LANES
    first = lax.broadcasted_iota(jnp.int32, (rows, LANES), 1) < HALF
    before, total, squares = None, None, None
    for j in range(-1, tiles):
        if j < 0:
            window = jnp.concatenate([halo, x_ref[:, :LANES]], axis=1)
        elif j == tiles - 1:
            window = jnp.concatenate([x_ref[:, j * LANES :], halo], axis=1)
        else:
            window = x_ref[:, j * LANES : (j + 2) * LANES]
        now = jnp.dot(window, w_ref[j + 1], preferred_element_type=jnp.float32)
        if j >= 0:
            values = jnp.where(first, before, now)
            store(j, values.astype(jnp.bfloat16))
            squares = values * values if j % 2 == 0 else squares + values * values
            if j % 2 == 1:
                total = squares if total is None else total + squares
        before = now
    return total


def row_sums(part):
    return jnp.sum(part.T, axis=0, keepdims=True)


def gram_of(left, right):
    return lax.dot_general(
        left, right, (((1,), (1,)), ((), ())), preferred_element_type=jnp.float32
    )


def by_core(gram, chips, core):
    parts = gram.reshape(chips, 2, gram.shape[0] // (2 * chips), gram.shape[1])
    even, odd = parts[:, 0].astype(jnp.bfloat16), parts[:, 1].astype(jnp.bfloat16)
    return jnp.where(core == 0, even, odd), jnp.where(core == 0, odd, even)


def write_weights(stencil_ref, out_ref):
    tiles = stencil_ref.shape[1] // LANES
    out_ref[...] = jnp.zeros_like(out_ref)
    k0, rows = 3 * LANES // 8, 5 * LANES // 4
    k = lax.broadcasted_iota(jnp.int32, (rows, LANES), 0) + k0
    lane = lax.broadcasted_iota(jnp.int32, (rows, LANES), 1)
    tap = k - lane + jnp.where(lane < HALF, 2 - LANES, 2)
    early = lax.broadcasted_iota(jnp.int32, (TAPS, LANES), 1) < HALF
    zeros = jnp.zeros((TAPS, LANES), jnp.float32)
    for j in range(-1, tiles):
        here = stencil_ref[:, j * LANES : (j + 1) * LANES] if j >= 0 else zeros
        after = stencil_ref[:, (j + 1) * LANES : (j + 2) * LANES] if j + 1 < tiles else zeros
        taps = jnp.where(early, after, here)
        w = jnp.zeros((rows, LANES), jnp.float32)
        for t in range(TAPS):
            w = jnp.where(tap == t, taps[t : t + 1, :], w)
        out_ref[j + 1, k0 : k0 + rows] = w.astype(jnp.bfloat16)


def cut_kernel(images_ref, stencil_ref, near_rows, far_rows, near_columns, far_columns, w_ref, bands, strips, sems):
    rows, width = images_ref.shape
    edge = near_rows.shape[0]
    odd = lax.axis_index("ion") % 2
    starts = [pl.multiple_of(k * (rows - edge), edge // REACH) for k in (1 - odd, odd)]
    reads = fetch(
        [images_ref.at[pl.ds(start, edge)] for start in starts]
        + [images_ref.at[:, pl.ds(start, LANES)] for start in (0, width - LANES)],
        [bands.at[0], bands.at[1], strips.at[0], strips.at[1]],
        sems,
    )
    writes = [
        pltpu.make_async_copy(bands.at[k], out, sems.at[4 + k]) for k, out in enumerate((near_rows, far_rows))
    ]
    write_weights(stencil_ref, w_ref)
    for read, write in zip(reads, writes):
        read.wait()
        write.start()
    row = lax.broadcasted_iota(jnp.int32, (8, LANES), 0)
    lane = lax.broadcasted_iota(jnp.int32, (8, LANES), 1)
    sides = []
    for k, shift in enumerate((0, LANES - 2)):
        reads[2 + k].wait()
        pick = (lane == row + shift).astype(jnp.bfloat16)
        sides.append(gram_of(pick, strips[k])[:2])
    head, tail = sides
    odd = lax.axis_index("pix") % 2 == 1
    near_columns[...] = jnp.where(odd, head, tail).astype(jnp.bfloat16)
    far_columns[...] = jnp.where(odd, tail, head).astype(jnp.bfloat16)
    for write in writes:
        write.wait()


def halo_tile(columns_ref):
    columns = columns_ref[...].astype(jnp.float32).T.astype(jnp.bfloat16)
    row = lax.broadcasted_iota(jnp.int32, (8, LANES), 0)
    lane = lax.broadcasted_iota(jnp.int32, (8, LANES), 1)
    place = (lane == row + jnp.where(row < 4, 0, LANES - 8)).astype(jnp.bfloat16)
    return jnp.dot(columns, place, preferred_element_type=jnp.float32).astype(jnp.bfloat16)


def main_kernel(steps, group, block, pairs_ref, x_ref, columns_ref, w_ref,
                out_hbm, energy_ref, keep_ref, give_ref, held, sems):
    step = pl.program_id(0)
    blocks = steps * group
    chips = keep_ref.shape[1]
    slots = pairs_ref.shape[1]

    def copy_out(k):
        here = pl.ds(k * group, group)
        return pltpu.make_async_copy(held.at[here], out_hbm.at[here], sems.at[k])

    @pl.when(step < steps)
    def smooth():
        def store(j, values):
            held[pl.ds(step * group, group), :, j * LANES : (j + 1) * LANES] = values.reshape(group, block, LANES)

        total = smooth_rows(x_ref, halo_tile(columns_ref), w_ref, store)
        for g in range(group):
            energy_ref[pl.ds(step * group + g, 1), :] = row_sums(total[g * block : (g + 1) * block, :])

    @pl.when(step == steps)
    def grams():
        for k in range(steps):
            copy_out(k).start()
        core = lax.axis_index("pix") % 2
        first = lax.axis_index("ion") * blocks

        def one(s, carry):
            a = pairs_ref[0, s] - first
            b = jnp.clip(pairs_ref[1, s] - first, 0, blocks - 1)
            keep_ref[s], give_ref[s] = by_core(gram_of(held[a], held[b]), chips, core)
            return carry

        lax.fori_loop(0, slots, one, 0, unroll=12)
        for k in range(steps):
            copy_out(k).wait()


def cross_kernel(blocks, block, pairs_ref, near_hbm, far_hbm, near_columns_hbm, far_columns_hbm, w_hbm, energy_hbm, smoothed_hbm, keep_hbm,
                 give_hbm, keep_ref, give_ref, x_ref, columns_ref, w_ref, energy_ref, own, other, table, sems):
    core = lax.axis_index("pix") % 2
    first_block = lax.axis_index("ion") * blocks
    slots = pairs_ref.shape[1]
    chips, share = keep_ref.shape[1:3]
    units = keep_ref.shape[0] - slots
    edge = REACH * block
    rows = blocks * block
    low, high = pl.ds(0, edge), pl.ds(edge, edge)
    odd = lax.axis_index("ion") % 2
    near, far = (pl.ds(pl.multiple_of(k * edge, edge), edge) for k in (1 - odd, odd))
    copies = fetch(
        (near_hbm, far_hbm, near_columns_hbm, far_columns_hbm, w_hbm, energy_hbm),
        (x_ref.at[near], x_ref.at[far], columns_ref.at[:, near], columns_ref.at[:, far], w_ref, energy_ref),
        sems,
    )
    for copy in copies:
        copy.wait()
    copies = fetch(
        (smoothed_hbm.at[low], smoothed_hbm.at[pl.ds(rows - edge, edge)], keep_hbm, give_hbm),
        (own.at[low], own.at[high], keep_ref, give_ref),
        sems,
    )
    table[...] = jnp.zeros_like(table)
    table[REACH : REACH + blocks, :] = energy_ref[...]
    def store(j, values):
        other[:, j * LANES : (j + 1) * LANES] = values

    total = smooth_rows(x_ref, halo_tile(columns_ref), w_ref, store)
    for k in range(2 * REACH):
        row = k if k < REACH else k + blocks
        table[row : row + 1, :] = row_sums(total[k * block : (k + 1) * block, :])
    for copy in copies:
        copy.wait()

    shape = (units, chips, share, LANES)
    for ref in (keep_ref, give_ref):
        ref[slots:] = table[...].reshape(shape).astype(jnp.bfloat16)

    def one(s, carry):
        a, b = pairs_ref[0, s] - first_block, pairs_ref[1, s] - first_block

        @pl.when((b < 0) | (b >= blocks))
        def crossing():
            side = (b >= 0).astype(jnp.int32)
            a_row = pl.multiple_of((a - side * (blocks - 2 * REACH)) * block, block)
            b_row = pl.multiple_of((b + REACH - side * blocks) * block, block)
            gram = gram_of(own[pl.ds(a_row, block), :], other[pl.ds(b_row, block), :])
            keep_ref[s], give_ref[s] = by_core(gram, chips, core)

        return carry

    lax.fori_loop(0, slots, one, 0)


def chip_kernel(slots, units, keep_hbm, got_hbm, own_ref, *refs):
    out_refs, (keep_ref, got_ref, sems) = refs[:-3], refs[-3:]
    chip = lax.axis_index("pix") // 2
    chips, share = keep_ref.shape[1:3]
    shape = (units * chips, share, LANES)
    for copy in fetch((keep_hbm, got_hbm), (keep_ref, got_ref), sems):
        copy.wait()
    energies = (keep_ref[slots:].astype(jnp.float32) + got_ref[slots:].astype(jnp.float32)).reshape(shape)
    for d in range(chips):
        total = keep_ref[:slots, chip ^ d].astype(jnp.float32) + got_ref[:slots, chip ^ d].astype(jnp.float32)
        if d == 0:
            own_ref[:slots] = total
            own_ref[slots:] = energies
        else:
            out = out_refs[d - 1]
            out[:slots] = total.astype(jnp.bfloat16)
            out[slots:] = energies.astype(jnp.bfloat16)


def score_kernel(blocks, place_of, pixel_count, pairs_ref, live_ref, rules_ref, *refs):
    chips = (len(refs) - 9) // 2
    sources, out_ref, own_ref = refs[: chips + 2], refs[chips + 2], refs[chips + 3]
    got_refs, (table_ref, inverse, left, right, coloc, place, sems) = refs[chips + 4 : -7], refs[-7:]
    slots, share, block = out_ref.shape
    half = table_ref.shape[0] // 2
    targets = (own_ref, *got_refs, table_ref.at[pl.ds(0, half)], table_ref.at[pl.ds(half, half)])
    copies = fetch(sources, targets, sems)
    pix, first = lax.axis_index("pix"), lax.axis_index("ion") * blocks
    pieces = place.shape[0]
    depth = block // pieces

    def find(s, carry):
        for k, at in enumerate(place_of(rules_ref[pairs_ref[1, s]])):
            place[k, s] = at
        return carry

    lax.fori_loop(0, slots, find, 0)
    for copy in copies[:-2]:
        copy.wait()
    gram = own_ref[:slots]
    energies = own_ref[slots:]
    for got in got_refs:
        gram = gram + got[:slots].astype(jnp.float32)
        energies = energies + got[slots:].astype(jnp.float32)
    inverse[...] = (1.0 / jnp.sqrt(energies / pixel_count + 1e-06)).reshape(inverse.shape)

    def pick(s, carry):
        left[pl.ds(s, 1), :] = inverse[pl.ds(pairs_ref[0, s] - first + REACH, 1), :]
        right[pl.ds(s, 1), :] = inverse[pl.ds(pairs_ref[1, s] - first + REACH, 1), :]
        return carry

    lax.fori_loop(0, slots, pick, 0, unroll=8)
    lane = lax.broadcasted_iota(jnp.int32, (1, share, LANES), 2)
    mine = lane == lax.broadcasted_iota(jnp.int32, (1, share, LANES), 1) + pix * share
    inv_a = jnp.sum(jnp.where(mine, left[...][:, None, :], 0.0), axis=2, keepdims=True)
    coloc[...] = (gram * inv_a * right[...][:, None, :] / pixel_count).astype(jnp.bfloat16)
    for copy in copies[-2:]:
        copy.wait()

    def matrix(s):
        rows = [table_ref[pl.ds(pl.multiple_of(place[k, s], depth), depth), :] for k in range(pieces)]
        return jnp.concatenate(rows, axis=0)

    for s in range(0, slots, 2):
        both = jnp.concatenate([matrix(s), matrix(s + 1)], axis=1)
        rows = coloc[s : s + 2].reshape(2 * share, block)
        scores = jnp.dot(rows, both, preferred_element_type=jnp.float32)
        for k in range(2):
            part = scores[k * share : (k + 1) * share, k * block : (k + 1) * block]
            out_ref[s + k] = jnp.where(s + k < live_ref[0], part, 0.0).astype(jnp.bfloat16)


def on_device(images, stencil, pairs, live, rule_of_block, adduct):
    rows, width = images.shape
    rules_here, block, _ = adduct.shape
    blocks = rows // block
    slots = pairs.shape[0]
    n_pix, n_ion = lax.axis_size("pix"), lax.axis_size("ion")
    pix, ion = lax.axis_index("pix"), lax.axis_index("ion")
    pixel_count = width * n_pix
    chips, share = n_pix // 2, block // n_pix
    core, chip = pix % 2, pix // 2
    edge = REACH * block

    def swapped(axis, size, near, far):
        pairs_of = [[(i, i + 1) for i in range(first, size - 1, 2)] for first in (0, 1)]
        return [
            lax.ppermute(value, axis, both + [(j, i) for i, j in both]) for value, both in zip((near, far), pairs_of)
        ]

    vmem = pl.BlockSpec(memory_space=pltpu.VMEM)
    smem = pl.BlockSpec(memory_space=pltpu.SMEM)
    hbm = pl.BlockSpec(memory_space=pl.ANY)
    fixed = pl.BlockSpec(memory_space=pltpu.HBM)

    part = rules_here * block // n_pix
    mine = lax.dynamic_slice_in_dim(adduct.reshape(rules_here * block, block), pix * part, part, 0)
    turns = [lax.ppermute(mine, "ion", [(i, i ^ d) for i in range(n_ion)]) for d in range(1, n_ion)]

    edge_rows = jax.ShapeDtypeStruct((edge, width), images.dtype)
    edge_columns = jax.ShapeDtypeStruct((2, rows), images.dtype)
    near_rows, far_rows, near, far, weights = pl.pallas_call(
        cut_kernel,
        in_specs=[hbm, vmem],
        out_specs=[hbm, hbm, vmem, vmem, vmem],
        out_shape=[
            edge_rows,
            edge_rows,
            edge_columns,
            edge_columns,
            jax.ShapeDtypeStruct((width // LANES + 1, DEPTH, LANES), jnp.bfloat16),
        ],
        scratch_shapes=[
            pltpu.VMEM((2, edge, width), images.dtype),
            pltpu.VMEM((2, rows, LANES), images.dtype),
            pltpu.SemaphoreType.DMA((6,)),
        ],
        compiler_params=params(),
        cost_estimate=cost(0, 8 * edge * width),
        name="cut_edges",
    )(images, stencil)
    near_rows, far_rows = swapped("ion", n_ion, near_rows, far_rows)
    near, far, *turns = lax.optimization_barrier((near, far, *turns))
    mine = jnp.concatenate([mine, *turns], axis=0)
    near, far, mine = lax.optimization_barrier((near, far, mine))
    near, far = swapped("pix", n_pix, near, far)
    odd = pix % 2 == 1
    after, before = jnp.where(odd, far, near), jnp.where(odd, near, far)
    columns = jnp.concatenate([after, jnp.zeros((4, rows), images.dtype), before], axis=0)
    first, last = columns[:, :edge], columns[:, rows - edge :]
    odd = ion % 2 == 1
    near_columns, far_columns = swapped("ion", n_ion, jnp.where(odd, first, last), jnp.where(odd, last, first))

    distances = [n_pix >> k for k in range(1, n_pix.bit_length())]

    def exchange(value, distance):
        return lax.ppermute(value, "pix", [(i, i ^ distance) for i in range(n_pix)])

    mine = jnp.concatenate([mine, exchange(mine, distances[0])], axis=0)

    def place_of(rule):
        row = (rule & (rules_here - 1)) * block
        turn = (rule >> (rules_here.bit_length() - 1)) ^ lax.axis_index("ion")
        pieces = []
        for offset in range(0, block, min(part, block)):
            share_of = ((row + offset) >> (part.bit_length() - 1)) ^ lax.axis_index("pix")
            at = turn * part + ((row + offset) & (part - 1))
            for k, distance in enumerate(distances):
                at = at + jnp.where((share_of & distance) != 0, n_ion * part << k, 0)
            pieces.append(at)
        return pieces

    table_pairs = pairs.T
    group = next(g for g in (8, 5, 4, 2, 1) if blocks % g == 0)
    steps = blocks // group
    units = -(-2 * (blocks + 2 * REACH) // block)
    half = (chips, share, LANES)
    half_shape = (slots + units, *half)
    both_halves = [jax.ShapeDtypeStruct(half_shape, jnp.bfloat16)] * 2

    def rows_at(columns):
        return pl.BlockSpec((group * block, columns), lambda i, *_: (jnp.minimum(i, steps - 1), 0))

    smoothed, energy, keep, give = pl.pallas_call(
        functools.partial(main_kernel, steps, group, block),
        grid_spec=pltpu.PrefetchScalarGridSpec(
            num_scalar_prefetch=1,
            grid=(steps + 1,),
            in_specs=[
                rows_at(width),
                pl.BlockSpec((8, group * block), lambda i, *_: (0, jnp.minimum(i, steps - 1))),
                whole(weights.shape),
            ],
            out_specs=[hbm, whole((blocks, LANES)), whole(half_shape), whole(half_shape)],
            scratch_shapes=[pltpu.VMEM((blocks, block, width), jnp.bfloat16), pltpu.SemaphoreType.DMA((steps,))],
        ),
        out_shape=[
            jax.ShapeDtypeStruct((blocks, block, width), jnp.bfloat16),
            jax.ShapeDtypeStruct((blocks, LANES), jnp.float32),
            *both_halves,
        ],
        compiler_params=pltpu.CompilerParams(vmem_limit_bytes=MAIN_VMEM_BYTES),
        cost_estimate=cost(2 * rows * width * DEPTH + 2 * slots * block * block * width, 4 * rows * width),
        name="smooth_and_gram",
    )(table_pairs, images, columns, weights)
    smoothed = smoothed.reshape(rows, width)
    received = (near_rows, far_rows, near_columns, far_columns)
    energy, mine, *received = lax.optimization_barrier((energy, mine, *received))
    for distance in distances[1:-1]:
        mine = jnp.concatenate([mine, exchange(mine, distance)], axis=0)

    keep, give = pl.pallas_call(
        functools.partial(cross_kernel, blocks, block),
        in_specs=[smem] + [hbm] * 4 + [fixed] * 5,
        out_specs=[vmem, vmem],
        out_shape=both_halves,
        scratch_shapes=[
            pltpu.VMEM((2 * edge, width), jnp.bfloat16),
            pltpu.VMEM((8, 2 * edge), jnp.bfloat16),
            pltpu.VMEM(weights.shape, jnp.bfloat16),
            pltpu.VMEM((blocks, LANES), jnp.float32),
            pltpu.VMEM((2 * edge, width), jnp.bfloat16),
            pltpu.VMEM((2 * edge, width), jnp.bfloat16),
            pltpu.VMEM((units * block // 2, LANES), jnp.float32),
            pltpu.SemaphoreType.DMA((10,)),
        ],
        compiler_params=params(),
        cost_estimate=cost(4 * edge * width * DEPTH, 8 * edge * width),
        name="cross_grams",
    )(table_pairs, *received, weights, energy, smoothed, keep, give)

    got = lax.ppermute(give, "pix", [(i, i ^ 1) for i in range(n_pix)])
    message = jax.ShapeDtypeStruct((slots + units * chips, share, LANES), jnp.bfloat16)
    own_rows = jax.ShapeDtypeStruct((slots + units * chips, share, LANES), jnp.float32)
    small = pltpu.CompilerParams(vmem_limit_bytes=16 * 1024 * 1024)
    own, *messages = pl.pallas_call(
        functools.partial(chip_kernel, slots, units),
        in_specs=[fixed, hbm],
        out_specs=[vmem] * chips,
        out_shape=[own_rows] + [message] * (chips - 1),
        scratch_shapes=[
            pltpu.VMEM(half_shape, jnp.bfloat16),
            pltpu.VMEM(half_shape, jnp.bfloat16),
            pltpu.SemaphoreType.DMA((2,)),
        ],
        compiler_params=small,
        name="chip_sums",
    )(keep, got)
    own, mine = lax.optimization_barrier((own, mine))
    other = exchange(mine, distances[-1])
    received = [
        lax.ppermute(m, "pix", [(i, i ^ (2 * (d + 1))) for i in range(n_pix)]) for d, m in enumerate(messages)
    ]

    scores = pl.pallas_call(
        functools.partial(score_kernel, blocks, place_of, pixel_count),
        in_specs=[smem] * 3 + [hbm] * (chips + 2),
        out_specs=vmem,
        out_shape=jax.ShapeDtypeStruct((slots, share, block), jnp.bfloat16),
        scratch_shapes=[
            pltpu.VMEM(own_rows.shape, jnp.float32),
            *[pltpu.VMEM(message.shape, jnp.bfloat16)] * (chips - 1),
            pltpu.VMEM((2 * mine.shape[0], block), jnp.bfloat16),
            pltpu.VMEM((units * block // 2, LANES), jnp.float32),
            pltpu.VMEM((slots, LANES), jnp.float32),
            pltpu.VMEM((slots, LANES), jnp.float32),
            pltpu.VMEM((slots, share, LANES), jnp.bfloat16),
            pltpu.SMEM((-(-block // part), slots), jnp.int32),
            pltpu.SemaphoreType.DMA((chips + 2,)),
        ],
        compiler_params=small,
        name="scores",
    )(table_pairs, live, rule_of_block, own, *received, mine, other)
    return (smoothed, scores)


def solution(mesh):
    return jax.shard_map(
        on_device,
        mesh=mesh,
        in_specs=(
            P("ion", "pix"),
            P(None, "pix"),
            P("ion", None),
            P("ion"),
            P(),
            P("ion", None, None),
        ),
        out_specs=(P("ion", "pix"), P("ion", "pix", None)),
        check_vma=False,
    )
```

```python
import functools

import jax
import jax.numpy as jnp
from jax import lax
from jax.experimental import pallas as pl
from jax.experimental.pallas import tpu as pltpu
from jax.sharding import PartitionSpec as P

REACH = 3
TAPS = 5
LANES = 128
HALF = LANES // 2
DEPTH = 2 * LANES
VMEM_BYTES = 58 * 1024 * 1024
MAIN_VMEM_BYTES = 125 * 1024 * 512


def params():
    return pltpu.CompilerParams(vmem_limit_bytes=VMEM_BYTES)


def cost(flops, moved):
    return pl.CostEstimate(flops=flops, bytes_accessed=moved, transcendentals=0)


def whole(shape):
    return pl.BlockSpec(shape, lambda *_: (0,) * len(shape))


def fetch(sources, targets, sems):
    copies = [pltpu.make_async_copy(x, y, sems.at[k]) for k, (x, y) in enumerate(zip(sources, targets))]
    for copy in copies:
        copy.start()
    return copies


def smooth_rows(x_ref, halo, w_ref, store):
    rows, width = x_ref.shape
    tiles = width // LANES
    first = lax.broadcasted_iota(jnp.int32, (rows, LANES), 1) < HALF
    before, total, squares = None, None, None
    for j in range(-1, tiles):
        if j < 0:
            window = jnp.concatenate([halo, x_ref[:, :LANES]], axis=1)
        elif j == tiles - 1:
            window = jnp.concatenate([x_ref[:, j * LANES :], halo], axis=1)
        else:
            window = x_ref[:, j * LANES : (j + 2) * LANES]
        now = jnp.dot(window, w_ref[j + 1], preferred_element_type=jnp.float32)
        if j >= 0:
            values = jnp.where(first, before, now)
            store(j, values.astype(jnp.bfloat16))
            squares = values * values if j % 2 == 0 else squares + values * values
            if j % 2 == 1:
                total = squares if total is None else total + squares
        before = now
    return total


def row_sums(part):
    return jnp.sum(part.T, axis=0, keepdims=True)


def gram_of(left, right):
    return lax.dot_general(
        left, right, (((1,), (1,)), ((), ())), preferred_element_type=jnp.float32
    )


def by_core(gram, chips, core):
    parts = gram.reshape(chips, 2, gram.shape[0] // (2 * chips), gram.shape[1])
    even, odd = parts[:, 0].astype(jnp.bfloat16), parts[:, 1].astype(jnp.bfloat16)
    return jnp.where(core == 0, even, odd), jnp.where(core == 0, odd, even)


def write_weights(stencil_ref, out_ref):
    tiles = stencil_ref.shape[1] // LANES
    out_ref[...] = jnp.zeros_like(out_ref)
    k0, rows = 3 * LANES // 8, 5 * LANES // 4
    k = lax.broadcasted_iota(jnp.int32, (rows, LANES), 0) + k0
    lane = lax.broadcasted_iota(jnp.int32, (rows, LANES), 1)
    tap = k - lane + jnp.where(lane < HALF, 2 - LANES, 2)
    early = lax.broadcasted_iota(jnp.int32, (TAPS, LANES), 1) < HALF
    zeros = jnp.zeros((TAPS, LANES), jnp.float32)
    for j in range(-1, tiles):
        here = stencil_ref[:, j * LANES : (j + 1) * LANES] if j >= 0 else zeros
        after = stencil_ref[:, (j + 1) * LANES : (j + 2) * LANES] if j + 1 < tiles else zeros
        taps = jnp.where(early, after, here)
        w = jnp.zeros((rows, LANES), jnp.float32)
        for t in range(TAPS):
            w = jnp.where(tap == t, taps[t : t + 1, :], w)
        out_ref[j + 1, k0 : k0 + rows] = w.astype(jnp.bfloat16)


def cut_kernel(images_ref, stencil_ref, near_rows, far_rows, near_columns, far_columns, w_ref, bands, strips, sems):
    rows, width = images_ref.shape
    edge = near_rows.shape[0]
    odd = lax.axis_index("ion") % 2
    starts = [pl.multiple_of(k * (rows - edge), edge // REACH) for k in (1 - odd, odd)]
    reads = fetch(
        [images_ref.at[pl.ds(start, edge)] for start in starts]
        + [images_ref.at[:, pl.ds(start, LANES)] for start in (0, width - LANES)],
        [bands.at[0], bands.at[1], strips.at[0], strips.at[1]],
        sems,
    )
    writes = [
        pltpu.make_async_copy(bands.at[k], out, sems.at[4 + k]) for k, out in enumerate((near_rows, far_rows))
    ]
    write_weights(stencil_ref, w_ref)
    for read, write in zip(reads, writes):
        read.wait()
        write.start()
    row = lax.broadcasted_iota(jnp.int32, (8, LANES), 0)
    lane = lax.broadcasted_iota(jnp.int32, (8, LANES), 1)
    sides = []
    for k, shift in enumerate((0, LANES - 2)):
        reads[2 + k].wait()
        pick = (lane == row + shift).astype(jnp.bfloat16)
        sides.append(gram_of(pick, strips[k])[:2])
    head, tail = sides
    odd = lax.axis_index("pix") % 2 == 1
    near_columns[...] = jnp.where(odd, head, tail).astype(jnp.bfloat16)
    far_columns[...] = jnp.where(odd, tail, head).astype(jnp.bfloat16)
    for write in writes:
        write.wait()


def halo_tile(columns_ref):
    columns = columns_ref[...].astype(jnp.float32).T.astype(jnp.bfloat16)
    row = lax.broadcasted_iota(jnp.int32, (8, LANES), 0)
    lane = lax.broadcasted_iota(jnp.int32, (8, LANES), 1)
    place = (lane == row + jnp.where(row < 4, 0, LANES - 8)).astype(jnp.bfloat16)
    return jnp.dot(columns, place, preferred_element_type=jnp.float32).astype(jnp.bfloat16)


def main_kernel(steps, group, block, pairs_ref, x_ref, columns_ref, w_ref,
                out_hbm, energy_ref, keep_ref, give_ref, held, sems):
    step = pl.program_id(0)
    blocks = steps * group
    chips = keep_ref.shape[1]
    slots = pairs_ref.shape[1]

    def copy_out(k):
        here = pl.ds(k * group, group)
        return pltpu.make_async_copy(held.at[here], out_hbm.at[here], sems.at[k])

    @pl.when(step < steps)
    def smooth():
        def store(j, values):
            held[pl.ds(step * group, group), :, j * LANES : (j + 1) * LANES] = values.reshape(group, block, LANES)

        total = smooth_rows(x_ref, halo_tile(columns_ref), w_ref, store)
        for g in range(group):
            energy_ref[pl.ds(step * group + g, 1), :] = row_sums(total[g * block : (g + 1) * block, :])

    @pl.when(step == steps)
    def grams():
        for k in range(steps):
            copy_out(k).start()
        core = lax.axis_index("pix") % 2
        first = lax.axis_index("ion") * blocks

        def one(s, carry):
            a = pairs_ref[0, s] - first
            b = jnp.clip(pairs_ref[1, s] - first, 0, blocks - 1)
            keep_ref[s], give_ref[s] = by_core(gram_of(held[a], held[b]), chips, core)
            return carry

        lax.fori_loop(0, slots, one, 0, unroll=12)
        for k in range(steps):
            copy_out(k).wait()


def cross_kernel(blocks, block, pairs_ref, near_hbm, far_hbm, near_columns_hbm, far_columns_hbm, w_hbm, energy_hbm, smoothed_hbm, keep_hbm,
                 give_hbm, keep_ref, give_ref, x_ref, columns_ref, w_ref, energy_ref, own, other, table, sems):
    core = lax.axis_index("pix") % 2
    first_block = lax.axis_index("ion") * blocks
    slots = pairs_ref.shape[1]
    chips, share = keep_ref.shape[1:3]
    units = keep_ref.shape[0] - slots
    edge = REACH * block
    rows = blocks * block
    low, high = pl.ds(0, edge), pl.ds(edge, edge)
    odd = lax.axis_index("ion") % 2
    near, far = (pl.ds(pl.multiple_of(k * edge, edge), edge) for k in (1 - odd, odd))
    copies = fetch(
        (near_hbm, far_hbm, near_columns_hbm, far_columns_hbm, w_hbm, energy_hbm),
        (x_ref.at[near], x_ref.at[far], columns_ref.at[:, near], columns_ref.at[:, far], w_ref, energy_ref),
        sems,
    )
    for copy in copies:
        copy.wait()
    copies = fetch(
        (smoothed_hbm.at[low], smoothed_hbm.at[pl.ds(rows - edge, edge)], keep_hbm, give_hbm),
        (own.at[low], own.at[high], keep_ref, give_ref),
        sems,
    )
    table[...] = jnp.zeros_like(table)
    table[REACH : REACH + blocks, :] = energy_ref[...]
    def store(j, values):
        other[:, j * LANES : (j + 1) * LANES] = values

    total = smooth_rows(x_ref, halo_tile(columns_ref), w_ref, store)
    for k in range(2 * REACH):
        row = k if k < REACH else k + blocks
        table[row : row + 1, :] = row_sums(total[k * block : (k + 1) * block, :])
    for copy in copies:
        copy.wait()

    shape = (units, chips, share, LANES)
    for ref in (keep_ref, give_ref):
        ref[slots:] = table[...].reshape(shape).astype(jnp.bfloat16)

    def one(s, carry):
        a, b = pairs_ref[0, s] - first_block, pairs_ref[1, s] - first_block

        @pl.when((b < 0) | (b >= blocks))
        def crossing():
            side = (b >= 0).astype(jnp.int32)
            a_row = pl.multiple_of((a - side * (blocks - 2 * REACH)) * block, block)
            b_row = pl.multiple_of((b + REACH - side * blocks) * block, block)
            gram = gram_of(own[pl.ds(a_row, block), :], other[pl.ds(b_row, block), :])
            keep_ref[s], give_ref[s] = by_core(gram, chips, core)

        return carry

    lax.fori_loop(0, slots, one, 0)


def chip_kernel(slots, units, keep_hbm, got_hbm, own_ref, *refs):
    out_refs, (keep_ref, got_ref, sems) = refs[:-3], refs[-3:]
    chip = lax.axis_index("pix") // 2
    chips, share = keep_ref.shape[1:3]
    shape = (units * chips, share, LANES)
    for copy in fetch((keep_hbm, got_hbm), (keep_ref, got_ref), sems):
        copy.wait()
    energies = (keep_ref[slots:].astype(jnp.float32) + got_ref[slots:].astype(jnp.float32)).reshape(shape)
    for d in range(chips):
        total = keep_ref[:slots, chip ^ d].astype(jnp.float32) + got_ref[:slots, chip ^ d].astype(jnp.float32)
        if d == 0:
            own_ref[:slots] = total
            own_ref[slots:] = energies
        else:
            out = out_refs[d - 1]
            out[:slots] = total.astype(jnp.bfloat16)
            out[slots:] = energies.astype(jnp.bfloat16)


def score_kernel(blocks, place_of, pixel_count, pairs_ref, live_ref, rules_ref, *refs):
    chips = (len(refs) - 9) // 2
    sources, out_ref, own_ref = refs[: chips + 2], refs[chips + 2], refs[chips + 3]
    got_refs, (table_ref, inverse, left, right, coloc, place, sems) = refs[chips + 4 : -7], refs[-7:]
    slots, share, block = out_ref.shape
    half = table_ref.shape[0] // 2
    targets = (own_ref, *got_refs, table_ref.at[pl.ds(0, half)], table_ref.at[pl.ds(half, half)])
    copies = fetch(sources, targets, sems)
    pix, first = lax.axis_index("pix"), lax.axis_index("ion") * blocks
    pieces = place.shape[0]
    depth = block // pieces

    def find(s, carry):
        for k, at in enumerate(place_of(rules_ref[pairs_ref[1, s]])):
            place[k, s] = at
        return carry

    lax.fori_loop(0, slots, find, 0)
    for copy in copies[:-2]:
        copy.wait()
    gram = own_ref[:slots]
    energies = own_ref[slots:]
    for got in got_refs:
        gram = gram + got[:slots].astype(jnp.float32)
        energies = energies + got[slots:].astype(jnp.float32)
    inverse[...] = (1.0 / jnp.sqrt(energies / pixel_count + 1e-06)).reshape(inverse.shape)

    def pick(s, carry):
        left[pl.ds(s, 1), :] = inverse[pl.ds(pairs_ref[0, s] - first + REACH, 1), :]
        right[pl.ds(s, 1), :] = inverse[pl.ds(pairs_ref[1, s] - first + REACH, 1), :]
        return carry

    lax.fori_loop(0, slots, pick, 0, unroll=8)
    lane = lax.broadcasted_iota(jnp.int32, (1, share, LANES), 2)
    mine = lane == lax.broadcasted_iota(jnp.int32, (1, share, LANES), 1) + pix * share
    inv_a = jnp.sum(jnp.where(mine, left[...][:, None, :], 0.0), axis=2, keepdims=True)
    coloc[...] = (gram * inv_a * right[...][:, None, :] / pixel_count).astype(jnp.bfloat16)
    for copy in copies[-2:]:
        copy.wait()

    def matrix(s):
        rows = [table_ref[pl.ds(pl.multiple_of(place[k, s], depth), depth), :] for k in range(pieces)]
        return jnp.concatenate(rows, axis=0)

    for s in range(0, slots, 2):
        both = jnp.concatenate([matrix(s), matrix(s + 1)], axis=1)
        rows = coloc[s : s + 2].reshape(2 * share, block)
        scores = jnp.dot(rows, both, preferred_element_type=jnp.float32)
        for k in range(2):
            part = scores[k * share : (k + 1) * share, k * block : (k + 1) * block]
            out_ref[s + k] = jnp.where(s + k < live_ref[0], part, 0.0).astype(jnp.bfloat16)


def on_device(images, stencil, pairs, live, rule_of_block, adduct):
    rows, width = images.shape
    rules_here, block, _ = adduct.shape
    blocks = rows // block
    slots = pairs.shape[0]
    n_pix, n_ion = lax.axis_size("pix"), lax.axis_size("ion")
    pix, ion = lax.axis_index("pix"), lax.axis_index("ion")
    pixel_count = width * n_pix
    chips, share = n_pix // 2, block // n_pix
    core, chip = pix % 2, pix // 2
    edge = REACH * block

    def swapped(axis, size, near, far):
        pairs_of = [[(i, i + 1) for i in range(first, size - 1, 2)] for first in (0, 1)]
        return [
            lax.ppermute(value, axis, both + [(j, i) for i, j in both]) for value, both in zip((near, far), pairs_of)
        ]

    vmem = pl.BlockSpec(memory_space=pltpu.VMEM)
    smem = pl.BlockSpec(memory_space=pltpu.SMEM)
    hbm = pl.BlockSpec(memory_space=pl.ANY)
    fixed = pl.BlockSpec(memory_space=pltpu.HBM)

    part = rules_here * block // n_pix
    mine = lax.dynamic_slice_in_dim(adduct.reshape(rules_here * block, block), pix * part, part, 0)
    turns = [lax.ppermute(mine, "ion", [(i, i ^ d) for i in range(n_ion)]) for d in range(1, n_ion)]

    edge_rows = jax.ShapeDtypeStruct((edge, width), images.dtype)
    edge_columns = jax.ShapeDtypeStruct((2, rows), images.dtype)
    near_rows, far_rows, near, far, weights = pl.pallas_call(
        cut_kernel,
        in_specs=[hbm, vmem],
        out_specs=[hbm, hbm, vmem, vmem, vmem],
        out_shape=[
            edge_rows,
            edge_rows,
            edge_columns,
            edge_columns,
            jax.ShapeDtypeStruct((width // LANES + 1, DEPTH, LANES), jnp.bfloat16),
        ],
        scratch_shapes=[
            pltpu.VMEM((2, edge, width), images.dtype),
            pltpu.VMEM((2, rows, LANES), images.dtype),
            pltpu.SemaphoreType.DMA((6,)),
        ],
        compiler_params=params(),
        cost_estimate=cost(0, 8 * edge * width),
        name="cut_edges",
    )(images, stencil)
    near_rows, far_rows = swapped("ion", n_ion, near_rows, far_rows)
    near, far, *turns = lax.optimization_barrier((near, far, *turns))
    mine = jnp.concatenate([mine, *turns], axis=0)
    near, far, mine = lax.optimization_barrier((near, far, mine))
    near, far = swapped("pix", n_pix, near, far)
    odd = pix % 2 == 1
    after, before = jnp.where(odd, far, near), jnp.where(odd, near, far)
    columns = jnp.concatenate([after, jnp.zeros((4, rows), images.dtype), before], axis=0)
    first, last = columns[:, :edge], columns[:, rows - edge :]
    odd = ion % 2 == 1
    near_columns, far_columns = swapped("ion", n_ion, jnp.where(odd, first, last), jnp.where(odd, last, first))

    distances = [n_pix >> k for k in range(1, n_pix.bit_length())]

    def exchange(value, distance):
        return lax.ppermute(value, "pix", [(i, i ^ distance) for i in range(n_pix)])

    for distance in distances[:-1]:
        mine = jnp.concatenate([mine, exchange(mine, distance)], axis=0)

    def place_of(rule):
        row = (rule & (rules_here - 1)) * block
        turn = (rule >> (rules_here.bit_length() - 1)) ^ lax.axis_index("ion")
        pieces = []
        for offset in range(0, block, min(part, block)):
            share_of = ((row + offset) >> (part.bit_length() - 1)) ^ lax.axis_index("pix")
            at = turn * part + ((row + offset) & (part - 1))
            for k, distance in enumerate(distances):
                at = at + jnp.where((share_of & distance) != 0, n_ion * part << k, 0)
            pieces.append(at)
        return pieces

    table_pairs = pairs.T
    group = next(g for g in (8, 5, 4, 2, 1) if blocks % g == 0)
    steps = blocks // group
    units = -(-2 * (blocks + 2 * REACH) // block)
    half = (chips, share, LANES)
    half_shape = (slots + units, *half)
    both_halves = [jax.ShapeDtypeStruct(half_shape, jnp.bfloat16)] * 2

    def rows_at(columns):
        return pl.BlockSpec((group * block, columns), lambda i, *_: (jnp.minimum(i, steps - 1), 0))

    smoothed, energy, keep, give = pl.pallas_call(
        functools.partial(main_kernel, steps, group, block),
        grid_spec=pltpu.PrefetchScalarGridSpec(
            num_scalar_prefetch=1,
            grid=(steps + 1,),
            in_specs=[
                rows_at(width),
                pl.BlockSpec((8, group * block), lambda i, *_: (0, jnp.minimum(i, steps - 1))),
                whole(weights.shape),
            ],
            out_specs=[hbm, whole((blocks, LANES)), whole(half_shape), whole(half_shape)],
            scratch_shapes=[pltpu.VMEM((blocks, block, width), jnp.bfloat16), pltpu.SemaphoreType.DMA((steps,))],
        ),
        out_shape=[
            jax.ShapeDtypeStruct((blocks, block, width), jnp.bfloat16),
            jax.ShapeDtypeStruct((blocks, LANES), jnp.float32),
            *both_halves,
        ],
        compiler_params=pltpu.CompilerParams(vmem_limit_bytes=MAIN_VMEM_BYTES),
        cost_estimate=cost(2 * rows * width * DEPTH + 2 * slots * block * block * width, 4 * rows * width),
        name="smooth_and_gram",
    )(table_pairs, images, columns, weights)
    smoothed = smoothed.reshape(rows, width)
    keep, give = pl.pallas_call(
        functools.partial(cross_kernel, blocks, block),
        in_specs=[smem] + [hbm] * 4 + [fixed] * 5,
        out_specs=[vmem, vmem],
        out_shape=both_halves,
        scratch_shapes=[
            pltpu.VMEM((2 * edge, width), jnp.bfloat16),
            pltpu.VMEM((8, 2 * edge), jnp.bfloat16),
            pltpu.VMEM(weights.shape, jnp.bfloat16),
            pltpu.VMEM((blocks, LANES), jnp.float32),
            pltpu.VMEM((2 * edge, width), jnp.bfloat16),
            pltpu.VMEM((2 * edge, width), jnp.bfloat16),
            pltpu.VMEM((units * block // 2, LANES), jnp.float32),
            pltpu.SemaphoreType.DMA((10,)),
        ],
        compiler_params=params(),
        cost_estimate=cost(4 * edge * width * DEPTH, 8 * edge * width),
        name="cross_grams",
    )(table_pairs, near_rows, far_rows, near_columns, far_columns, weights, energy, smoothed, keep, give)

    got = lax.ppermute(give, "pix", [(i, i ^ 1) for i in range(n_pix)])
    message = jax.ShapeDtypeStruct((slots + units * chips, share, LANES), jnp.bfloat16)
    own_rows = jax.ShapeDtypeStruct((slots + units * chips, share, LANES), jnp.float32)
    small = pltpu.CompilerParams(vmem_limit_bytes=16 * 1024 * 1024)
    own, *messages = pl.pallas_call(
        functools.partial(chip_kernel, slots, units),
        in_specs=[fixed, hbm],
        out_specs=[vmem] * chips,
        out_shape=[own_rows] + [message] * (chips - 1),
        scratch_shapes=[
            pltpu.VMEM(half_shape, jnp.bfloat16),
            pltpu.VMEM(half_shape, jnp.bfloat16),
            pltpu.SemaphoreType.DMA((2,)),
        ],
        compiler_params=small,
        name="chip_sums",
    )(keep, got)
    own, mine = lax.optimization_barrier((own, mine))
    other = exchange(mine, distances[-1])
    received = [
        lax.ppermute(m, "pix", [(i, i ^ (2 * (d + 1))) for i in range(n_pix)]) for d, m in enumerate(messages)
    ]

    scores = pl.pallas_call(
        functools.partial(score_kernel, blocks, place_of, pixel_count),
        in_specs=[smem] * 3 + [hbm] * (chips + 2),
        out_specs=vmem,
        out_shape=jax.ShapeDtypeStruct((slots, share, block), jnp.bfloat16),
        scratch_shapes=[
            pltpu.VMEM(own_rows.shape, jnp.float32),
            *[pltpu.VMEM(message.shape, jnp.bfloat16)] * (chips - 1),
            pltpu.VMEM((2 * mine.shape[0], block), jnp.bfloat16),
            pltpu.VMEM((units * block // 2, LANES), jnp.float32),
            pltpu.VMEM((slots, LANES), jnp.float32),
            pltpu.VMEM((slots, LANES), jnp.float32),
            pltpu.VMEM((slots, share, LANES), jnp.bfloat16),
            pltpu.SMEM((-(-block // part), slots), jnp.int32),
            pltpu.SemaphoreType.DMA((chips + 2,)),
        ],
        compiler_params=small,
        name="scores",
    )(table_pairs, live, rule_of_block, own, *received, mine, other)
    return (smoothed, scores)


def solution(mesh):
    return jax.shard_map(
        on_device,
        mesh=mesh,
        in_specs=(
            P("ion", "pix"),
            P(None, "pix"),
            P("ion", None),
            P("ion"),
            P(),
            P("ion", None, None),
        ),
        out_specs=(P("ion", "pix"), P("ion", "pix", None)),
        check_vma=False,
    )
```

```python
import functools

import jax
import jax.numpy as jnp
from jax import lax
from jax.experimental import pallas as pl
from jax.experimental.pallas import tpu as pltpu
from jax.sharding import PartitionSpec as P

REACH = 3
TAPS = 5
LANES = 128
HALF = LANES // 2
DEPTH = 2 * LANES
VMEM_BYTES = 58 * 1024 * 1024
MAIN_VMEM_BYTES = 125 * 1024 * 512


def params():
    return pltpu.CompilerParams(vmem_limit_bytes=VMEM_BYTES)


def cost(flops, moved):
    return pl.CostEstimate(flops=flops, bytes_accessed=moved, transcendentals=0)


def whole(shape):
    return pl.BlockSpec(shape, lambda *_: (0,) * len(shape))


def fetch(sources, targets, sems):
    copies = [pltpu.make_async_copy(x, y, sems.at[k]) for k, (x, y) in enumerate(zip(sources, targets))]
    for copy in copies:
        copy.start()
    return copies


def smooth_rows(x_ref, halo, w_ref, store):
    rows, width = x_ref.shape
    tiles = width // LANES
    first = lax.broadcasted_iota(jnp.int32, (rows, LANES), 1) < HALF
    before, total, squares = None, None, None
    for j in range(-1, tiles):
        if j < 0:
            window = jnp.concatenate([halo, x_ref[:, :LANES]], axis=1)
        elif j == tiles - 1:
            window = jnp.concatenate([x_ref[:, j * LANES :], halo], axis=1)
        else:
            window = x_ref[:, j * LANES : (j + 2) * LANES]
        now = jnp.dot(window, w_ref[j + 1], preferred_element_type=jnp.float32)
        if j >= 0:
            values = jnp.where(first, before, now)
            store(j, values.astype(jnp.bfloat16))
            squares = values * values if j % 2 == 0 else squares + values * values
            if j % 2 == 1:
                total = squares if total is None else total + squares
        before = now
    return total


def row_sums(part):
    return jnp.sum(part.T, axis=0, keepdims=True)


def gram_of(left, right):
    return lax.dot_general(
        left, right, (((1,), (1,)), ((), ())), preferred_element_type=jnp.float32
    )


def by_core(gram, chips, core):
    parts = gram.reshape(chips, 2, gram.shape[0] // (2 * chips), gram.shape[1])
    even, odd = parts[:, 0].astype(jnp.bfloat16), parts[:, 1].astype(jnp.bfloat16)
    return jnp.where(core == 0, even, odd), jnp.where(core == 0, odd, even)


def write_weights(stencil_ref, out_ref):
    tiles = stencil_ref.shape[1] // LANES
    out_ref[...] = jnp.zeros_like(out_ref)
    k0, rows = 3 * LANES // 8, 5 * LANES // 4
    k = lax.broadcasted_iota(jnp.int32, (rows, LANES), 0) + k0
    lane = lax.broadcasted_iota(jnp.int32, (rows, LANES), 1)
    tap = k - lane + jnp.where(lane < HALF, 2 - LANES, 2)
    early = lax.broadcasted_iota(jnp.int32, (TAPS, LANES), 1) < HALF
    zeros = jnp.zeros((TAPS, LANES), jnp.float32)
    for j in range(-1, tiles):
        here = stencil_ref[:, j * LANES : (j + 1) * LANES] if j >= 0 else zeros
        after = stencil_ref[:, (j + 1) * LANES : (j + 2) * LANES] if j + 1 < tiles else zeros
        taps = jnp.where(early, after, here)
        w = jnp.zeros((rows, LANES), jnp.float32)
        for t in range(TAPS):
            w = jnp.where(tap == t, taps[t : t + 1, :], w)
        out_ref[j + 1, k0 : k0 + rows] = w.astype(jnp.bfloat16)


def cut_kernel(images_ref, stencil_ref, near_rows, far_rows, near_columns, far_columns, w_ref, bands, strips, sems):
    rows, width = images_ref.shape
    edge = near_rows.shape[0]
    odd = lax.axis_index("ion") % 2
    starts = [pl.multiple_of(k * (rows - edge), edge // REACH) for k in (1 - odd, odd)]
    reads = fetch(
        [images_ref.at[pl.ds(start, edge)] for start in starts]
        + [images_ref.at[:, pl.ds(start, LANES)] for start in (0, width - LANES)],
        [bands.at[0], bands.at[1], strips.at[0], strips.at[1]],
        sems,
    )
    writes = [
        pltpu.make_async_copy(bands.at[k], out, sems.at[4 + k]) for k, out in enumerate((near_rows, far_rows))
    ]
    write_weights(stencil_ref, w_ref)
    for read, write in zip(reads, writes):
        read.wait()
        write.start()
    row = lax.broadcasted_iota(jnp.int32, (8, LANES), 0)
    lane = lax.broadcasted_iota(jnp.int32, (8, LANES), 1)
    sides = []
    for k, shift in enumerate((0, LANES - 2)):
        reads[2 + k].wait()
        pick = (lane == row + shift).astype(jnp.bfloat16)
        sides.append(gram_of(pick, strips[k])[:2])
    head, tail = sides
    odd = lax.axis_index("pix") % 2 == 1
    near_columns[...] = jnp.where(odd, head, tail).astype(jnp.bfloat16)
    far_columns[...] = jnp.where(odd, tail, head).astype(jnp.bfloat16)
    for write in writes:
        write.wait()


def halo_tile(columns_ref):
    columns = columns_ref[...].astype(jnp.float32).T.astype(jnp.bfloat16)
    row = lax.broadcasted_iota(jnp.int32, (8, LANES), 0)
    lane = lax.broadcasted_iota(jnp.int32, (8, LANES), 1)
    place = (lane == row + jnp.where(row < 4, 0, LANES - 8)).astype(jnp.bfloat16)
    return jnp.dot(columns, place, preferred_element_type=jnp.float32).astype(jnp.bfloat16)


def main_kernel(steps, group, block, pairs_ref, x_ref, columns_ref, w_ref,
                out_hbm, energy_ref, keep_ref, give_ref, held, sems):
    step = pl.program_id(0)
    blocks = steps * group
    chips = keep_ref.shape[1]
    slots = pairs_ref.shape[1]

    def copy_out(k):
        here = pl.ds(k * group, group)
        return pltpu.make_async_copy(held.at[here], out_hbm.at[here], sems.at[k])

    @pl.when(step < steps)
    def smooth():
        def store(j, values):
            held[pl.ds(step * group, group), :, j * LANES : (j + 1) * LANES] = values.reshape(group, block, LANES)

        total = smooth_rows(x_ref, halo_tile(columns_ref), w_ref, store)
        for g in range(group):
            energy_ref[pl.ds(step * group + g, 1), :] = row_sums(total[g * block : (g + 1) * block, :])

    @pl.when(step == steps)
    def grams():
        for k in range(steps):
            copy_out(k).start()
        core = lax.axis_index("pix") % 2
        first = lax.axis_index("ion") * blocks

        def one(s, carry):
            a = pairs_ref[0, s] - first
            b = jnp.clip(pairs_ref[1, s] - first, 0, blocks - 1)
            keep_ref[s], give_ref[s] = by_core(gram_of(held[a], held[b]), chips, core)
            return carry

        lax.fori_loop(0, slots, one, 0, unroll=24)
        for k in range(steps):
            copy_out(k).wait()


def cross_kernel(blocks, block, pairs_ref, near_hbm, far_hbm, near_columns_hbm, far_columns_hbm, w_hbm, energy_hbm, smoothed_hbm, keep_hbm,
                 give_hbm, keep_ref, give_ref, x_ref, columns_ref, w_ref, energy_ref, own, other, table, found, sems):
    core = lax.axis_index("pix") % 2
    first_block = lax.axis_index("ion") * blocks
    slots = pairs_ref.shape[1]
    chips, share = keep_ref.shape[1:3]
    units = keep_ref.shape[0] - slots
    edge = REACH * block
    rows = blocks * block
    low, high = pl.ds(0, edge), pl.ds(edge, edge)
    odd = lax.axis_index("ion") % 2
    near, far = (pl.ds(pl.multiple_of(k * edge, edge), edge) for k in (1 - odd, odd))
    copies = fetch(
        (near_hbm, far_hbm, near_columns_hbm, far_columns_hbm, w_hbm, energy_hbm),
        (x_ref.at[near], x_ref.at[far], columns_ref.at[:, near], columns_ref.at[:, far], w_ref, energy_ref),
        sems,
    )
    for copy in copies:
        copy.wait()
    copies = fetch(
        (smoothed_hbm.at[low], smoothed_hbm.at[pl.ds(rows - edge, edge)], keep_hbm, give_hbm),
        (own.at[low], own.at[high], keep_ref, give_ref),
        sems,
    )
    table[...] = jnp.zeros_like(table)
    table[REACH : REACH + blocks, :] = energy_ref[...]
    def store(j, values):
        other[:, j * LANES : (j + 1) * LANES] = values

    total = smooth_rows(x_ref, halo_tile(columns_ref), w_ref, store)
    for k in range(2 * REACH):
        row = k if k < REACH else k + blocks
        table[row : row + 1, :] = row_sums(total[k * block : (k + 1) * block, :])
    for copy in copies:
        copy.wait()

    shape = (units, chips, share, LANES)
    for ref in (keep_ref, give_ref):
        ref[slots:] = table[...].reshape(shape).astype(jnp.bfloat16)

    def gather(s, count):
        b = pairs_ref[1, s] - first_block
        found[count] = s
        return count + ((b < 0) | (b >= blocks)).astype(jnp.int32)

    count = lax.fori_loop(0, slots, gather, 0)

    def four(k, carry):
        for i in range(4):
            s = found[jnp.minimum(4 * k + i, count - 1)]
            a, b = pairs_ref[0, s] - first_block, pairs_ref[1, s] - first_block
            side = (b >= 0).astype(jnp.int32)
            a_row = pl.multiple_of((a - side * (blocks - 2 * REACH)) * block, block)
            b_row = pl.multiple_of((b + REACH - side * blocks) * block, block)
            gram = gram_of(own[pl.ds(a_row, block), :], other[pl.ds(b_row, block), :])
            keep_ref[s], give_ref[s] = by_core(gram, chips, core)
        return carry

    lax.fori_loop(0, (count + 3) // 4, four, 0)


def chip_kernel(slots, units, keep_hbm, got_hbm, own_ref, *refs):
    out_refs, (keep_ref, got_ref, sems) = refs[:-3], refs[-3:]
    chip = lax.axis_index("pix") // 2
    chips, share = keep_ref.shape[1:3]
    shape = (units * chips, share, LANES)
    for copy in fetch((keep_hbm, got_hbm), (keep_ref, got_ref), sems):
        copy.wait()
    energies = (keep_ref[slots:].astype(jnp.float32) + got_ref[slots:].astype(jnp.float32)).reshape(shape)
    for d in range(chips):
        total = keep_ref[:slots, chip ^ d].astype(jnp.float32) + got_ref[:slots, chip ^ d].astype(jnp.float32)
        if d == 0:
            own_ref[:slots] = total
            own_ref[slots:] = energies
        else:
            out = out_refs[d - 1]
            out[:slots] = total.astype(jnp.bfloat16)
            out[slots:] = energies.astype(jnp.bfloat16)


def score_kernel(blocks, place_of, pixel_count, pairs_ref, live_ref, rules_ref, *refs):
    chips = (len(refs) - 9) // 2
    sources, out_ref, own_ref = refs[: chips + 2], refs[chips + 2], refs[chips + 3]
    got_refs, (table_ref, inverse, left, right, coloc, place, sems) = refs[chips + 4 : -7], refs[-7:]
    slots, share, block = out_ref.shape
    half = table_ref.shape[0] // 2
    targets = (own_ref, *got_refs, table_ref.at[pl.ds(0, half)], table_ref.at[pl.ds(half, half)])
    copies = fetch(sources, targets, sems)
    pix, first = lax.axis_index("pix"), lax.axis_index("ion") * blocks
    pieces = place.shape[0]
    depth = block // pieces

    def find(s, carry):
        for k, at in enumerate(place_of(rules_ref[pairs_ref[1, s]])):
            place[k, s] = at
        return carry

    lax.fori_loop(0, slots, find, 0, unroll=8)
    for copy in copies[:-2]:
        copy.wait()
    gram = own_ref[:slots]
    energies = own_ref[slots:]
    for got in got_refs:
        gram = gram + got[:slots].astype(jnp.float32)
        energies = energies + got[slots:].astype(jnp.float32)
    inverse[...] = (1.0 / jnp.sqrt(energies / pixel_count + 1e-06)).reshape(inverse.shape)

    def pick(s, carry):
        left[pl.ds(s, 1), :] = inverse[pl.ds(pairs_ref[0, s] - first + REACH, 1), :]
        right[pl.ds(s, 1), :] = inverse[pl.ds(pairs_ref[1, s] - first + REACH, 1), :]
        return carry

    lax.fori_loop(0, slots, pick, 0, unroll=8)
    lane = lax.broadcasted_iota(jnp.int32, (1, share, LANES), 2)
    mine = lane == lax.broadcasted_iota(jnp.int32, (1, share, LANES), 1) + pix * share
    inv_a = jnp.sum(jnp.where(mine, left[...][:, None, :], 0.0), axis=2, keepdims=True)
    coloc[...] = (gram * inv_a * right[...][:, None, :] / pixel_count).astype(jnp.bfloat16)
    for copy in copies[-2:]:
        copy.wait()

    def matrix(s):
        rows = [table_ref[pl.ds(pl.multiple_of(place[k, s], depth), depth), :] for k in range(pieces)]
        return jnp.concatenate(rows, axis=0)

    for s in range(0, slots, 2):
        both = jnp.concatenate([matrix(s), matrix(s + 1)], axis=1)
        rows = coloc[s : s + 2].reshape(2 * share, block)
        scores = jnp.dot(rows, both, preferred_element_type=jnp.float32)
        for k in range(2):
            part = scores[k * share : (k + 1) * share, k * block : (k + 1) * block]
            out_ref[s + k] = jnp.where(s + k < live_ref[0], part, 0.0).astype(jnp.bfloat16)


def on_device(images, stencil, pairs, live, rule_of_block, adduct):
    rows, width = images.shape
    rules_here, block, _ = adduct.shape
    blocks = rows // block
    slots = pairs.shape[0]
    n_pix, n_ion = lax.axis_size("pix"), lax.axis_size("ion")
    pix, ion = lax.axis_index("pix"), lax.axis_index("ion")
    pixel_count = width * n_pix
    chips, share = n_pix // 2, block // n_pix
    core, chip = pix % 2, pix // 2
    edge = REACH * block

    def swapped(axis, size, near, far):
        pairs_of = [[(i, i + 1) for i in range(first, size - 1, 2)] for first in (0, 1)]
        return [
            lax.ppermute(value, axis, both + [(j, i) for i, j in both]) for value, both in zip((near, far), pairs_of)
        ]

    vmem = pl.BlockSpec(memory_space=pltpu.VMEM)
    smem = pl.BlockSpec(memory_space=pltpu.SMEM)
    hbm = pl.BlockSpec(memory_space=pl.ANY)
    fixed = pl.BlockSpec(memory_space=pltpu.HBM)

    part = rules_here * block // n_pix
    mine = lax.dynamic_slice_in_dim(adduct.reshape(rules_here * block, block), pix * part, part, 0)
    turns = [lax.ppermute(mine, "ion", [(i, i ^ d) for i in range(n_ion)]) for d in range(1, n_ion)]

    edge_rows = jax.ShapeDtypeStruct((edge, width), images.dtype)
    edge_columns = jax.ShapeDtypeStruct((2, rows), images.dtype)
    near_rows, far_rows, near, far, weights = pl.pallas_call(
        cut_kernel,
        in_specs=[hbm, vmem],
        out_specs=[hbm, hbm, vmem, vmem, vmem],
        out_shape=[
            edge_rows,
            edge_rows,
            edge_columns,
            edge_columns,
            jax.ShapeDtypeStruct((width // LANES + 1, DEPTH, LANES), jnp.bfloat16),
        ],
        scratch_shapes=[
            pltpu.VMEM((2, edge, width), images.dtype),
            pltpu.VMEM((2, rows, LANES), images.dtype),
            pltpu.SemaphoreType.DMA((6,)),
        ],
        compiler_params=params(),
        cost_estimate=cost(0, 8 * edge * width),
        name="cut_edges",
    )(images, stencil)
    near_rows, far_rows = swapped("ion", n_ion, near_rows, far_rows)
    near, far, *turns = lax.optimization_barrier((near, far, *turns))
    mine = jnp.concatenate([mine, *turns], axis=0)
    near, far, mine = lax.optimization_barrier((near, far, mine))
    near, far = swapped("pix", n_pix, near, far)
    odd = pix % 2 == 1
    after, before = jnp.where(odd, far, near), jnp.where(odd, near, far)
    columns = jnp.concatenate([after, jnp.zeros((4, rows), images.dtype), before], axis=0)
    first, last = columns[:, :edge], columns[:, rows - edge :]
    odd = ion % 2 == 1
    near_columns, far_columns = swapped("ion", n_ion, jnp.where(odd, first, last), jnp.where(odd, last, first))

    distances = [n_pix >> k for k in range(1, n_pix.bit_length())]

    def exchange(value, distance):
        return lax.ppermute(value, "pix", [(i, i ^ distance) for i in range(n_pix)])

    for distance in distances[:-1]:
        mine = jnp.concatenate([mine, exchange(mine, distance)], axis=0)

    def place_of(rule):
        row = (rule & (rules_here - 1)) * block
        turn = (rule >> (rules_here.bit_length() - 1)) ^ lax.axis_index("ion")
        pieces = []
        for offset in range(0, block, min(part, block)):
            share_of = ((row + offset) >> (part.bit_length() - 1)) ^ lax.axis_index("pix")
            at = turn * part + ((row + offset) & (part - 1))
            for k, distance in enumerate(distances):
                at = at + jnp.where((share_of & distance) != 0, n_ion * part << k, 0)
            pieces.append(at)
        return pieces

    table_pairs = pairs.T
    group = next(g for g in (8, 5, 4, 2, 1) if blocks % g == 0)
    steps = blocks // group
    units = -(-2 * (blocks + 2 * REACH) // block)
    half = (chips, share, LANES)
    half_shape = (slots + units, *half)
    both_halves = [jax.ShapeDtypeStruct(half_shape, jnp.bfloat16)] * 2

    def rows_at(columns):
        return pl.BlockSpec((group * block, columns), lambda i, *_: (jnp.minimum(i, steps - 1), 0))

    smoothed, energy, keep, give = pl.pallas_call(
        functools.partial(main_kernel, steps, group, block),
        grid_spec=pltpu.PrefetchScalarGridSpec(
            num_scalar_prefetch=1,
            grid=(steps + 1,),
            in_specs=[
                rows_at(width),
                pl.BlockSpec((8, group * block), lambda i, *_: (0, jnp.minimum(i, steps - 1))),
                whole(weights.shape),
            ],
            out_specs=[hbm, whole((blocks, LANES)), whole(half_shape), whole(half_shape)],
            scratch_shapes=[pltpu.VMEM((blocks, block, width), jnp.bfloat16), pltpu.SemaphoreType.DMA((steps,))],
        ),
        out_shape=[
            jax.ShapeDtypeStruct((blocks, block, width), jnp.bfloat16),
            jax.ShapeDtypeStruct((blocks, LANES), jnp.float32),
            *both_halves,
        ],
        compiler_params=pltpu.CompilerParams(vmem_limit_bytes=MAIN_VMEM_BYTES),
        cost_estimate=cost(2 * rows * width * DEPTH + 2 * slots * block * block * width, 4 * rows * width),
        name="smooth_and_gram",
    )(table_pairs, images, columns, weights)
    smoothed = smoothed.reshape(rows, width)
    keep, give = pl.pallas_call(
        functools.partial(cross_kernel, blocks, block),
        in_specs=[smem] + [hbm] * 4 + [fixed] * 5,
        out_specs=[vmem, vmem],
        out_shape=both_halves,
        scratch_shapes=[
            pltpu.VMEM((2 * edge, width), jnp.bfloat16),
            pltpu.VMEM((8, 2 * edge), jnp.bfloat16),
            pltpu.VMEM(weights.shape, jnp.bfloat16),
            pltpu.VMEM((blocks, LANES), jnp.float32),
            pltpu.VMEM((2 * edge, width), jnp.bfloat16),
            pltpu.VMEM((2 * edge, width), jnp.bfloat16),
            pltpu.VMEM((units * block // 2, LANES), jnp.float32),
            pltpu.SMEM((slots + 1,), jnp.int32),
            pltpu.SemaphoreType.DMA((10,)),
        ],
        compiler_params=params(),
        cost_estimate=cost(4 * edge * width * DEPTH, 8 * edge * width),
        name="cross_grams",
    )(table_pairs, near_rows, far_rows, near_columns, far_columns, weights, energy, smoothed, keep, give)

    got = lax.ppermute(give, "pix", [(i, i ^ 1) for i in range(n_pix)])
    message = jax.ShapeDtypeStruct((slots + units * chips, share, LANES), jnp.bfloat16)
    own_rows = jax.ShapeDtypeStruct((slots + units * chips, share, LANES), jnp.float32)
    small = pltpu.CompilerParams(vmem_limit_bytes=16 * 1024 * 1024)
    own, *messages = pl.pallas_call(
        functools.partial(chip_kernel, slots, units),
        in_specs=[fixed, hbm],
        out_specs=[vmem] * chips,
        out_shape=[own_rows] + [message] * (chips - 1),
        scratch_shapes=[
            pltpu.VMEM(half_shape, jnp.bfloat16),
            pltpu.VMEM(half_shape, jnp.bfloat16),
            pltpu.SemaphoreType.DMA((2,)),
        ],
        compiler_params=small,
        name="chip_sums",
    )(keep, got)
    own, mine = lax.optimization_barrier((own, mine))
    other = exchange(mine, distances[-1])
    received = [
        lax.ppermute(m, "pix", [(i, i ^ (2 * (d + 1))) for i in range(n_pix)]) for d, m in enumerate(messages)
    ]

    scores = pl.pallas_call(
        functools.partial(score_kernel, blocks, place_of, pixel_count),
        in_specs=[smem] * 3 + [hbm] * (chips + 2),
        out_specs=vmem,
        out_shape=jax.ShapeDtypeStruct((slots, share, block), jnp.bfloat16),
        scratch_shapes=[
            pltpu.VMEM(own_rows.shape, jnp.float32),
            *[pltpu.VMEM(message.shape, jnp.bfloat16)] * (chips - 1),
            pltpu.VMEM((2 * mine.shape[0], block), jnp.bfloat16),
            pltpu.VMEM((units * block // 2, LANES), jnp.float32),
            pltpu.VMEM((slots, LANES), jnp.float32),
            pltpu.VMEM((slots, LANES), jnp.float32),
            pltpu.VMEM((slots, share, LANES), jnp.bfloat16),
            pltpu.SMEM((-(-block // part), slots), jnp.int32),
            pltpu.SemaphoreType.DMA((chips + 2,)),
        ],
        compiler_params=small,
        name="scores",
    )(table_pairs, live, rule_of_block, own, *received, mine, other)
    return (smoothed, scores)


def solution(mesh):
    return jax.shard_map(
        on_device,
        mesh=mesh,
        in_specs=(
            P("ion", "pix"),
            P(None, "pix"),
            P("ion", None),
            P("ion"),
            P(),
            P("ion", None, None),
        ),
        out_specs=(P("ion", "pix"), P("ion", "pix", None)),
        check_vma=False,
    )
```
